32 devices in a mesh: groups: 2 (over x), replica: 4 (over y, core), tensor: 4 (over z).
Axes of the slice: x: 2, y: 2, z: 4, core: 2. Of those that a mesh axis runs over, the one named last changes fastest.
Arguments:
- queries: bfloat16 [256, 32, 8192], P(('groups', 'replica'), None, 'tensor'), parts along dimension 0, may hold values from -15 to 15
- suffix_key_value: bfloat16 [256, 32, 8, 256], P(('groups', 'replica'), None, 'tensor'), parts along dimension 0, may hold values from -6 to 6
- kv_pool: bfloat16 [512, 64, 8, 256], P(('groups', 'replica'), None, 'tensor'), parts along dimension 0, may hold values from -7 to 7
- page_table: int32 [256, 16], P(('groups', 'replica')), parts along dimension 0, may hold values from 0 to 63
- lengths: int32 [256], P(('groups', 'replica')), parts along dimension 0, may hold values from 1 to 32, 2048 in all
- destination: int32 [256, 1], P(('groups', 'replica')), parts along dimension 0, may hold values from 0 to 3; in each aligned block of 32 rows (0 to 31, 32 to 63, ...) at most 9 rows name the same one
Outputs:
- context: bfloat16 [256, 32, 8192], P(('groups', 'replica'), None, 'tensor'), parts along dimension 0
The draws below stay inside these ranges and needn't reach their ends.
There are 2 independent parts, one for each index of `groups`. The reference program is written for one: setup_inputs(seed, part) draws one part's arguments, and reference() takes and returns one part's arrays. A program takes and returns all parts, laid end to end along the dimension named above; each array names one. Nothing has to cross between parts.
Inputs may be any that keep to these rules, and one draw needn't show every extreme that they name: `page_table`: entries name pages of the destination replica's pool; pages may repeat. In each part of groups the lengths sum to 2048, and some request has all 32 tokens live. Among the requests of one replica at most 9 name the same destination, and in every draw some replica sends exactly 9 to one destination.
All inputs are finite; a program needn't handle non-finite values.
Results may differ from the reference program's by a relative error of at most 0.0049.
Values may be sent and summed in bfloat16 or wider, within the bound.
No kernel may reach another device: no remote copies, remote signals or barrier semaphores. Data moves between devices by JAX's collectives and lax.ppermute only.
A program may use at most 128 MiB of HBM per device.

```python
import math
import jax
import jax.numpy as jnp
import numpy as np
from jax import lax

HQ = 64
KEY_VALUE_HEADS = 8
HEAD_WIDTH = 128
SUFFIX_TOKENS = 32
PAGE_TOKENS = 64
PREFIX_PAGES = 16
POOL = 64
REQ_DEV = 32
CAP = 9
REQUEST_COUNT = 128
GLOBAL_PAGES = 256
N_REPLICA = 4


def draw_queries(key, part):
    key = jax.random.fold_in(key, 5)
    first_key = jax.random.fold_in(key, 0)
    noise_base = jnp.clip(2.5 * jax.random.normal(first_key, (REQUEST_COUNT, SUFFIX_TOKENS, HQ, HEAD_WIDTH), jnp.float32), -15.0, 15.0)
    return noise_base.reshape(REQUEST_COUNT, SUFFIX_TOKENS, HQ * HEAD_WIDTH).astype(jnp.bfloat16)


def draw_kv_pool(key, part):
    key = jax.random.fold_in(key, 9)
    page_pool_dims = (GLOBAL_PAGES, PAGE_TOKENS, KEY_VALUE_HEADS, 2 * HEAD_WIDTH)
    noise_base = jnp.clip(jax.random.normal(key, page_pool_dims, jnp.float32), -6.0, 6.0)
    return noise_base.astype(jnp.bfloat16)


def place_ends(entries, own_key, least, top_value):
    shape = entries.shape
    spot = [jax.random.randint(jax.random.fold_in(own_key, axis), (), 0, shape[axis]) for axis in range(len(shape))]
    entries = entries.at[tuple(spot)].set(least)
    longest = shape.index(max(shape))
    spot[longest] = (spot[longest] + 1) % shape[longest]
    return entries.at[tuple(spot)].set(top_value)


def block_scale(stream_key, extent, cuts, least, largest):
    loudness = 1.0
    for axis_at, shards_of in cuts:
        heights = jax.random.uniform(jax.random.fold_in(jax.random.fold_in(stream_key, 6), axis_at), (shards_of,), jnp.float32, least / len(cuts), largest / len(cuts))
        loudness = loudness * jnp.repeat(jnp.exp(heights), extent[axis_at] // shards_of).reshape((-1,) + (1,) * (len(extent) - 1 - axis_at))
    return loudness


def profile(number_of, total, bound, slope):
    portions = [(1 << 20) // math.isqrt(rank ** slope) + 1 for rank in range(2, number_of + 1)]
    spare, given = total - bound - (number_of - 1), [1] * (number_of - 1)
    while spare > 0:
        movable = [i for i in range(number_of - 1) if given[i] < bound]
        pool, left = sum([portions[i] for i in movable]), spare
        for i in movable:
            more = min(bound - given[i], max(1, left * portions[i] // pool), spare)
            given[i] = given[i] + more
            spare = spare - more
    return np.array([bound] + given)


def ragged_sizes(own_key, count, total, bound, lean):
    if count == 2:
        one = jax.random.randint(own_key, (), max(1, total - bound), min(bound, total - 1) + 1)
        return jnp.stack([one, total - one])
    tallies = jnp.asarray(profile(count, total, bound, lean), jnp.int32)
    pairs = (count - 1) // 2
    giver, receiver = tallies[1:1 + 2 * pairs:2], tallies[2:2 + 2 * pairs:2]
    room = jnp.minimum(giver - 1, bound - receiver)
    passed = jax.random.randint(jax.random.fold_in(own_key, 1), (pairs,), 0, 1 << 20) % (room + 1)
    tallies = tallies.at[1:1 + 2 * pairs:2].set(giver - passed).at[2:2 + 2 * pairs:2].set(receiver + passed)
    return tallies[jax.random.permutation(jax.random.fold_in(own_key, 2), count)]


def routed_block(key, own, number, rows, number_of, top, limit, skew):
    ranking = jax.random.permutation(key, number_of)
    heavy_load, ordinary = load_shares(number_of, rows * top, limit, skew, True), load_shares(number_of, rows * top, limit, skew, False)
    places = jnp.arange(number_of)

    def named(sizes, offset_by):
        used = int((sizes > 0).sum())
        fixed = max(1, used // 4)
        shifted = fixed + (places - fixed + offset_by * (used - fixed)) % max(1, number_of - fixed)
        return jnp.zeros((number_of,), jnp.int32).at[ranking[jnp.where(places < fixed, places, shifted)]].set(jnp.asarray(sizes, jnp.int32))

    sizes = jnp.where(number % 4 == 0, named(heavy_load, number // 4), named(ordinary, number - number // 4 - 1))
    mixed = jax.random.permutation(jax.random.fold_in(own, 3), number_of)
    source_of, sink = mixed[0:number_of // 2 * 2:2], mixed[1:number_of // 2 * 2:2]
    margin = jnp.minimum(sizes[source_of] - 1, limit - sizes[sink]) // 2
    margin = jnp.where((source_of == ranking[0]) | (sink == ranking[0]) | (sizes[sink] == 0), 0, jnp.maximum(margin, 0))
    shifted = jax.random.randint(jax.random.fold_in(own, 4), (number_of // 2,), 0, 1 << 20) % (margin + 1)
    sizes = sizes.at[source_of].add(-shifted).at[sink].add(shifted)
    items = jnp.searchsorted(jnp.cumsum(sizes), jnp.arange(rows * top), side="right").astype(jnp.int32)
    listing = items.reshape(top, rows).T
    listing = listing[jax.random.permutation(jax.random.fold_in(own, 1), rows)]
    offset_by = jax.random.randint(jax.random.fold_in(own, 2), (rows, 1), 0, top)
    return jnp.take_along_axis(listing, (jnp.arange(top)[None, :] + offset_by) % top, axis=1)


def load_shares(amount, total, reach, slope, full):
    portions = [(1 << 20) // math.isqrt(grade ** slope) + 1 for grade in range(1, amount + 1)]
    largest = reach if full else min(reach, max(-(-total // amount), total * portions[0] // sum(portions)))
    least = 1 if total - largest >= amount - 1 else 0
    holding, spare = [largest] + [least] * (amount - 1), total - largest - least * (amount - 1)
    while spare > 0:
        free = [i for i in range(1, amount) if holding[i] < largest] or [i for i in range(1, amount) if holding[i] < reach]
        mass, remaining = sum([portions[i] for i in free]), spare
        for i in free:
            extra = min(reach - holding[i], max(1, remaining * portions[i] // mass), spare)
            holding[i] = holding[i] + extra
            spare = spare - extra
    return np.array(holding)


def bell_draw(stream_key, extent, width, bound, cuts=(), kind=jnp.bfloat16):
    loudness = block_scale(stream_key, extent, cuts, -0.22, 0.18) if cuts else 1.0
    values = jax.random.normal(stream_key, extent, jnp.float32) * width * loudness
    return jnp.minimum(jnp.maximum(values, -bound), bound).astype(kind)


def setup_inputs(seed: int = 0, part: int = 0) -> dict:
    key_of = jax.random.split(jax.random.key(seed), 7)
    own_keys = jax.random.split(jax.random.fold_in(key_of[6], part), 7)
    queries = draw_queries(jax.random.fold_in(jax.random.fold_in(key_of[6], part), 71), part)
    suffix_key_value = bell_draw(own_keys[1], (REQUEST_COUNT, SUFFIX_TOKENS, KEY_VALUE_HEADS, 2 * HEAD_WIDTH), 1.0, 6.0, ((0, 4), (2, 4)))
    kv_pool = draw_kv_pool(jax.random.fold_in(jax.random.fold_in(key_of[6], part), 71), part)
    page_table = place_ends(jax.random.randint(own_keys[3], (REQUEST_COUNT, PREFIX_PAGES), 0, POOL), jax.random.fold_in(own_keys[3], 1), 0, POOL - 1).astype(jnp.int32)
    lengths = ragged_sizes(own_keys[4], REQUEST_COUNT, REQUEST_COUNT * SUFFIX_TOKENS // 2, SUFFIX_TOKENS, 2).astype(jnp.int32)
    destination_keys = jax.random.split(jax.random.fold_in(own_keys[5], 1), REQUEST_COUNT // REQ_DEV)
    destination_turns = jax.random.permutation(jax.random.fold_in(own_keys[5], 3), REQUEST_COUNT // REQ_DEV)
    destination = jax.vmap(lambda own, number: routed_block(jax.random.fold_in(own_keys[5], 2), own, number, REQ_DEV, N_REPLICA, 1, CAP, 2))(destination_keys, destination_turns).reshape((REQUEST_COUNT, 1))
    return {"queries": queries, "suffix_key_value": suffix_key_value, "kv_pool": kv_pool, "page_table": page_table, "lengths": lengths, "destination": destination}


def attend(query_rows, suffix_rows, prefix_rows, length):
    steps = query_rows.shape[0]
    kv_heads = suffix_rows.shape[1]
    head_size = suffix_rows.shape[2] // 2
    groups = query_rows.shape[1] // (kv_heads * head_size)
    stacked = jnp.concatenate([prefix_rows, suffix_rows], axis=0).astype(jnp.float32)
    key_rows = stacked[:, :, :head_size]
    values = stacked[:, :, head_size:]
    grouped = query_rows.reshape(steps, kv_heads, groups, head_size).astype(jnp.float32)
    scores = jnp.einsum('skgd,pkd->kgsp', grouped, key_rows) * (1.0 / math.sqrt(head_size))
    before = prefix_rows.shape[0]
    key_index = jnp.arange(before + steps, dtype=jnp.int32)
    query_index = jnp.arange(steps, dtype=jnp.int32)
    allowed = key_index[None, :] <= before + query_index[:, None]
    scores = jnp.where(allowed, scores, -1e+30)
    row_max = lax.optimization_barrier(jnp.max(scores, axis=-1, keepdims=True))
    exponent = jnp.where(allowed, jnp.exp(scores - row_max), 0.0)
    weights = (exponent / lax.optimization_barrier(jnp.sum(exponent, axis=-1, keepdims=True))).astype(jnp.bfloat16)
    mixed = jnp.einsum('kgsp,pkd->skgd', weights.astype(jnp.float32), values)
    live_rows = query_index < length
    mixed = jnp.where(live_rows[:, None, None, None], mixed, 0.0)
    return mixed.reshape(steps, kv_heads * groups * head_size).astype(jnp.bfloat16)

def reference(queries, suffix_key_value, kv_pool, page_table, lengths, destination):

    def per_request(request_item):
        query_rows, suffix_rows, page_ids, length, target = request_item
        prefix_tokens = kv_pool[target * POOL + page_ids]
        prefix_tokens = prefix_tokens.reshape(PREFIX_PAGES * PAGE_TOKENS, KEY_VALUE_HEADS, 2 * HEAD_WIDTH)
        return attend(query_rows, suffix_rows, prefix_tokens, length)
    return lax.map(per_request, (queries, suffix_key_value, page_table, lengths, destination[:, 0]))
```

```python
import functools
import math

import jax
import jax.numpy as jnp
from jax import lax
from jax.experimental import pallas as pl
from jax.experimental.pallas import tpu as pltpu
from jax.sharding import PartitionSpec as P

BIG = 1 << 14
STAT = 128


def vspec():
    return pl.BlockSpec(memory_space=pltpu.VMEM)


def sspec():
    return pl.BlockSpec(memory_space=pltpu.SMEM)


def shift_of(target, chips):
    here = lax.axis_index("replica") >> 1
    step = (target >> 1) - here
    return jnp.where(step < 0, step + chips, step)


def pack_kernel(chips, steps, requests, chunks, len_ref, dst_ref, q_ref, *rest):
    outs = rest[: len(chunks)]
    hot_refs = rest[len(chunks) : 2 * len(chunks)]
    fill = rest[-1]

    @pl.when(pl.program_id(0) == 0)
    def _():
        for s in range(chips):
            fill[s] = 0
        lane = lax.broadcasted_iota(jnp.int32, (1, requests * steps), 1)
        token = lax.rem(lane, steps)
        owner = lane // steps
        place = jnp.full((1, requests * steps), -1, jnp.int32)
        for i in range(requests):
            s = shift_of(dst_ref[i], chips)
            begin = fill[s]
            fill[s] = begin + len_ref[i]
            mine = (owner == i) & (token < len_ref[i])
            place = jnp.where(mine, s * BIG + begin + token, place)
        for (s, first, rows), hot in zip(chunks, hot_refs):
            row = lax.broadcasted_iota(jnp.int32, (rows, requests * steps), 0)
            match = (row + (s * BIG + first)) == place
            hot[...] = jnp.where(match, 1.0, 0.0).astype(jnp.bfloat16)

    block = q_ref[...]
    for hot, out in zip(hot_refs, outs):
        out[...] = jnp.dot(hot[...], block, preferred_element_type=jnp.float32).astype(out.dtype)


def pack(queries, lengths, target, chips, chunks):
    requests, steps, width = queries.shape
    flat = queries.reshape(requests * steps, width)
    columns = min(width, 512)
    return pl.pallas_call(
        functools.partial(pack_kernel, chips, steps, requests, chunks),
        grid=(width // columns,),
        in_specs=[sspec(), sspec(), pl.BlockSpec((requests * steps, columns), lambda j: (0, j))],
        out_specs=[pl.BlockSpec((rows, columns), lambda j: (0, j)) for _, _, rows in chunks],
        out_shape=[jax.ShapeDtypeStruct((rows, width), jnp.bfloat16) for _, _, rows in chunks],
        scratch_shapes=[pltpu.VMEM((rows, requests * steps), jnp.bfloat16) for _, _, rows in chunks]
        + [pltpu.SMEM((chips,), jnp.int32)],
        compiler_params=pltpu.CompilerParams(vmem_limit_bytes=40 << 20),
        cost_estimate=pl.CostEstimate(
            flops=2 * sum(c[2] for c in chunks) * requests * steps * width,
            bytes_accessed=2 * flat.size,
            transcendentals=0,
        ),
        name="pack",
    )(lengths, target, flat)


def stack_heads(q, k, group, head):
    return jnp.concatenate(
        [q[:, (k * group + g) * head : (k * group + g + 1) * head] for g in range(group)], axis=0
    )


def nt_dot(a, b):
    return lax.dot_general(a, b, (((1,), (1,)), ((), ())), preferred_element_type=jnp.float32)


def causal(window, group, steps):
    row = lax.broadcasted_iota(jnp.int32, (group * window, steps), 0)
    col = lax.broadcasted_iota(jnp.int32, (group * window, steps), 1)
    return col <= lax.rem(row, window)


def split_stat(values, window):
    lane = lax.broadcasted_iota(jnp.int32, (window, STAT), 1)
    count = len(values)
    stat = jnp.zeros((window, STAT), jnp.float32)
    for h, column in enumerate(values):
        stat = jnp.where(lax.rem(lane, count) == h, column, stat)
    high = stat.astype(jnp.bfloat16).astype(jnp.float32)
    rest = stat - high
    middle = rest.astype(jnp.bfloat16).astype(jnp.float32)
    low = rest - middle
    part = lane // count
    stat = jnp.where(part == 0, high, jnp.where(part == 1, middle, low))
    return jnp.where(part < 3, stat, 0.0).astype(jnp.bfloat16)


def page_copies(table_ref, request, pages, pool_ref, buffer, slot, sem):
    for p in range(pages):
        pltpu.make_async_copy(
            pool_ref.at[table_ref[request, p]], buffer.at[slot, p], sem.at[slot]
        ).start()


def fetch(table_ref, request, own, pages, own_ref, sib_ref, buffer, slot, sem):
    @pl.when(own)
    def _():
        page_copies(table_ref, request, pages, own_ref, buffer, slot, sem)

    @pl.when(jnp.logical_not(own))
    def _():
        page_copies(table_ref, request, pages, sib_ref, buffer, slot, sem)


def await_pages(own_ref, pages, buffer, slot, sem):
    pltpu.make_async_copy(own_ref.at[pl.ds(0, pages)], buffer.at[slot], sem.at[slot]).wait()


def prefix_part(buffer, slot, k, head):
    keys = buffer[slot, :, k, :, 0:head]
    values = buffer[slot, :, k, :, head : 2 * head]
    count = keys.shape[0] * keys.shape[1]
    return keys.reshape(count, head), values.reshape(count, head)


def local_kernel(
    chips, dims, len_ref, dst_ref, table_ref, q_ref, suf_ref, own_ref, sib_ref,
    ctx_ref, stat_ref, buffer, todo, sem,
):
    requests, steps, kv, group, head, pages = dims
    core = lax.rem(lax.axis_index("replica"), 2)
    coeff = math.log2(math.e) / math.sqrt(head)

    def listing(i, count):
        todo[count] = i
        return count + (shift_of(dst_ref[i], chips) == 0).astype(jnp.int32)

    count = lax.fori_loop(0, requests, listing, jnp.int32(0))

    def start(j, slot):
        i = todo[j]
        own = lax.rem(dst_ref[i], 2) == core
        fetch(table_ref, i, own, pages, own_ref, sib_ref, buffer, slot, sem)

    @pl.when(count > 0)
    def _():
        start(0, 0)

    def near_only(i, carry):
        @pl.when(shift_of(dst_ref[i], chips) != 0)
        def _():
            q = q_ref[i]
            mask = causal(steps, group, steps)
            sums = []
            for k in range(kv):
                qk = stack_heads(q, k, group, head)
                score = jnp.where(mask, nt_dot(qk, suf_ref[i, k, :, 0:head]), -1e30)
                top = jnp.max(score, axis=1, keepdims=True)
                weight = jnp.where(mask, jnp.exp2((score - top) * coeff), 0.0)
                total = jnp.sum(weight, axis=1, keepdims=True)
                mixed = jnp.dot(
                    weight.astype(jnp.bfloat16),
                    suf_ref[i, k, :, head : 2 * head],
                    preferred_element_type=jnp.float32,
                )
                mixed = mixed / total
                lse = top * coeff + jnp.log2(total)
                for g in range(group):
                    h = k * group + g
                    ctx_ref[i, :, h * head : (h + 1) * head] = mixed[
                        g * steps : (g + 1) * steps
                    ].astype(jnp.bfloat16)
                    sums.append(lse[g * steps : (g + 1) * steps])
            stat_ref[i] = split_stat(sums, steps)

        return carry

    lax.fori_loop(0, requests, near_only, 0)

    def compute(i, slot, window):
        q = q_ref[i, 0:window, :]
        mask = causal(window, group, steps)
        live = lax.broadcasted_iota(jnp.int32, (window, head), 0) < len_ref[i]
        for k in range(kv):
            qk = stack_heads(q, k, group, head)
            keys, values = prefix_part(buffer, slot, k, head)
            score = nt_dot(qk, keys)
            near = jnp.where(mask, nt_dot(qk, suf_ref[i, k, :, 0:head]), -1e30)
            top = jnp.maximum(
                jnp.max(score, axis=1, keepdims=True), jnp.max(near, axis=1, keepdims=True)
            )
            weight = jnp.exp2((score - top) * coeff)
            near = jnp.where(mask, jnp.exp2((near - top) * coeff), 0.0)
            total = jnp.sum(weight, axis=1, keepdims=True) + jnp.sum(near, axis=1, keepdims=True)
            mixed = jnp.dot(
                weight.astype(jnp.bfloat16), values, preferred_element_type=jnp.float32
            )
            mixed += jnp.dot(
                near.astype(jnp.bfloat16),
                suf_ref[i, k, :, head : 2 * head],
                preferred_element_type=jnp.float32,
            )
            mixed = mixed / total
            for g in range(group):
                h = k * group + g
                part = jnp.where(live, mixed[g * window : (g + 1) * window], 0.0)
                ctx_ref[i, 0:window, h * head : (h + 1) * head] = part.astype(jnp.bfloat16)
        if window < steps:
            ctx_ref[i, window:steps, :] = jnp.zeros(
                (steps - window, ctx_ref.shape[2]), jnp.bfloat16
            )

    def step(j, carry):
        slot = lax.rem(j, 2)

        @pl.when(j + 1 < count)
        def _():
            start(j + 1, 1 - slot)

        await_pages(own_ref, pages, buffer, slot, sem)
        i = todo[j]
        stat_ref[i] = jnp.zeros((steps, STAT), jnp.bfloat16)
        small = len_ref[i] <= steps // 2

        @pl.when(small)
        def _():
            compute(i, slot, steps // 2)

        @pl.when(jnp.logical_not(small))
        def _():
            compute(i, slot, steps)

        return carry

    lax.fori_loop(0, count, step, 0)


def local(queries, suffix, own, sib, table, lengths, target, chips):
    requests, steps, width = queries.shape
    kv, head = suffix.shape[1], suffix.shape[3] // 2
    pages = table.shape[1]
    dims = (requests, steps, kv, width // (kv * head), head, pages)
    hbm = pl.BlockSpec(memory_space=pl.ANY)
    return pl.pallas_call(
        functools.partial(local_kernel, chips, dims),
        in_specs=[sspec(), sspec(), sspec(), vspec(), vspec(), hbm, hbm],
        out_specs=[vspec(), vspec()],
        out_shape=[
            jax.ShapeDtypeStruct(queries.shape, jnp.bfloat16),
            jax.ShapeDtypeStruct((requests, steps, STAT), jnp.bfloat16),
        ],
        scratch_shapes=[
            pltpu.VMEM((2, pages) + own.shape[1:], jnp.bfloat16),
            pltpu.SMEM((requests + 1,), jnp.int32),
            pltpu.SemaphoreType.DMA((2,)),
        ],
        compiler_params=pltpu.CompilerParams(vmem_limit_bytes=40 << 20),
        cost_estimate=pl.CostEstimate(
            flops=8 << 30, bytes_accessed=30 << 20, transcendentals=8 << 20
        ),
        name="local",
    )(lengths, target, table, queries, suffix, own, sib)


def far_kernel(
    chips, dims, first, rows, meta_ref, q_ref, own_ref, sib_ref, out_ref, buffer, todo, begin, end,
    sem,
):
    requests, steps, kv, group, head, pages = dims
    core = lax.rem(lax.axis_index("replica"), 2)
    coeff = math.log2(math.e) / math.sqrt(head)
    width = kv * group * head

    def listing(i, carry):
        count, row = carry
        size = jnp.where(shift_of(meta_ref[i, pages + 1], chips) == 0, meta_ref[i, pages], 0)
        low = jnp.maximum(row - first, 0)
        high = jnp.minimum(row + size - first, rows)
        todo[count] = i
        begin[count] = low
        end[count] = high
        return count + (high > low).astype(jnp.int32), row + size

    count, _ = lax.fori_loop(0, requests, listing, (jnp.int32(0), jnp.int32(0)))

    def start(j, slot):
        i = todo[j]
        own = lax.rem(meta_ref[i, pages + 1], 2) == core
        fetch(meta_ref, i, own, pages, own_ref, sib_ref, buffer, slot, sem)

    @pl.when(count > 0)
    def _():
        start(0, 0)

    out_ref[...] = jnp.zeros_like(out_ref)

    def compute(j, slot, window):
        base = jnp.minimum((begin[j] // 16) * 16, rows - window)
        base = pl.multiple_of(base, 16)
        span = pl.ds(base, window)
        q = q_ref[span, :]
        row = base + lax.broadcasted_iota(jnp.int32, (window, head), 0)
        live = (row >= begin[j]) & (row < end[j])
        sums = []
        for k in range(kv):
            qk = stack_heads(q, k, group, head)
            keys, values = prefix_part(buffer, slot, k, head)
            score = nt_dot(qk, keys)
            top = jnp.max(score, axis=1, keepdims=True)
            weight = jnp.exp2((score - top) * coeff)
            total = jnp.sum(weight, axis=1, keepdims=True)
            mixed = jnp.dot(
                weight.astype(jnp.bfloat16), values, preferred_element_type=jnp.float32
            )
            mixed = mixed / total
            lse = top * coeff + jnp.log2(total)
            for g in range(group):
                h = k * group + g
                part = mixed[g * window : (g + 1) * window]
                old = out_ref[span, h * head : (h + 1) * head].astype(jnp.float32)
                out_ref[span, h * head : (h + 1) * head] = jnp.where(live, part, old).astype(
                    jnp.bfloat16
                )
                sums.append(lse[g * window : (g + 1) * window])
        old = out_ref[span, width : width + STAT].astype(jnp.float32)
        new = split_stat(sums, window).astype(jnp.float32)
        live = live[:, 0:STAT] if head >= STAT else live
        out_ref[span, width : width + STAT] = jnp.where(live, new, old).astype(jnp.bfloat16)

    def step(j, carry):
        slot = lax.rem(j, 2)

        @pl.when(j + 1 < count)
        def _():
            start(j + 1, 1 - slot)

        await_pages(own_ref, pages, buffer, slot, sem)
        need = (end[j] - (begin[j] // 16) * 16 + 15) // 16
        for blocks in (1, 2, 3):

            @pl.when(need == blocks)
            def _():
                compute(j, slot, 16 * blocks)

        return carry

    lax.fori_loop(0, count, step, 0)


def far(chunk, meta, own, sib, dims, chips, first):
    rows, width = chunk.shape
    requests, pages = dims[0], dims[5]
    hbm = pl.BlockSpec(memory_space=pl.ANY)
    return pl.pallas_call(
        functools.partial(far_kernel, chips, dims, first, rows),
        in_specs=[sspec(), vspec(), hbm, hbm],
        out_specs=vspec(),
        out_shape=jax.ShapeDtypeStruct((rows, width + STAT), jnp.bfloat16),
        scratch_shapes=[
            pltpu.VMEM((2, pages) + own.shape[1:], jnp.bfloat16),
            pltpu.SMEM((requests + 1,), jnp.int32),
            pltpu.SMEM((requests + 1,), jnp.int32),
            pltpu.SMEM((requests + 1,), jnp.int32),
            pltpu.SemaphoreType.DMA((2,)),
        ],
        compiler_params=pltpu.CompilerParams(vmem_limit_bytes=40 << 20),
        cost_estimate=pl.CostEstimate(
            flops=rows * (6 << 20), bytes_accessed=rows * (60 << 10), transcendentals=rows * (16 << 10)
        ),
        name="far",
    )(meta, chunk, own, sib)


def merge_kernel(chips, steps, requests, chunks, per, len_ref, dst_ref, ctx_ref, stat_ref, *rest):
    backs = rest[: len(chunks)]
    out_ref = rest[len(chunks)]
    fill, begin = rest[-2], rest[-1]
    width = ctx_ref.shape[2]
    heads = width // STAT
    at = pl.program_id(0)

    @pl.when(at == 0)
    def _():
        for s in range(chips):
            fill[s] = 0

        def place(i, carry):
            s = shift_of(dst_ref[i], chips)
            begin[i] = s * BIG + fill[s]
            fill[s] = fill[s] + len_ref[i]
            return carry

        lax.fori_loop(0, requests, place, 0)

    lane = lax.broadcasted_iota(jnp.int32, (STAT, width), 0)
    col = lax.broadcasted_iota(jnp.int32, (STAT, width), 1) // (width // heads)
    spread = jnp.where((lax.rem(lane, heads) == col) & (lane < 3 * heads), 1.0, 0.0)
    spread = spread.astype(jnp.bfloat16)
    for u in range(per):
        i = at * per + u
        away = begin[i] >= BIG

        @pl.when(jnp.logical_not(away))
        def _():
            out_ref[u] = ctx_ref[u]

        @pl.when(away)
        def _():
            got = jnp.zeros((steps, width + STAT), jnp.float32)
            for (s, first, rows), back in zip(chunks, backs):
                token = lax.broadcasted_iota(jnp.int32, (steps, rows), 0)
                row = lax.broadcasted_iota(jnp.int32, (steps, rows), 1)
                hot = (begin[i] + token == row + (s * BIG + first)) & (token < len_ref[i])
                hot = jnp.where(hot, 1.0, 0.0).astype(jnp.bfloat16)
                got += jnp.dot(hot, back[...], preferred_element_type=jnp.float32)
            far_sum = jnp.dot(
                got[:, width:].astype(jnp.bfloat16), spread, preferred_element_type=jnp.float32
            )
            near_sum = jnp.dot(stat_ref[u], spread, preferred_element_type=jnp.float32)
            share = 1.0 / (1.0 + jnp.exp2(near_sum - far_sum))
            near = ctx_ref[u].astype(jnp.float32)
            mixed = near + share * (got[:, 0:width] - near)
            live = lax.broadcasted_iota(jnp.int32, (steps, width), 0) < len_ref[i]
            out_ref[u] = jnp.where(live, mixed, 0.0).astype(jnp.bfloat16)


def merge(ctx, stat, backs, lengths, target, chips, chunks):
    requests, steps, width = ctx.shape
    per = 4
    return pl.pallas_call(
        functools.partial(merge_kernel, chips, steps, requests, chunks, per),
        grid=(requests // per,),
        in_specs=[
            sspec(),
            sspec(),
            pl.BlockSpec((per, steps, width), lambda j: (j, 0, 0)),
            pl.BlockSpec((per, steps, STAT), lambda j: (j, 0, 0)),
        ]
        + [vspec()] * len(chunks),
        out_specs=pl.BlockSpec((per, steps, width), lambda j: (j, 0, 0)),
        out_shape=jax.ShapeDtypeStruct(ctx.shape, jnp.bfloat16),
        scratch_shapes=[pltpu.SMEM((chips,), jnp.int32), pltpu.SMEM((requests,), jnp.int32)],
        compiler_params=pltpu.CompilerParams(vmem_limit_bytes=40 << 20),
        name="merge",
    )(lengths, target, ctx, stat, *backs)


def split_rows(chips, low, high, size):
    return tuple(
        (s, first, min(size, high - first))
        for s in range(1, chips)
        for first in range(low, high, size)
    )


def shards(queries, suffix_key_value, kv_pool, page_table, lengths, destination):
    replicas = lax.axis_size("replica")
    chips = replicas // 2
    requests, steps, width = queries.shape
    kv, head = suffix_key_value.shape[2], suffix_key_value.shape[3] // 2
    pages = page_table.shape[1]
    dims = (requests, steps, kv, width // (kv * head), head, pages)
    target = destination[:, 0]

    most = 2 * (requests // replicas + 1) * steps
    usual = min(most, -(-(requests * steps * 11) // (16 * chips * 32)) * 32)
    main = split_rows(chips, 0, usual, 96)
    extra = split_rows(chips, usual, most, 256)

    def away(s):
        return [(r, (r + 2 * s) % replicas) for r in range(replicas)]

    def back(s):
        return [((r + 2 * s) % replicas, r) for r in range(replicas)]

    meta = jnp.concatenate([page_table, lengths[:, None], destination], axis=1)
    packed = pack(queries, lengths, target, chips, main)
    metas = {s: lax.ppermute(meta, "replica", away(s)) for s in range(1, chips)}
    arrived = [lax.ppermute(rows, "replica", away(c[0])) for rows, c in zip(packed, main)]

    own = jnp.transpose(kv_pool, (0, 2, 1, 3))
    sib = lax.ppermute(own, "replica", [(r, r ^ 1) for r in range(replicas)])
    suffix = jnp.transpose(suffix_key_value, (0, 2, 1, 3))
    ctx, stat = local(queries, suffix, own, sib, page_table, lengths, target, chips)

    def serve(rows, c):
        return lax.ppermute(
            far(rows, metas[c[0]], own, sib, dims, chips, c[1]), "replica", back(c[0])
        )

    returned = [serve(rows, c) for rows, c in zip(arrived, main)]

    if not extra:
        return merge(ctx, stat, returned, lengths, target, chips, main)

    step = lax.rem((target >> 1) - (lax.axis_index("replica") >> 1) + chips, chips)
    sent = jnp.sum(
        jnp.where(step[None, :] == jnp.arange(1, chips)[:, None], lengths[None, :], 0), axis=1
    )
    widest = lax.pmax(jnp.max(sent), ("groups", "replica", "tensor"))

    def overflow():
        more = pack(queries, lengths, target, chips, extra)
        more = [serve(lax.ppermute(r, "replica", away(c[0])), c) for r, c in zip(more, extra)]
        return merge(ctx, stat, returned + more, lengths, target, chips, main + extra)

    def common():
        return merge(ctx, stat, returned, lengths, target, chips, main)

    return lax.cond(widest > usual, overflow, common)


def solution(mesh):
    return jax.shard_map(
        shards,
        mesh=mesh,
        in_specs=(
            P(("groups", "replica"), None, "tensor"),
            P(("groups", "replica"), None, "tensor", None),
            P(("groups", "replica"), None, "tensor", None),
            P(("groups", "replica"), None),
            P(("groups", "replica")),
            P(("groups", "replica"), None),
        ),
        out_specs=P(("groups", "replica"), None, "tensor"),
        check_vma=False,
    )
```

```python
import functools
import math

import jax
import jax.numpy as jnp
from jax import lax
from jax.experimental import pallas as pl
from jax.experimental.pallas import tpu as pltpu
from jax.sharding import PartitionSpec as P

BIG = 1 << 14
STAT = 128
VMEM_LIMIT = 48 << 20


def vspec():
    return pl.BlockSpec(memory_space=pltpu.VMEM)


def sspec():
    return pl.BlockSpec(memory_space=pltpu.SMEM)


def anyspec():
    return pl.BlockSpec(memory_space=pl.ANY)


def shift_of(target, chips):
    here = lax.axis_index("replica") >> 1
    step = (target >> 1) - here
    return jnp.where(step < 0, step + chips, step)


def pack_kernel(chips, steps, requests, chunks, len_ref, dst_ref, q_ref, *rest):
    outs = rest[: len(chunks)]
    hot_refs = rest[len(chunks) : 2 * len(chunks)]
    fill = rest[-1]

    @pl.when(pl.program_id(0) == 0)
    def _():
        for s in range(chips):
            fill[s] = 0
        lane = lax.broadcasted_iota(jnp.int32, (1, requests * steps), 1)
        token = lax.rem(lane, steps)
        owner = lane // steps
        place = jnp.full((1, requests * steps), -1, jnp.int32)
        for i in range(requests):
            s = shift_of(dst_ref[i], chips)
            begin = fill[s]
            fill[s] = begin + len_ref[i]
            mine = (owner == i) & (token < len_ref[i])
            place = jnp.where(mine, s * BIG + begin + token, place)
        for (s, first, rows), hot in zip(chunks, hot_refs):
            row = lax.broadcasted_iota(jnp.int32, (rows, requests * steps), 0)
            match = (row + (s * BIG + first)) == place
            hot[...] = jnp.where(match, 1.0, 0.0).astype(jnp.bfloat16)

    block = q_ref[...]
    for hot, out in zip(hot_refs, outs):
        out[...] = jnp.dot(hot[...], block, preferred_element_type=jnp.float32).astype(out.dtype)


def pack(queries, lengths, target, chips, chunks):
    requests, steps, width = queries.shape
    flat = queries.reshape(requests * steps, width)
    columns = min(width, 512)
    return pl.pallas_call(
        functools.partial(pack_kernel, chips, steps, requests, chunks),
        grid=(width // columns,),
        in_specs=[sspec(), sspec(), pl.BlockSpec((requests * steps, columns), lambda j: (0, j))],
        out_specs=[pl.BlockSpec((rows, columns), lambda j: (0, j)) for _, _, rows in chunks],
        out_shape=[jax.ShapeDtypeStruct((rows, width), jnp.bfloat16) for _, _, rows in chunks],
        scratch_shapes=[pltpu.VMEM((rows, requests * steps), jnp.bfloat16) for _, _, rows in chunks]
        + [pltpu.SMEM((chips,), jnp.int32)],
        compiler_params=pltpu.CompilerParams(vmem_limit_bytes=VMEM_LIMIT),
        cost_estimate=pl.CostEstimate(
            flops=2 * sum(c[2] for c in chunks) * requests * steps * width,
            bytes_accessed=2 * flat.size,
            transcendentals=0,
        ),
        name="pack",
    )(lengths, target, flat)


def nt_dot(a, b):
    return lax.dot_general(a, b, (((1,), (1,)), ((), ())), preferred_element_type=jnp.float32)


def tn_dot(a, b):
    return lax.dot_general(a, b, (((0,), (0,)), ((), ())), preferred_element_type=jnp.float32)


def fold(x, op):
    rows, cols = x.shape
    x = x.reshape(rows // 8, 8, cols)
    return jnp.max(x, axis=0) if op == "max" else jnp.sum(x, axis=0)


def attend(q, dims, window, pages_ref, suffix, s_refs, p_refs, want_sum):
    requests, steps, kv, group, head, pages = dims
    coeff = math.log2(math.e) / math.sqrt(head)
    cols = group * window
    found = []
    for k in range(kv):
        qk = jnp.concatenate(
            [q[:, (k * group + g) * head : (k * group + g + 1) * head] for g in range(group)], axis=0
        )
        top = None
        near = None
        if pages_ref is not None:
            per = pages_ref.shape[2]
            count = 4 if pages % 4 == 0 else 1
            for p in range(0, pages, count):
                keys = pages_ref[p : p + count, k, :, 0:head].reshape(count * per, head)
                score = nt_dot(keys, qk)
                s_refs[k][p * per : (p + count) * per, 0:cols] = score
                best = fold(score, "max")
                top = best if top is None else jnp.maximum(top, best)
        if suffix is not None:
            near = nt_dot(suffix[k, :, 0:head], qk)
            key = lax.broadcasted_iota(jnp.int32, (steps, cols), 0)
            token = lax.rem(lax.broadcasted_iota(jnp.int32, (steps, cols), 1), window)
            mask = key <= token
            near = jnp.where(mask, near, -1e30)
            best = fold(near, "max")
            top = best if top is None else jnp.maximum(top, best)
        found.append((jnp.max(top, axis=0, keepdims=True) * coeff, near))
    results = []
    for k in range(kv):
        level, near = found[k]
        total = None
        mixed = None
        if pages_ref is not None:
            per = pages_ref.shape[2]
            for p in range(pages):
                span = slice(p * per, (p + 1) * per)
                weight = jnp.exp2(s_refs[k][span, 0:cols] * coeff - level)
                part = fold(weight, "sum")
                total = part if total is None else total + part
                p_refs[k][span, 0:cols] = weight.astype(jnp.bfloat16)
            values = pages_ref[:, k, :, head : 2 * head].reshape(pages * per, head)
            mixed = tn_dot(values, p_refs[k][:, 0:cols])
        if near is not None:
            key = lax.broadcasted_iota(jnp.int32, (steps, cols), 0)
            token = lax.rem(lax.broadcasted_iota(jnp.int32, (steps, cols), 1), window)
            weight = jnp.where(key <= token, jnp.exp2(near * coeff - level), 0.0)
            part = fold(weight, "sum")
            total = part if total is None else total + part
            more = tn_dot(suffix[k, :, head : 2 * head], weight.astype(jnp.bfloat16))
            mixed = more if mixed is None else mixed + more
        total = jnp.sum(total, axis=0, keepdims=True)
        mixed = (mixed / total).T
        lse = None
        if want_sum:
            lse = jnp.broadcast_to(level + jnp.log2(total), (STAT, cols)).T
        results.append((mixed, lse))
    return results


def split_stat(values, group, window):
    lane = lax.broadcasted_iota(jnp.int32, (window, STAT), 1)
    count = len(values) * group
    which = lax.rem(lane, count)
    stat = jnp.zeros((window, STAT), jnp.float32)
    for k, value in enumerate(values):
        for g in range(group):
            stat = jnp.where(which == k * group + g, value[g * window : (g + 1) * window], stat)
    high = stat.astype(jnp.bfloat16).astype(jnp.float32)
    rest = stat - high
    middle = rest.astype(jnp.bfloat16).astype(jnp.float32)
    low = rest - middle
    part = lane // count
    stat = jnp.where(part == 0, high, jnp.where(part == 1, middle, low))
    return jnp.where(part < 3, stat, 0.0)


def fetch(table_ref, request, own, pages, own_ref, sib_ref, buffer, slot, sem):
    def copies(pool_ref):
        for p in range(pages):
            pltpu.make_async_copy(
                pool_ref.at[table_ref[request, p]], buffer.at[slot, p], sem.at[slot]
            ).start()

    @pl.when(own)
    def _():
        copies(own_ref)

    @pl.when(jnp.logical_not(own))
    def _():
        copies(sib_ref)


def await_pages(own_ref, pages, buffer, slot, sem):
    pltpu.make_async_copy(own_ref.at[pl.ds(0, pages)], buffer.at[slot], sem.at[slot]).wait()


def score_scratch(kv, keys, cols):
    return [pltpu.VMEM((keys, cols), jnp.float32) for _ in range(kv)] + [
        pltpu.VMEM((keys, cols), jnp.bfloat16) for _ in range(kv)
    ]


def near_kernel(
    chips, dims, len_ref, dst_ref, q_ref, suf_ref, ctx_ref, stat_ref, q_buf, o_buf, todo, q_sem, o_sem
):
    requests, steps, kv, group, head, pages = dims

    def listing(i, count):
        todo[count] = i
        return count + (shift_of(dst_ref[i], chips) != 0).astype(jnp.int32)

    count = lax.fori_loop(0, requests, listing, jnp.int32(0))

    def take(j, slot):
        return pltpu.make_async_copy(q_ref.at[todo[j]], q_buf.at[slot], q_sem.at[slot])

    def give(j, slot):
        return pltpu.make_async_copy(o_buf.at[slot], ctx_ref.at[todo[j]], o_sem.at[slot])

    @pl.when(count > 0)
    def _():
        take(0, 0).start()

    stat_ref[...] = jnp.zeros_like(stat_ref)

    def step(j, carry):
        slot = lax.rem(j, 2)

        @pl.when(j + 1 < count)
        def _():
            take(j + 1, 1 - slot).start()

        @pl.when(j >= 2)
        def _():
            give(j - 2, slot).wait()

        take(j, slot).wait()
        i = todo[j]
        found = attend(q_buf[slot], dims, steps, None, suf_ref.at[i], None, None, True)
        live = lax.broadcasted_iota(jnp.int32, (steps, head), 0) < len_ref[i]
        for k, (mixed, lse) in enumerate(found):
            for g in range(group):
                h = k * group + g
                part = jnp.where(live, mixed[g * steps : (g + 1) * steps], 0.0)
                o_buf[slot, :, h * head : (h + 1) * head] = part.astype(jnp.bfloat16)
        stat_ref[i] = split_stat([f[1] for f in found], group, steps).astype(jnp.bfloat16)
        give(j, slot).start()
        return carry

    lax.fori_loop(0, count, step, 0)

    def drain(j, carry):
        give(j, lax.rem(j, 2)).wait()
        return carry

    lax.fori_loop(jnp.maximum(count - 2, 0), count, drain, 0)


def near_part(queries, suffix, lengths, target, dims, chips):
    requests, steps, width = queries.shape
    return pl.pallas_call(
        functools.partial(near_kernel, chips, dims),
        in_specs=[sspec(), sspec(), anyspec(), vspec()],
        out_specs=[anyspec(), vspec()],
        out_shape=[
            jax.ShapeDtypeStruct(queries.shape, jnp.bfloat16),
            jax.ShapeDtypeStruct((requests, steps, STAT), jnp.bfloat16),
        ],
        scratch_shapes=[
            pltpu.VMEM((2, steps, width), jnp.bfloat16),
            pltpu.VMEM((2, steps, width), jnp.bfloat16),
            pltpu.SMEM((requests + 1,), jnp.int32),
            pltpu.SemaphoreType.DMA((2,)),
            pltpu.SemaphoreType.DMA((2,)),
        ],
        compiler_params=pltpu.CompilerParams(vmem_limit_bytes=VMEM_LIMIT),
        cost_estimate=pl.CostEstimate(
            flops=2 << 30, bytes_accessed=8 << 20, transcendentals=1 << 20
        ),
        name="near",
    )(lengths, target, queries, suffix)


def local_kernel(
    chips, dims, len_ref, dst_ref, table_ref, q_ref, suf_ref, own_ref, sib_ref, old_ref,
    ctx_ref, buffer, q_buf, o_buf, s0, s1, p0, p1, todo, sem, q_sem, o_sem,
):
    requests, steps, kv, group, head, pages = dims
    core = lax.rem(lax.axis_index("replica"), 2)

    def listing(i, count):
        todo[count] = i
        return count + (shift_of(dst_ref[i], chips) == 0).astype(jnp.int32)

    count = lax.fori_loop(0, requests, listing, jnp.int32(0))

    def take(j, slot):
        return pltpu.make_async_copy(q_ref.at[todo[j]], q_buf.at[slot], q_sem.at[slot])

    def give(j, slot):
        return pltpu.make_async_copy(o_buf.at[slot], ctx_ref.at[todo[j]], o_sem.at[slot])

    def start(j, slot):
        i = todo[j]
        own = lax.rem(dst_ref[i], 2) == core
        take(j, slot).start()
        fetch(table_ref, i, own, pages, own_ref, sib_ref, buffer, slot, sem)

    @pl.when(count > 0)
    def _():
        start(0, 0)

    def compute(i, slot, window):
        found = attend(
            q_buf[slot, 0:window, :], dims, window, buffer.at[slot], suf_ref.at[i], (s0, s1),
            (p0, p1), False,
        )
        live = lax.broadcasted_iota(jnp.int32, (window, head), 0) < len_ref[i]
        for k, (mixed, _) in enumerate(found):
            for g in range(group):
                h = k * group + g
                part = jnp.where(live, mixed[g * window : (g + 1) * window], 0.0)
                o_buf[slot, 0:window, h * head : (h + 1) * head] = part.astype(jnp.bfloat16)
        if window < steps:
            o_buf[slot, window:steps, :] = jnp.zeros(
                (steps - window, o_buf.shape[2]), jnp.bfloat16
            )

    def step(j, carry):
        slot = lax.rem(j, 2)

        @pl.when(j + 1 < count)
        def _():
            start(j + 1, 1 - slot)

        @pl.when(j >= 2)
        def _():
            give(j - 2, slot).wait()

        take(j, slot).wait()
        await_pages(own_ref, pages, buffer, slot, sem)
        i = todo[j]
        small = len_ref[i] <= steps // 2

        @pl.when(small)
        def _():
            compute(i, slot, steps // 2)

        @pl.when(jnp.logical_not(small))
        def _():
            compute(i, slot, steps)

        give(j, slot).start()
        return carry

    lax.fori_loop(0, count, step, 0)

    def drain(j, carry):
        give(j, lax.rem(j, 2)).wait()
        return carry

    lax.fori_loop(jnp.maximum(count - 2, 0), count, drain, 0)


def one_head_kernel(kernel, where):
    def wrapped(*refs):
        refs = list(refs)
        refs.insert(where + 1, None)
        refs.insert(where + 3, None)
        return kernel(*refs)

    return wrapped


def local(queries, suffix, own, sib, ctx, table, lengths, target, dims, chips):
    requests, steps, kv, group, head, pages = dims
    width = queries.shape[2]
    kernel = functools.partial(local_kernel, chips, dims)
    if kv == 1:
        kernel = one_head_kernel(kernel, 12)
    return pl.pallas_call(
        kernel,
        in_specs=[sspec(), sspec(), sspec(), anyspec(), vspec()] + [anyspec()] * 3,
        out_specs=anyspec(),
        out_shape=jax.ShapeDtypeStruct(queries.shape, jnp.bfloat16),
        input_output_aliases={7: 0},
        scratch_shapes=[
            pltpu.VMEM((2, pages) + own.shape[1:], jnp.bfloat16),
            pltpu.VMEM((2, steps, width), jnp.bfloat16),
            pltpu.VMEM((2, steps, width), jnp.bfloat16),
        ]
        + score_scratch(kv, pages * own.shape[2], group * steps)
        + [
            pltpu.SMEM((requests + 1,), jnp.int32),
            pltpu.SemaphoreType.DMA((2,)),
            pltpu.SemaphoreType.DMA((2,)),
            pltpu.SemaphoreType.DMA((2,)),
        ],
        compiler_params=pltpu.CompilerParams(vmem_limit_bytes=VMEM_LIMIT),
        cost_estimate=pl.CostEstimate(
            flops=8 << 30, bytes_accessed=30 << 20, transcendentals=8 << 20
        ),
        name="local",
    )(lengths, target, table, queries, suffix, own, sib, ctx)


def far_kernel(
    chips, dims, first, rows, meta_ref, q_ref, own_ref, sib_ref, out_ref, buffer, s0, s1, p0, p1,
    todo, begin, end, sem,
):
    requests, steps, kv, group, head, pages = dims
    core = lax.rem(lax.axis_index("replica"), 2)
    width = kv * group * head

    def listing(i, carry):
        count, row = carry
        size = jnp.where(shift_of(meta_ref[i, pages + 1], chips) == 0, meta_ref[i, pages], 0)
        low = jnp.maximum(row - first, 0)
        high = jnp.minimum(row + size - first, rows)
        todo[count] = i
        begin[count] = low
        end[count] = high
        return count + (high > low).astype(jnp.int32), row + size

    count, _ = lax.fori_loop(0, requests, listing, (jnp.int32(0), jnp.int32(0)))

    def start(j, slot):
        i = todo[j]
        own = lax.rem(meta_ref[i, pages + 1], 2) == core
        fetch(meta_ref, i, own, pages, own_ref, sib_ref, buffer, slot, sem)

    @pl.when(count > 0)
    def _():
        start(0, 0)

    out_ref[...] = jnp.zeros_like(out_ref)

    def compute(j, slot, window):
        base = jnp.minimum((begin[j] // 16) * 16, rows - window)
        base = pl.multiple_of(base, 16)
        span = pl.ds(base, window)
        found = attend(
            q_ref[span, :], dims, window, buffer.at[slot], None, (s0, s1), (p0, p1), True
        )
        row = base + lax.broadcasted_iota(jnp.int32, (window, STAT), 0)
        live = (row >= begin[j]) & (row < end[j])
        for k, (mixed, _) in enumerate(found):
            for g in range(group):
                cut = slice((k * group + g) * head, (k * group + g + 1) * head)
                old = out_ref[span, cut].astype(jnp.float32)
                part = jnp.where(live, mixed[g * window : (g + 1) * window], old)
                out_ref[span, cut] = part.astype(jnp.bfloat16)
        old = out_ref[span, width : width + STAT].astype(jnp.float32)
        new = split_stat([f[1] for f in found], group, window)
        out_ref[span, width : width + STAT] = jnp.where(live, new, old).astype(jnp.bfloat16)

    def step(j, carry):
        slot = lax.rem(j, 2)

        @pl.when(j + 1 < count)
        def _():
            start(j + 1, 1 - slot)

        await_pages(own_ref, pages, buffer, slot, sem)
        need = (end[j] - (begin[j] // 16) * 16 + 15) // 16
        for blocks in (1, 2, 3):
            if 16 * blocks <= rows:

                @pl.when(need == blocks)
                def _():
                    compute(j, slot, 16 * blocks)

        return carry

    lax.fori_loop(0, count, step, 0)


def far(chunk, meta, own, sib, dims, chips, first):
    rows, width = chunk.shape
    requests, steps, kv, group, head, pages = dims
    kernel = functools.partial(far_kernel, chips, dims, first, rows)
    if kv == 1:
        kernel = one_head_kernel(kernel, 6)
    return pl.pallas_call(
        kernel,
        in_specs=[sspec(), vspec(), anyspec(), anyspec()],
        out_specs=vspec(),
        out_shape=jax.ShapeDtypeStruct((rows, width + STAT), jnp.bfloat16),
        scratch_shapes=[pltpu.VMEM((2, pages) + own.shape[1:], jnp.bfloat16)]
        + score_scratch(kv, pages * own.shape[2], group * min(48, rows))
        + [
            pltpu.SMEM((requests + 1,), jnp.int32),
            pltpu.SMEM((requests + 1,), jnp.int32),
            pltpu.SMEM((requests + 1,), jnp.int32),
            pltpu.SemaphoreType.DMA((2,)),
        ],
        compiler_params=pltpu.CompilerParams(vmem_limit_bytes=VMEM_LIMIT),
        cost_estimate=pl.CostEstimate(
            flops=rows * (24 << 20),
            bytes_accessed=rows * (60 << 10),
            transcendentals=rows * (16 << 10),
        ),
        name="far",
    )(meta, chunk, own, sib)


def merge_kernel(
    chips, dims, chunk, len_ref, dst_ref, old_ref, stat_ref, back_ref, ctx_ref, tiles, todo, begin,
    take_sem, give_sem,
):
    requests, steps, kv, group, head, pages = dims
    way, first, rows = chunk
    heads = kv * group
    width = heads * head

    def listing(i, carry):
        count, row = carry
        size = jnp.where(shift_of(dst_ref[i], chips) == way, len_ref[i], 0)
        low = jnp.maximum(row, first)
        high = jnp.minimum(row + size, first + rows)
        todo[count] = i
        begin[count] = row - first
        return count + (high > low).astype(jnp.int32), row + size

    count, _ = lax.fori_loop(0, requests, listing, (jnp.int32(0), jnp.int32(0)))

    def take(j):
        return pltpu.make_async_copy(old_ref.at[todo[j]], tiles.at[j], take_sem.at[j])

    def give(j):
        return pltpu.make_async_copy(tiles.at[j], ctx_ref.at[todo[j]], give_sem.at[j])

    def issue(j, carry):
        take(j).start()
        return carry

    lax.fori_loop(0, count, issue, 0)
    lane = lax.broadcasted_iota(jnp.int32, (STAT, width), 0)
    col = lax.broadcasted_iota(jnp.int32, (STAT, width), 1) // head
    spread = jnp.where((lax.rem(lane, heads) == col) & (lane < 3 * heads), 1.0, 0.0)
    spread = spread.astype(jnp.bfloat16)

    def step(j, carry):
        i = todo[j]
        token = lax.broadcasted_iota(jnp.int32, (steps, rows), 0)
        row = lax.broadcasted_iota(jnp.int32, (steps, rows), 1)
        hot = (begin[j] + token == row) & (token < len_ref[i])
        hot = jnp.where(hot, 1.0, 0.0).astype(jnp.bfloat16)
        got = jnp.dot(hot, back_ref[...], preferred_element_type=jnp.float32)
        far_sum = jnp.dot(
            got[:, width:].astype(jnp.bfloat16), spread, preferred_element_type=jnp.float32
        )
        near_sum = jnp.dot(stat_ref[i], spread, preferred_element_type=jnp.float32)
        share = 1.0 / (1.0 + jnp.exp2(near_sum - far_sum))
        take(j).wait()
        near = tiles[j].astype(jnp.float32)
        mixed = near + share * (got[:, 0:width] - near)
        token = lax.broadcasted_iota(jnp.int32, (steps, width), 0)
        here = begin[j] + token
        live = (token < len_ref[i]) & (here >= 0) & (here < rows)
        tiles[j] = jnp.where(live, mixed, near).astype(jnp.bfloat16)
        give(j).start()
        return carry

    lax.fori_loop(0, count, step, 0)

    def drain(j, carry):
        give(j).wait()
        return carry

    lax.fori_loop(0, count, drain, 0)


def merge(ctx, stat, back, lengths, target, dims, chips, chunk, room):
    requests, steps, width = ctx.shape
    return pl.pallas_call(
        functools.partial(merge_kernel, chips, dims, chunk),
        in_specs=[sspec(), sspec(), anyspec(), vspec(), vspec()],
        out_specs=anyspec(),
        out_shape=jax.ShapeDtypeStruct(ctx.shape, jnp.bfloat16),
        input_output_aliases={2: 0},
        scratch_shapes=[
            pltpu.VMEM((room, steps, width), jnp.bfloat16),
            pltpu.SMEM((requests + 1,), jnp.int32),
            pltpu.SMEM((requests + 1,), jnp.int32),
            pltpu.SemaphoreType.DMA((room,)),
            pltpu.SemaphoreType.DMA((room,)),
        ],
        compiler_params=pltpu.CompilerParams(vmem_limit_bytes=VMEM_LIMIT),
        cost_estimate=pl.CostEstimate(
            flops=chunk[2] * (12 << 20), bytes_accessed=chunk[2] * (16 << 10), transcendentals=0
        ),
        name="merge",
    )(lengths, target, ctx, stat, back)


def shards(queries, suffix_key_value, kv_pool, page_table, lengths, destination):
    replicas = lax.axis_size("replica")
    chips = replicas // 2
    requests, steps, width = queries.shape
    kv, head = suffix_key_value.shape[2], suffix_key_value.shape[3] // 2
    pages = page_table.shape[1]
    dims = (requests, steps, kv, width // (kv * head), head, pages)
    target = destination[:, 0]
    here = lax.axis_index("replica") >> 1
    ways = range(1, chips)

    room = 2 * (requests // replicas + 1)
    most = room * steps
    sizes = [most]
    if chips == 2:
        mean = requests * steps // (2 * chips)
        sizes = []
        for eighths in (9, 10, 11, 13):
            size = -(-(mean * eighths) // (8 * 32)) * 32
            if size < most and size not in sizes:
                sizes.append(size)
        sizes.append(most)
    base = sizes[0]
    main = [(s, f, min(96, base - f)) for s in ways for f in range(0, base, 96)]
    extra = [(1, low, high - low) for low, high in zip(sizes[:-1], sizes[1:])]

    def away(s):
        return [(r, (r + 2 * s) % replicas) for r in range(replicas)]

    def back(s):
        return [((r + 2 * s) % replicas, r) for r in range(replicas)]

    meta = jnp.concatenate([page_table, lengths[:, None], destination], axis=1)
    metas = {s: lax.ppermute(meta, "replica", away(s)) for s in ways}
    packed = pack(queries, lengths, target, chips, main)
    arrived = [lax.ppermute(rows, "replica", away(c[0])) for rows, c in zip(packed, main)]
    kv_pool, packed = lax.optimization_barrier((kv_pool, packed))

    own = jnp.transpose(kv_pool, (0, 2, 1, 3))
    sib = lax.ppermute(own, "replica", [(r, r ^ 1) for r in range(replicas)])
    suffix = jnp.transpose(suffix_key_value, (0, 2, 1, 3))
    ctx, stat = near_part(queries, suffix, lengths, target, dims, chips)
    ctx = local(queries, suffix, own, sib, ctx, page_table, lengths, target, dims, chips)

    def serve(rows, c):
        return far(rows, metas[c[0]], own, sib, dims, chips, c[1])

    def finish(ctx, served, chunks):
        came = [lax.ppermute(rows, "replica", back(c[0])) for rows, c in zip(served, chunks)]
        for rows, c in zip(came, chunks):
            ctx = merge(ctx, stat, rows, lengths, target, dims, chips, c, room)
        return ctx

    if not extra:
        return finish(ctx, [serve(r, c) for r, c in zip(arrived, main)], main)

    widest = jnp.zeros((), jnp.int32)
    for s, table in [(0, meta)] + [(s, metas[s]) for s in ways]:
        sender = lax.rem(here - s + chips, chips)
        for chip in range(chips):
            goes = ((table[:, pages + 1] >> 1) == chip) & (sender != chip)
            widest = jnp.maximum(widest, jnp.sum(jnp.where(goes, table[:, pages], 0)))
    widest = widest.reshape(1)
    widest = jnp.maximum(
        widest, lax.ppermute(widest, "replica", [(r, r ^ 1) for r in range(replicas)])
    )
    parts = lax.axis_size("groups")
    for hop in range(1, parts):
        widest = jnp.maximum(
            widest,
            lax.ppermute(widest, "groups", [(g, (g + hop) % parts) for g in range(parts)]),
        )
    widest = widest[0]

    packed_more = pack(queries, lengths, target, chips, extra)
    served = [serve(r, c) for r, c in zip(arrived[:-1], main[:-1])]

    def branch(count):
        def run():
            more = [lax.ppermute(r, "replica", away(1)) for r in packed_more[:count]]
            last = [serve(arrived[-1], main[-1])]
            rest = [serve(r, c) for r, c in zip(more, extra)]
            return finish(ctx, served + last + rest, main + extra[:count])

        return run

    level = sum((widest > size).astype(jnp.int32) for size in sizes[:-1])
    return lax.switch(level, [branch(n) for n in range(len(sizes))])


def solution(mesh):
    return jax.shard_map(
        shards,
        mesh=mesh,
        in_specs=(
            P(("groups", "replica"), None, "tensor"),
            P(("groups", "replica"), None, "tensor", None),
            P(("groups", "replica"), None, "tensor", None),
            P(("groups", "replica"), None),
            P(("groups", "replica")),
            P(("groups", "replica"), None),
        ),
        out_specs=P(("groups", "replica"), None, "tensor"),
        check_vma=False,
    )
```

```python
import functools
import math

import jax
import jax.numpy as jnp
from jax import lax
from jax.experimental import pallas as pl
from jax.experimental.pallas import tpu as pltpu
from jax.sharding import PartitionSpec as P

BIG = 1 << 14
STAT = 128
VMEM_LIMIT = 60 << 20


def vspec():
    return pl.BlockSpec(memory_space=pltpu.VMEM)


def sspec():
    return pl.BlockSpec(memory_space=pltpu.SMEM)


def anyspec():
    return pl.BlockSpec(memory_space=pl.ANY)


def shift_of(target, chips):
    here = lax.axis_index("replica") >> 1
    step = (target >> 1) - here
    return jnp.where(step < 0, step + chips, step)


def flow(chips, requests, way, first, rows, size_of, to_of, todo, begin):
    def listing(i, carry):
        count, row = carry
        size = jnp.where(shift_of(to_of(i), chips) == way, size_of(i), 0)
        low = jnp.maximum(row, first)
        high = jnp.minimum(row + size, first + rows)
        todo[count] = i
        begin[count] = row - first
        return count + (high > low).astype(jnp.int32), row + size

    return lax.fori_loop(0, requests, listing, (jnp.int32(0), jnp.int32(0)))[0]


def pack_kernel(
    chips, chunk, requests, len_ref, dst_ref, q_ref, out_ref, tiles, total, hot, todo, begin, sem
):
    way, first, rows = chunk
    many, steps, width = tiles.shape[1:]
    count = flow(
        chips, requests, way, first, rows, lambda i: len_ref[i], lambda i: dst_ref[i], todo, begin
    )
    blocks = (count + many - 1) // many

    def take(j, slot, u):
        i = todo[jnp.minimum(j * many + u, count - 1)]
        return pltpu.make_async_copy(q_ref.at[i], tiles.at[slot, u], sem.at[slot, u])

    def start(j, slot):
        for u in range(many):
            take(j, slot, u).start()

    @pl.when(count > 0)
    def _():
        start(0, 0)

    total[...] = jnp.zeros_like(total)

    def step(j, carry):
        slot = lax.rem(j, 2)

        @pl.when(j + 1 < blocks)
        def _():
            start(j + 1, 1 - slot)

        row = lax.broadcasted_iota(jnp.int32, (rows, many * steps), 0)
        lane = lax.broadcasted_iota(jnp.int32, (1, many * steps), 1)
        place = jnp.full((1, many * steps), -1, jnp.int32)
        for u in range(many):
            n = jnp.minimum(j * many + u, count - 1)
            size = jnp.where(j * many + u < count, len_ref[todo[n]], 0)
            token = lane - u * steps
            place = jnp.where((token >= 0) & (token < size), begin[n] + token, place)
        hot[...] = jnp.where(row == place, 1.0, 0.0).astype(jnp.bfloat16)
        for u in range(many):
            take(j, slot, u).wait()
        block = tiles[slot].reshape(many * steps, width)
        total[...] += jnp.dot(hot[...], block, preferred_element_type=jnp.float32)
        return carry

    lax.fori_loop(0, blocks, step, 0)
    out_ref[...] = total[...].astype(out_ref.dtype)


def pack(queries, lengths, target, chips, chunk):
    requests, steps, width = queries.shape
    rows = chunk[2]
    many = 8
    return pl.pallas_call(
        functools.partial(pack_kernel, chips, chunk, requests),
        in_specs=[sspec(), sspec(), anyspec()],
        out_specs=vspec(),
        out_shape=jax.ShapeDtypeStruct((rows, width), jnp.bfloat16),
        scratch_shapes=[
            pltpu.VMEM((2, many, steps, width), jnp.bfloat16),
            pltpu.VMEM((rows, width), jnp.float32),
            pltpu.VMEM((rows, many * steps), jnp.bfloat16),
            pltpu.SMEM((requests + 1,), jnp.int32),
            pltpu.SMEM((requests + 1,), jnp.int32),
            pltpu.SemaphoreType.DMA((2, many)),
        ],
        compiler_params=pltpu.CompilerParams(vmem_limit_bytes=VMEM_LIMIT),
        cost_estimate=pl.CostEstimate(
            flops=1 << 28, bytes_accessed=rows * width * 4, transcendentals=0
        ),
        name="pack",
    )(lengths, target, queries)


def nt_dot(a, b):
    return lax.dot_general(a, b, (((1,), (1,)), ((), ())), preferred_element_type=jnp.float32)


def tn_dot(a, b):
    return lax.dot_general(a, b, (((0,), (0,)), ((), ())), preferred_element_type=jnp.float32)


def fold(x, op):
    rows, cols = x.shape
    x = x.reshape(rows // 8, 8, cols)
    return jnp.max(x, axis=0) if op == "max" else jnp.sum(x, axis=0)


def attend(q, dims, window, pool, ids, suffix, s_refs, p_refs, want_sum):
    requests, steps, kv, group, head, pages = dims
    coeff = math.log2(math.e) / math.sqrt(head)
    cols = group * window
    found = []
    for k in range(kv):
        qk = jnp.concatenate(
            [q[:, (k * group + g) * head : (k * group + g + 1) * head] for g in range(group)], axis=0
        )
        top = None
        near = None
        if pool is not None:
            per = pool.shape[2]
            count = 4 if pages % 4 == 0 else 1
            for p in range(0, pages, count):
                keys = jnp.concatenate(
                    [pool[ids[n], k, :, 0:head] for n in range(p, p + count)], axis=0
                )
                score = nt_dot(keys, qk)
                s_refs[k][p * per : (p + count) * per, 0:cols] = score
                best = fold(score, "max")
                top = best if top is None else jnp.maximum(top, best)
        if suffix is not None:
            near = nt_dot(suffix[k, :, 0:head], qk)
            key = lax.broadcasted_iota(jnp.int32, (steps, cols), 0)
            token = lax.rem(lax.broadcasted_iota(jnp.int32, (steps, cols), 1), window)
            mask = key <= token
            near = jnp.where(mask, near, -1e30)
            best = fold(near, "max")
            top = best if top is None else jnp.maximum(top, best)
        found.append((jnp.max(top, axis=0, keepdims=True) * coeff, near))
    results = []
    for k in range(kv):
        level, near = found[k]
        total = None
        mixed = None
        if pool is not None:
            per = pool.shape[2]
            for p in range(pages):
                span = slice(p * per, (p + 1) * per)
                weight = jnp.exp2(s_refs[k][span, 0:cols] * coeff - level)
                part = fold(weight, "sum")
                total = part if total is None else total + part
                p_refs[k][span, 0:cols] = weight.astype(jnp.bfloat16)
            values = jnp.concatenate([pool[n, k, :, head : 2 * head] for n in ids], axis=0)
            mixed = tn_dot(values, p_refs[k][:, 0:cols])
        if near is not None:
            key = lax.broadcasted_iota(jnp.int32, (steps, cols), 0)
            token = lax.rem(lax.broadcasted_iota(jnp.int32, (steps, cols), 1), window)
            weight = jnp.where(key <= token, jnp.exp2(near * coeff - level), 0.0)
            part = fold(weight, "sum")
            total = part if total is None else total + part
            more = tn_dot(suffix[k, :, head : 2 * head], weight.astype(jnp.bfloat16))
            mixed = more if mixed is None else mixed + more
        total = jnp.sum(total, axis=0, keepdims=True)
        mixed = (mixed * (1.0 / total)).T
        lse = None
        if want_sum:
            lse = jnp.broadcast_to(level + jnp.log2(total), (STAT, cols)).T
        results.append((mixed, lse))
    return results


def split_stat(values, group, window):
    lane = lax.broadcasted_iota(jnp.int32, (window, STAT), 1)
    count = len(values) * group
    which = lax.rem(lane, count)
    stat = jnp.zeros((window, STAT), jnp.float32)
    for k, value in enumerate(values):
        for g in range(group):
            stat = jnp.where(which == k * group + g, value[g * window : (g + 1) * window], stat)
    high = stat.astype(jnp.bfloat16).astype(jnp.float32)
    rest = stat - high
    middle = rest.astype(jnp.bfloat16).astype(jnp.float32)
    low = rest - middle
    part = lane // count
    stat = jnp.where(part == 0, high, jnp.where(part == 1, middle, low))
    return jnp.where(part < 3, stat, 0.0)


def load_pools(own_ref, sib_ref, pool, sem):
    count = own_ref.shape[0]
    return (
        pltpu.make_async_copy(own_ref, pool.at[pl.ds(0, count)], sem.at[0]),
        pltpu.make_async_copy(sib_ref, pool.at[pl.ds(count, count)], sem.at[1]),
    )


def own_first(count, is_own, todo, others):
    def move(j, owned):
        own = is_own(todo[j])
        for ref in (todo,) + others:
            here, there = ref[j], ref[owned]
            ref[j] = jnp.where(own, there, here)
            ref[owned] = jnp.where(own, here, there)
        return owned + own.astype(jnp.int32)

    return lax.fori_loop(0, count, move, jnp.int32(0))


def score_scratch(kv, keys, cols):
    return [pltpu.VMEM((keys, cols), jnp.float32) for _ in range(kv)] + [
        pltpu.VMEM((keys, cols), jnp.bfloat16) for _ in range(kv)
    ]


RING = 4


def near_kernel(
    chips, dims, len_ref, dst_ref, q_ref, suf_ref, ctx_ref, stat_ref, q_buf, o_buf, todo, q_sem, o_sem
):
    requests, steps, kv, group, head, pages = dims

    def listing(i, count):
        todo[count] = i
        return count + (shift_of(dst_ref[i], chips) != 0).astype(jnp.int32)

    count = lax.fori_loop(0, requests, listing, jnp.int32(0))

    def take(j):
        slot = lax.rem(j, RING)
        return pltpu.make_async_copy(q_ref.at[todo[j]], q_buf.at[slot], q_sem.at[slot])

    def give(j):
        slot = lax.rem(j, RING)
        return pltpu.make_async_copy(o_buf.at[slot], ctx_ref.at[todo[j]], o_sem.at[slot])

    def ahead(j, carry):
        take(j).start()
        return carry

    lax.fori_loop(0, jnp.minimum(count, RING - 1), ahead, 0)
    stat_ref[...] = jnp.zeros_like(stat_ref)

    def step(j, carry):
        slot = lax.rem(j, RING)

        @pl.when(j + RING - 1 < count)
        def _():
            take(j + RING - 1).start()

        @pl.when(j >= RING)
        def _():
            give(j - RING).wait()

        take(j).wait()
        i = todo[j]
        found = attend(q_buf[slot], dims, steps, None, None, suf_ref.at[i], None, None, True)
        live = lax.broadcasted_iota(jnp.int32, (steps, head), 0) < len_ref[i]
        for k, (mixed, lse) in enumerate(found):
            for g in range(group):
                h = k * group + g
                part = jnp.where(live, mixed[g * steps : (g + 1) * steps], 0.0)
                o_buf[slot, :, h * head : (h + 1) * head] = part.astype(jnp.bfloat16)
        stat_ref[i] = split_stat([f[1] for f in found], group, steps).astype(jnp.bfloat16)
        give(j).start()
        return carry

    lax.fori_loop(0, count, step, 0)

    def drain(j, carry):
        give(j).wait()
        return carry

    lax.fori_loop(jnp.maximum(count - RING, 0), count, drain, 0)


def near_part(queries, suffix, lengths, target, dims, chips):
    requests, steps, width = queries.shape
    return pl.pallas_call(
        functools.partial(near_kernel, chips, dims),
        in_specs=[sspec(), sspec(), anyspec(), vspec()],
        out_specs=[anyspec(), vspec()],
        out_shape=[
            jax.ShapeDtypeStruct(queries.shape, jnp.bfloat16),
            jax.ShapeDtypeStruct((requests, steps, STAT), jnp.bfloat16),
        ],
        scratch_shapes=[
            pltpu.VMEM((RING, steps, width), jnp.bfloat16),
            pltpu.VMEM((RING, steps, width), jnp.bfloat16),
            pltpu.SMEM((requests + 1,), jnp.int32),
            pltpu.SemaphoreType.DMA((RING,)),
            pltpu.SemaphoreType.DMA((RING,)),
        ],
        compiler_params=pltpu.CompilerParams(vmem_limit_bytes=VMEM_LIMIT),
        cost_estimate=pl.CostEstimate(
            flops=1 << 30, bytes_accessed=2 << 20, transcendentals=1 << 10
        ),
        name="near",
    )(lengths, target, queries, suffix)


def local_kernel(
    chips, dims, len_ref, dst_ref, table_ref, q_ref, suf_ref, own_ref, sib_ref, old_ref,
    ctx_ref, pool, q_buf, o_buf, todo, sem, q_sem, o_sem, *scores,
):
    requests, steps, kv, group, head, pages = dims
    core = lax.rem(lax.axis_index("replica"), 2)
    s_refs, p_refs = scores[:kv], scores[kv:]
    held = own_ref.shape[0]
    load_own, load_sib = load_pools(own_ref, sib_ref, pool, sem)
    load_own.start()
    load_sib.start()

    def listing(i, count):
        todo[count] = i
        return count + (shift_of(dst_ref[i], chips) == 0).astype(jnp.int32)

    count = lax.fori_loop(0, requests, listing, jnp.int32(0))
    owned = own_first(count, lambda i: lax.rem(dst_ref[i], 2) == core, todo, ())

    def take(j):
        slot = lax.rem(j, RING)
        return pltpu.make_async_copy(q_ref.at[todo[j]], q_buf.at[slot], q_sem.at[slot])

    def give(j):
        slot = lax.rem(j, RING)
        return pltpu.make_async_copy(o_buf.at[slot], ctx_ref.at[todo[j]], o_sem.at[slot])

    def ahead(j, carry):
        take(j).start()
        return carry

    lax.fori_loop(0, jnp.minimum(count, RING - 1), ahead, 0)

    def compute(i, slot, ids, window):
        found = attend(
            q_buf[slot, 0:window, :], dims, window, pool, ids, suf_ref.at[i], s_refs, p_refs, False
        )
        live = lax.broadcasted_iota(jnp.int32, (window, head), 0) < len_ref[i]
        for k, (mixed, _) in enumerate(found):
            for g in range(group):
                h = k * group + g
                part = jnp.where(live, mixed[g * window : (g + 1) * window], 0.0)
                o_buf[slot, 0:window, h * head : (h + 1) * head] = part.astype(jnp.bfloat16)
        if window < steps:
            o_buf[slot, window:steps, :] = jnp.zeros(
                (steps - window, o_buf.shape[2]), jnp.bfloat16
            )

    load_own.wait()

    @pl.when(owned == count)
    def _():
        load_sib.wait()

    def step(j, carry):
        slot = lax.rem(j, RING)

        @pl.when(j + RING - 1 < count)
        def _():
            take(j + RING - 1).start()

        @pl.when(j >= RING)
        def _():
            give(j - RING).wait()

        @pl.when(j == owned)
        def _():
            load_sib.wait()

        take(j).wait()
        i = todo[j]
        shift = jnp.where(j < owned, 0, held)
        ids = [table_ref[i, p] + shift for p in range(pages)]
        small = len_ref[i] <= steps // 2

        @pl.when(small)
        def _():
            compute(i, slot, ids, steps // 2)

        @pl.when(jnp.logical_not(small))
        def _():
            compute(i, slot, ids, steps)

        give(j).start()
        return carry

    lax.fori_loop(0, count, step, 0)

    def drain(j, carry):
        give(j).wait()
        return carry

    lax.fori_loop(jnp.maximum(count - RING, 0), count, drain, 0)


def local(queries, suffix, own, sib, ctx, table, lengths, target, dims, chips):
    requests, steps, kv, group, head, pages = dims
    width = queries.shape[2]
    held = own.shape[0]
    return pl.pallas_call(
        functools.partial(local_kernel, chips, dims),
        in_specs=[sspec(), sspec(), sspec(), anyspec(), vspec()] + [anyspec()] * 3,
        out_specs=anyspec(),
        out_shape=jax.ShapeDtypeStruct(queries.shape, jnp.bfloat16),
        input_output_aliases={7: 0},
        scratch_shapes=[
            pltpu.VMEM((2 * held,) + own.shape[1:], jnp.bfloat16),
            pltpu.VMEM((RING, steps, width), jnp.bfloat16),
            pltpu.VMEM((RING, steps, width), jnp.bfloat16),
            pltpu.SMEM((requests + 1,), jnp.int32),
            pltpu.SemaphoreType.DMA((2,)),
            pltpu.SemaphoreType.DMA((RING,)),
            pltpu.SemaphoreType.DMA((RING,)),
        ]
        + score_scratch(kv, pages * own.shape[2], group * steps),
        compiler_params=pltpu.CompilerParams(vmem_limit_bytes=VMEM_LIMIT),
        cost_estimate=pl.CostEstimate(
            flops=2 << 30, bytes_accessed=8 << 20, transcendentals=1 << 10
        ),
        name="local",
    )(lengths, target, table, queries, suffix, own, sib, ctx)


def far_kernel(
    chips, dims, first, rows, meta_ref, q_ref, own_ref, sib_ref, out_ref, pool, todo, begin, sem,
    *scores,
):
    requests, steps, kv, group, head, pages = dims
    core = lax.rem(lax.axis_index("replica"), 2)
    width = kv * group * head
    s_refs, p_refs = scores[:kv], scores[kv:]
    held = own_ref.shape[0]
    load_own, load_sib = load_pools(own_ref, sib_ref, pool, sem)
    load_own.start()
    load_sib.start()
    count = flow(
        chips, requests, 0, first, rows, lambda i: meta_ref[i, pages],
        lambda i: meta_ref[i, pages + 1], todo, begin,
    )
    owned = own_first(
        count, lambda i: lax.rem(meta_ref[i, pages + 1], 2) == core, todo, (begin,)
    )
    out_ref[...] = jnp.zeros_like(out_ref)

    def compute(low, high, ids, window):
        base = jnp.minimum((low // 16) * 16, rows - window)
        base = pl.multiple_of(base, 16)
        span = pl.ds(base, window)
        found = attend(q_ref[span, :], dims, window, pool, ids, None, s_refs, p_refs, True)
        row = base + lax.broadcasted_iota(jnp.int32, (window, STAT), 0)
        live = (row >= low) & (row < high)
        for k, (mixed, _) in enumerate(found):
            for g in range(group):
                cut = slice((k * group + g) * head, (k * group + g + 1) * head)
                old = out_ref[span, cut].astype(jnp.float32)
                part = jnp.where(live, mixed[g * window : (g + 1) * window], old)
                out_ref[span, cut] = part.astype(jnp.bfloat16)
        old = out_ref[span, width : width + STAT].astype(jnp.float32)
        new = split_stat([f[1] for f in found], group, window)
        out_ref[span, width : width + STAT] = jnp.where(live, new, old).astype(jnp.bfloat16)

    load_own.wait()

    @pl.when(owned == count)
    def _():
        load_sib.wait()

    def step(j, carry):
        @pl.when(j == owned)
        def _():
            load_sib.wait()

        i = todo[j]
        shift = jnp.where(j < owned, 0, held)
        ids = [meta_ref[i, p] + shift for p in range(pages)]
        low = jnp.maximum(begin[j], 0)
        high = jnp.minimum(begin[j] + meta_ref[i, pages], rows)
        need = (high - (low // 16) * 16 + 15) // 16
        for blocks in (1, 2, 3):
            if 16 * blocks <= rows:

                @pl.when(need == blocks)
                def _():
                    compute(low, high, ids, 16 * blocks)

        return carry

    lax.fori_loop(0, count, step, 0)


def far(chunk, meta, own, sib, dims, chips, first):
    rows, width = chunk.shape
    requests, steps, kv, group, head, pages = dims
    held = own.shape[0]
    return pl.pallas_call(
        functools.partial(far_kernel, chips, dims, first, rows),
        in_specs=[sspec(), vspec(), anyspec(), anyspec()],
        out_specs=vspec(),
        out_shape=jax.ShapeDtypeStruct((rows, width + STAT), jnp.bfloat16),
        scratch_shapes=[
            pltpu.VMEM((2 * held,) + own.shape[1:], jnp.bfloat16),
            pltpu.SMEM((requests + 1,), jnp.int32),
            pltpu.SMEM((requests + 1,), jnp.int32),
            pltpu.SemaphoreType.DMA((2,)),
        ]
        + score_scratch(kv, pages * own.shape[2], group * min(48, rows)),
        compiler_params=pltpu.CompilerParams(vmem_limit_bytes=VMEM_LIMIT),
        cost_estimate=pl.CostEstimate(
            flops=2 << 30, bytes_accessed=8 << 20, transcendentals=1 << 10
        ),
        name="far",
    )(meta, chunk, own, sib)


def merge_kernel(
    chips, dims, chunk, len_ref, dst_ref, old_ref, stat_ref, back_ref, ctx_ref, tiles, got, hot,
    todo, begin, take_sem, give_sem,
):
    requests, steps, kv, group, head, pages = dims
    way, first, rows = chunk
    heads = kv * group
    width = heads * head
    many = got.shape[0] // steps
    count = flow(
        chips, requests, way, first, rows, lambda i: len_ref[i], lambda i: dst_ref[i], todo, begin
    )

    def take(j):
        return pltpu.make_async_copy(old_ref.at[todo[j]], tiles.at[j], take_sem.at[j])

    def give(j):
        return pltpu.make_async_copy(tiles.at[j], ctx_ref.at[todo[j]], give_sem.at[j])

    def issue(j, carry):
        take(j).start()
        return carry

    lax.fori_loop(0, count, issue, 0)

    def whole(stat):
        return (
            stat
            + pltpu.roll(stat, STAT - heads, axis=1)
            + pltpu.roll(stat, STAT - 2 * heads, axis=1)
        )

    def one(j, u):
        i = todo[j]
        span = pl.ds(pl.multiple_of(u * steps, steps), steps)
        far_sum = whole(got[span, width : width + STAT])
        near_sum = whole(stat_ref[i].astype(jnp.float32))
        share = 1.0 / (1.0 + jnp.exp2(near_sum - far_sum))
        token = lax.broadcasted_iota(jnp.int32, (steps, STAT), 0)
        here = begin[j] + token
        share = jnp.where((token < len_ref[i]) & (here >= 0) & (here < rows), share, 0.0)
        take(j).wait()
        for h in range(heads):
            cut = slice(h * head, (h + 1) * head)
            near = tiles[j, :, cut].astype(jnp.float32)
            mixed = near + share[:, h : h + 1] * (got[span, cut] - near)
            tiles[j, :, cut] = mixed.astype(jnp.bfloat16)
        give(j).start()

    def block(b, carry):
        for u in range(many):
            j = jnp.minimum(b * many + u, count - 1)
            size = jnp.where(b * many + u < count, len_ref[todo[j]], 0)
            token = lax.broadcasted_iota(jnp.int32, (steps, rows), 0)
            row = lax.broadcasted_iota(jnp.int32, (steps, rows), 1)
            match = (begin[j] + token == row) & (token < size)
            hot[u * steps : (u + 1) * steps, :] = jnp.where(match, 1.0, 0.0).astype(jnp.bfloat16)
        got[...] = jnp.dot(hot[...], back_ref[...], preferred_element_type=jnp.float32)

        def each(u, inner):
            one(b * many + u, u)
            return inner

        lax.fori_loop(0, jnp.minimum(count - b * many, many), each, 0)
        return carry

    lax.fori_loop(0, (count + many - 1) // many, block, 0)

    def drain(j, carry):
        give(j).wait()
        return carry

    lax.fori_loop(0, count, drain, 0)


def merge(ctx, stat, back, lengths, target, dims, chips, chunk, room):
    requests, steps, width = ctx.shape
    many = 8
    return pl.pallas_call(
        functools.partial(merge_kernel, chips, dims, chunk),
        in_specs=[sspec(), sspec(), anyspec(), vspec(), vspec()],
        out_specs=anyspec(),
        out_shape=jax.ShapeDtypeStruct(ctx.shape, jnp.bfloat16),
        input_output_aliases={2: 0},
        scratch_shapes=[
            pltpu.VMEM((room, steps, width), jnp.bfloat16),
            pltpu.VMEM((many * steps, width + STAT), jnp.float32),
            pltpu.VMEM((many * steps, chunk[2]), jnp.bfloat16),
            pltpu.SMEM((requests + 1,), jnp.int32),
            pltpu.SMEM((requests + 1,), jnp.int32),
            pltpu.SemaphoreType.DMA((room,)),
            pltpu.SemaphoreType.DMA((room,)),
        ],
        compiler_params=pltpu.CompilerParams(vmem_limit_bytes=VMEM_LIMIT),
        cost_estimate=pl.CostEstimate(
            flops=1 << 29, bytes_accessed=chunk[2] * (8 << 10), transcendentals=0
        ),
        name="merge",
    )(lengths, target, ctx, stat, back)


def shards(queries, suffix_key_value, kv_pool, page_table, lengths, destination):
    replicas = lax.axis_size("replica")
    chips = replicas // 2
    requests, steps, width = queries.shape
    kv, head = suffix_key_value.shape[2], suffix_key_value.shape[3] // 2
    pages = page_table.shape[1]
    dims = (requests, steps, kv, width // (kv * head), head, pages)
    target = destination[:, 0]
    here = lax.axis_index("replica") >> 1
    ways = range(1, chips)

    room = 2 * (requests // replicas + 1)
    most = room * steps
    mean = requests * steps // (2 * chips)
    base = min(most, -(-(mean * 3) // (4 * 32)) * 32)
    sizes = [most - base]
    if chips == 2:
        sizes = []
        for eighths in (9, 10, 11, 13):
            size = -(-(mean * eighths) // (8 * 32)) * 32 - base
            if 0 < size < most - base and size not in sizes:
                sizes.append(size)
        sizes.append(most - base)

    def away(s):
        return [(r, (r + 2 * s) % replicas) for r in range(replicas)]

    def back(s):
        return [((r + 2 * s) % replicas, r) for r in range(replicas)]

    meta = jnp.concatenate([page_table, lengths[:, None], destination], axis=1)
    metas = {s: lax.ppermute(meta, "replica", away(s)) for s in ways}
    packed = [pack(queries, lengths, target, chips, (s, 0, base)) for s in ways]
    arrived = [lax.ppermute(rows, "replica", away(s)) for s, rows in zip(ways, packed)]
    kv_pool, packed = lax.optimization_barrier((kv_pool, packed))

    own = jnp.transpose(kv_pool, (0, 2, 1, 3))
    sib = lax.ppermute(own, "replica", [(r, r ^ 1) for r in range(replicas)])
    suffix = jnp.transpose(suffix_key_value, (0, 2, 1, 3))
    ctx, stat = near_part(queries, suffix, lengths, target, dims, chips)

    def serve(rows, s, first):
        out = far(rows, metas[s], own, sib, dims, chips, first)
        return lax.ppermute(out, "replica", back(s))

    packed_more = [pack(queries, lengths, target, chips, (s, base, most - base)) for s in ways]

    def finish(size):
        def run():
            more = [lax.ppermute(r[:size], "replica", away(s)) for s, r in zip(ways, packed_more)]
            came = [(serve(r, s, 0), (s, 0, base)) for s, r in zip(ways, arrived)]
            done = local(queries, suffix, own, sib, ctx, page_table, lengths, target, dims, chips)
            came += [(serve(r, s, base), (s, base, size)) for s, r in zip(ways, more)]
            for rows, chunk in came:
                done = merge(done, stat, rows, lengths, target, dims, chips, chunk, room)
            return done

        return run

    if len(sizes) == 1:
        return finish(sizes[0])()

    widest = jnp.zeros((), jnp.int32)
    for s, table in [(0, meta)] + [(s, metas[s]) for s in ways]:
        sender = lax.rem(here - s + chips, chips)
        for chip in range(chips):
            goes = ((table[:, pages + 1] >> 1) == chip) & (sender != chip)
            widest = jnp.maximum(widest, jnp.sum(jnp.where(goes, table[:, pages], 0)))
    widest = widest.reshape(1)
    widest = jnp.maximum(
        widest, lax.ppermute(widest, "replica", [(r, r ^ 1) for r in range(replicas)])
    )
    seen = widest
    parts = lax.axis_size("groups")
    for hop in range(1, parts):
        other = lax.ppermute(seen, "groups", [(g, (g + hop) % parts) for g in range(parts)])
        widest = jnp.maximum(widest, other)
    level = sum((widest[0] > base + size).astype(jnp.int32) for size in sizes[:-1])
    return lax.switch(level, [finish(size) for size in sizes])


def solution(mesh):
    return jax.shard_map(
        shards,
        mesh=mesh,
        in_specs=(
            P(("groups", "replica"), None, "tensor"),
            P(("groups", "replica"), None, "tensor", None),
            P(("groups", "replica"), None, "tensor", None),
            P(("groups", "replica"), None),
            P(("groups", "replica")),
            P(("groups", "replica"), None),
        ),
        out_specs=P(("groups", "replica"), None, "tensor"),
        check_vma=False,
    )
```

```python
import functools
import math

import jax
import jax.numpy as jnp
from jax import lax
from jax.experimental import pallas as pl
from jax.experimental.pallas import tpu as pltpu
from jax.sharding import PartitionSpec as P

BIG = 1 << 14
STAT = 128
VMEM_LIMIT = 60 << 20


def vspec():
    return pl.BlockSpec(memory_space=pltpu.VMEM)


def sspec():
    return pl.BlockSpec(memory_space=pltpu.SMEM)


def anyspec():
    return pl.BlockSpec(memory_space=pl.ANY)


def shift_of(target, chips):
    here = lax.axis_index("replica") >> 1
    step = (target >> 1) - here
    return jnp.where(step < 0, step + chips, step)


def flow(chips, requests, way, first, rows, size_of, to_of, todo, begin):
    def listing(i, carry):
        count, row = carry
        size = jnp.where(shift_of(to_of(i), chips) == way, size_of(i), 0)
        low = jnp.maximum(row, first)
        high = jnp.minimum(row + size, first + rows)
        todo[count] = i
        begin[count] = row - first
        return count + (high > low).astype(jnp.int32), row + size

    return lax.fori_loop(0, requests, listing, (jnp.int32(0), jnp.int32(0)), unroll=8)[0]


def pack_kernel(
    chips, chunk, requests, len_ref, dst_ref, q_ref, out_ref, tiles, total, hot, todo, begin, sem
):
    way, first, rows = chunk
    many, steps, width = tiles.shape[1:]
    count = flow(
        chips, requests, way, first, rows, lambda i: len_ref[i], lambda i: dst_ref[i], todo, begin
    )
    blocks = (count + many - 1) // many

    def take(j, slot, u):
        i = todo[jnp.minimum(j * many + u, count - 1)]
        return pltpu.make_async_copy(q_ref.at[i], tiles.at[slot, u], sem.at[slot, u])

    def start(j, slot):
        for u in range(many):
            take(j, slot, u).start()

    @pl.when(count > 0)
    def _():
        start(0, 0)

    total[...] = jnp.zeros_like(total)

    def step(j, carry):
        slot = lax.rem(j, 2)

        @pl.when(j + 1 < blocks)
        def _():
            start(j + 1, 1 - slot)

        row = lax.broadcasted_iota(jnp.int32, (rows, many * steps), 0)
        lane = lax.broadcasted_iota(jnp.int32, (1, many * steps), 1)
        place = jnp.full((1, many * steps), -1, jnp.int32)
        for u in range(many):
            n = jnp.minimum(j * many + u, count - 1)
            size = jnp.where(j * many + u < count, len_ref[todo[n]], 0)
            token = lane - u * steps
            place = jnp.where((token >= 0) & (token < size), begin[n] + token, place)
        hot[...] = jnp.where(row == place, 1.0, 0.0).astype(jnp.bfloat16)
        for u in range(many):
            take(j, slot, u).wait()
        block = tiles[slot].reshape(many * steps, width)
        total[...] += jnp.dot(hot[...], block, preferred_element_type=jnp.float32)
        return carry

    lax.fori_loop(0, blocks, step, 0)
    out_ref[...] = total[...].astype(out_ref.dtype)


def pack(queries, lengths, target, chips, chunk):
    requests, steps, width = queries.shape
    rows = chunk[2]
    many = 8
    return pl.pallas_call(
        functools.partial(pack_kernel, chips, chunk, requests),
        in_specs=[sspec(), sspec(), anyspec()],
        out_specs=vspec(),
        out_shape=jax.ShapeDtypeStruct((rows, width), jnp.bfloat16),
        scratch_shapes=[
            pltpu.VMEM((2, many, steps, width), jnp.bfloat16),
            pltpu.VMEM((rows, width), jnp.float32),
            pltpu.VMEM((rows, many * steps), jnp.bfloat16),
            pltpu.SMEM((requests + 1,), jnp.int32),
            pltpu.SMEM((requests + 1,), jnp.int32),
            pltpu.SemaphoreType.DMA((2, many)),
        ],
        compiler_params=pltpu.CompilerParams(vmem_limit_bytes=VMEM_LIMIT),
        cost_estimate=pl.CostEstimate(
            flops=1 << 28, bytes_accessed=rows * width * 4, transcendentals=0
        ),
        name="pack",
    )(lengths, target, queries)


def nt_dot(a, b):
    return lax.dot_general(a, b, (((1,), (1,)), ((), ())), preferred_element_type=jnp.float32)


def with_ones(values):
    return jnp.concatenate([values, jnp.ones_like(values)], axis=1)


def attend(q, dims, window, pool, ids, suffix, s_refs, p_refs, want_sum):
    requests, steps, kv, group, head, pages = dims
    coeff = 1.0 / math.sqrt(head)
    rows = group * window
    nears = []
    for k in range(kv):
        qk = jnp.concatenate(
            [q[:, (k * group + g) * head : (k * group + g + 1) * head] for g in range(group)], axis=0
        )
        if pool is not None:
            per = pool.shape[2]
            count = 4 if pages % 4 == 0 else 1
            for p in range(0, pages, count):
                keys = jnp.concatenate(
                    [pool[ids[n], k, :, 0:head] for n in range(p, p + count)], axis=0
                )
                s_refs[k][0:rows, p * per : (p + count) * per] = nt_dot(qk, keys)
        near = None
        if suffix is not None:
            near = nt_dot(qk, suffix[k, :, 0:head])
            key = lax.broadcasted_iota(jnp.int32, (rows, steps), 1)
            token = lax.rem(lax.broadcasted_iota(jnp.int32, (rows, steps), 0), window)
            near = jnp.where(key <= token, near, -1e30)
        nears.append(near)
    results = []
    for k in range(kv):
        near = nears[k]
        tops = []
        if pool is not None:
            for r in range(0, rows, 16):
                score = s_refs[k][r : r + 16, :]
                top = jnp.max(score, axis=1, keepdims=True)
                if near is not None:
                    top = jnp.maximum(top, jnp.max(near[r : r + 16], axis=1, keepdims=True))
                p_refs[k][r : r + 16, :] = jnp.exp((score - top) * coeff).astype(jnp.bfloat16)
                tops.append(top)
            top = jnp.concatenate(tops, axis=0)
        else:
            top = jnp.max(near, axis=1, keepdims=True)
        mixed = None
        if pool is not None:
            values = jnp.concatenate([pool[n, k, :, head : 2 * head] for n in ids], axis=0)
            mixed = jnp.dot(
                p_refs[k][0:rows, :], with_ones(values), preferred_element_type=jnp.float32
            )
        if near is not None:
            weight = jnp.exp((near - top) * coeff).astype(jnp.bfloat16)
            more = jnp.dot(
                weight,
                with_ones(suffix[k, :, head : 2 * head]),
                preferred_element_type=jnp.float32,
            )
            mixed = more if mixed is None else mixed + more
        total = mixed[:, head : 2 * head]
        lse = top * coeff + jnp.log(total) if want_sum else None
        results.append((mixed[:, 0:head] / total, lse))
    return results


def split_stat(values, group, window):
    lane = lax.broadcasted_iota(jnp.int32, (window, STAT), 1)
    count = len(values) * group
    which = lax.rem(lane, count)
    stat = jnp.zeros((window, STAT), jnp.float32)
    for k, value in enumerate(values):
        for g in range(group):
            stat = jnp.where(which == k * group + g, value[g * window : (g + 1) * window], stat)
    high = stat.astype(jnp.bfloat16).astype(jnp.float32)
    rest = stat - high
    middle = rest.astype(jnp.bfloat16).astype(jnp.float32)
    low = rest - middle
    part = lane // count
    stat = jnp.where(part == 0, high, jnp.where(part == 1, middle, low))
    return jnp.where(part < 3, stat, 0.0)


def load_pools(own_ref, sib_ref, pool, sem):
    count = own_ref.shape[0]
    return (
        pltpu.make_async_copy(own_ref, pool.at[pl.ds(0, count)], sem.at[0]),
        pltpu.make_async_copy(sib_ref, pool.at[pl.ds(count, count)], sem.at[1]),
    )


def own_first(count, is_own, todo, others):
    def move(j, owned):
        own = is_own(todo[j])
        for ref in (todo,) + others:
            here, there = ref[j], ref[owned]
            ref[j] = jnp.where(own, there, here)
            ref[owned] = jnp.where(own, here, there)
        return owned + own.astype(jnp.int32)

    return lax.fori_loop(0, count, move, jnp.int32(0))


def score_scratch(kv, keys, rows):
    return [pltpu.VMEM((rows, keys), jnp.float32) for _ in range(kv)] + [
        pltpu.VMEM((rows, keys), jnp.bfloat16) for _ in range(kv)
    ]


RING = 4


def near_kernel(
    chips, dims, len_ref, dst_ref, q_ref, suf_ref, ctx_ref, stat_ref, q_buf, o_buf, todo, q_sem, o_sem
):
    requests, steps, kv, group, head, pages = dims

    def listing(i, count):
        todo[count] = i
        return count + (shift_of(dst_ref[i], chips) != 0).astype(jnp.int32)

    count = lax.fori_loop(0, requests, listing, jnp.int32(0), unroll=8)

    def take(j):
        slot = lax.rem(j, RING)
        return pltpu.make_async_copy(q_ref.at[todo[j]], q_buf.at[slot], q_sem.at[slot])

    def give(j):
        slot = lax.rem(j, RING)
        return pltpu.make_async_copy(o_buf.at[slot], ctx_ref.at[todo[j]], o_sem.at[slot])

    def ahead(j, carry):
        take(j).start()
        return carry

    lax.fori_loop(0, jnp.minimum(count, RING - 1), ahead, 0)
    stat_ref[...] = jnp.zeros_like(stat_ref)

    def step(j, carry):
        slot = lax.rem(j, RING)

        @pl.when(j + RING - 1 < count)
        def _():
            take(j + RING - 1).start()

        @pl.when(j >= RING)
        def _():
            give(j - RING).wait()

        take(j).wait()
        i = todo[j]
        found = attend(q_buf[slot], dims, steps, None, None, suf_ref.at[i], None, None, True)
        live = lax.broadcasted_iota(jnp.int32, (steps, head), 0) < len_ref[i]
        for k, (mixed, lse) in enumerate(found):
            for g in range(group):
                h = k * group + g
                part = jnp.where(live, mixed[g * steps : (g + 1) * steps], 0.0)
                o_buf[slot, :, h * head : (h + 1) * head] = part.astype(jnp.bfloat16)
        stat_ref[i] = split_stat([f[1] for f in found], group, steps).astype(jnp.bfloat16)
        give(j).start()
        return carry

    lax.fori_loop(0, count, step, 0)

    def drain(j, carry):
        give(j).wait()
        return carry

    lax.fori_loop(jnp.maximum(count - RING, 0), count, drain, 0)


def near_part(queries, suffix, lengths, target, dims, chips):
    requests, steps, width = queries.shape
    return pl.pallas_call(
        functools.partial(near_kernel, chips, dims),
        in_specs=[sspec(), sspec(), anyspec(), vspec()],
        out_specs=[anyspec(), vspec()],
        out_shape=[
            jax.ShapeDtypeStruct(queries.shape, jnp.bfloat16),
            jax.ShapeDtypeStruct((requests, steps, STAT), jnp.bfloat16),
        ],
        scratch_shapes=[
            pltpu.VMEM((RING, steps, width), jnp.bfloat16),
            pltpu.VMEM((RING, steps, width), jnp.bfloat16),
            pltpu.SMEM((requests + 1,), jnp.int32),
            pltpu.SemaphoreType.DMA((RING,)),
            pltpu.SemaphoreType.DMA((RING,)),
        ],
        compiler_params=pltpu.CompilerParams(vmem_limit_bytes=VMEM_LIMIT),
        cost_estimate=pl.CostEstimate(
            flops=1 << 30, bytes_accessed=2 << 20, transcendentals=1 << 10
        ),
        name="near",
    )(lengths, target, queries, suffix)


def local_kernel(
    chips, dims, len_ref, dst_ref, table_ref, q_ref, suf_ref, own_ref, sib_ref, old_ref,
    ctx_ref, pool, q_buf, o_buf, todo, sem, q_sem, o_sem, *scores,
):
    requests, steps, kv, group, head, pages = dims
    core = lax.rem(lax.axis_index("replica"), 2)
    s_refs, p_refs = scores[:kv], scores[kv:]
    held = own_ref.shape[0]
    load_own, load_sib = load_pools(own_ref, sib_ref, pool, sem)
    load_own.start()
    load_sib.start()

    def listing(i, count):
        todo[count] = i
        return count + (shift_of(dst_ref[i], chips) == 0).astype(jnp.int32)

    count = lax.fori_loop(0, requests, listing, jnp.int32(0), unroll=8)
    owned = own_first(count, lambda i: lax.rem(dst_ref[i], 2) == core, todo, ())

    def take(j):
        slot = lax.rem(j, RING)
        return pltpu.make_async_copy(q_ref.at[todo[j]], q_buf.at[slot], q_sem.at[slot])

    def give(j):
        slot = lax.rem(j, RING)
        return pltpu.make_async_copy(o_buf.at[slot], ctx_ref.at[todo[j]], o_sem.at[slot])

    def ahead(j, carry):
        take(j).start()
        return carry

    lax.fori_loop(0, jnp.minimum(count, RING - 1), ahead, 0)

    def compute(i, slot, ids, window):
        found = attend(
            q_buf[slot, 0:window, :], dims, window, pool, ids, suf_ref.at[i], s_refs, p_refs, False
        )
        live = lax.broadcasted_iota(jnp.int32, (window, head), 0) < len_ref[i]
        for k, (mixed, _) in enumerate(found):
            for g in range(group):
                h = k * group + g
                part = jnp.where(live, mixed[g * window : (g + 1) * window], 0.0)
                o_buf[slot, 0:window, h * head : (h + 1) * head] = part.astype(jnp.bfloat16)
        if window < steps:
            o_buf[slot, window:steps, :] = jnp.zeros(
                (steps - window, o_buf.shape[2]), jnp.bfloat16
            )

    load_own.wait()

    @pl.when(owned == count)
    def _():
        load_sib.wait()

    def step(j, carry):
        slot = lax.rem(j, RING)

        @pl.when(j + RING - 1 < count)
        def _():
            take(j + RING - 1).start()

        @pl.when(j >= RING)
        def _():
            give(j - RING).wait()

        @pl.when(j == owned)
        def _():
            load_sib.wait()

        take(j).wait()
        i = todo[j]
        shift = jnp.where(j < owned, 0, held)
        ids = [table_ref[i, p] + shift for p in range(pages)]
        quarter = steps // 4
        need = (len_ref[i] + quarter - 1) // quarter
        for quarters in (1, 2, 3, 4):

            @pl.when(need == quarters)
            def _():
                compute(i, slot, ids, quarter * quarters)

        give(j).start()
        return carry

    lax.fori_loop(0, count, step, 0)

    def drain(j, carry):
        give(j).wait()
        return carry

    lax.fori_loop(jnp.maximum(count - RING, 0), count, drain, 0)


def local(queries, suffix, own, sib, ctx, table, lengths, target, dims, chips):
    requests, steps, kv, group, head, pages = dims
    width = queries.shape[2]
    held = own.shape[0]
    return pl.pallas_call(
        functools.partial(local_kernel, chips, dims),
        in_specs=[sspec(), sspec(), sspec(), anyspec(), vspec()] + [anyspec()] * 3,
        out_specs=anyspec(),
        out_shape=jax.ShapeDtypeStruct(queries.shape, jnp.bfloat16),
        input_output_aliases={7: 0},
        scratch_shapes=[
            pltpu.VMEM((2 * held,) + own.shape[1:], jnp.bfloat16),
            pltpu.VMEM((RING, steps, width), jnp.bfloat16),
            pltpu.VMEM((RING, steps, width), jnp.bfloat16),
            pltpu.SMEM((requests + 1,), jnp.int32),
            pltpu.SemaphoreType.DMA((2,)),
            pltpu.SemaphoreType.DMA((RING,)),
            pltpu.SemaphoreType.DMA((RING,)),
        ]
        + score_scratch(kv, pages * own.shape[2], group * steps),
        compiler_params=pltpu.CompilerParams(vmem_limit_bytes=VMEM_LIMIT),
        cost_estimate=pl.CostEstimate(
            flops=2 << 30, bytes_accessed=8 << 20, transcendentals=1 << 10
        ),
        name="local",
    )(lengths, target, table, queries, suffix, own, sib, ctx)


def far_kernel(
    chips, dims, first, rows, meta_ref, q_ref, own_ref, sib_ref, out_ref, pool, todo, begin, sem,
    *scores,
):
    requests, steps, kv, group, head, pages = dims
    core = lax.rem(lax.axis_index("replica"), 2)
    width = kv * group * head
    s_refs, p_refs = scores[:kv], scores[kv:]
    held = own_ref.shape[0]
    load_own, load_sib = load_pools(own_ref, sib_ref, pool, sem)
    load_own.start()
    load_sib.start()
    count = flow(
        chips, requests, 0, first, rows, lambda i: meta_ref[i, pages],
        lambda i: meta_ref[i, pages + 1], todo, begin,
    )
    owned = own_first(
        count, lambda i: lax.rem(meta_ref[i, pages + 1], 2) == core, todo, (begin,)
    )
    out_ref[...] = jnp.zeros_like(out_ref)

    def compute(low, high, ids, window):
        base = jnp.minimum((low // 16) * 16, rows - window)
        base = pl.multiple_of(base, 16)
        span = pl.ds(base, window)
        found = attend(q_ref[span, :], dims, window, pool, ids, None, s_refs, p_refs, True)
        row = base + lax.broadcasted_iota(jnp.int32, (window, STAT), 0)
        live = (row >= low) & (row < high)
        for k, (mixed, _) in enumerate(found):
            for g in range(group):
                cut = slice((k * group + g) * head, (k * group + g + 1) * head)
                old = out_ref[span, cut].astype(jnp.float32)
                part = jnp.where(live, mixed[g * window : (g + 1) * window], old)
                out_ref[span, cut] = part.astype(jnp.bfloat16)
        old = out_ref[span, width : width + STAT].astype(jnp.float32)
        new = split_stat([f[1] for f in found], group, window)
        out_ref[span, width : width + STAT] = jnp.where(live, new, old).astype(jnp.bfloat16)

    load_own.wait()

    @pl.when(owned == count)
    def _():
        load_sib.wait()

    def step(j, carry):
        @pl.when(j == owned)
        def _():
            load_sib.wait()

        i = todo[j]
        shift = jnp.where(j < owned, 0, held)
        ids = [meta_ref[i, p] + shift for p in range(pages)]
        low = jnp.maximum(begin[j], 0)
        high = jnp.minimum(begin[j] + meta_ref[i, pages], rows)
        need = (high - (low // 16) * 16 + 15) // 16
        for blocks in (1, 2, 3):
            if 16 * blocks <= rows:

                @pl.when(need == blocks)
                def _():
                    compute(low, high, ids, 16 * blocks)

        return carry

    lax.fori_loop(0, count, step, 0)


def far(chunk, meta, own, sib, dims, chips, first):
    rows, width = chunk.shape
    requests, steps, kv, group, head, pages = dims
    held = own.shape[0]
    return pl.pallas_call(
        functools.partial(far_kernel, chips, dims, first, rows),
        in_specs=[sspec(), vspec(), anyspec(), anyspec()],
        out_specs=vspec(),
        out_shape=jax.ShapeDtypeStruct((rows, width + STAT), jnp.bfloat16),
        scratch_shapes=[
            pltpu.VMEM((2 * held,) + own.shape[1:], jnp.bfloat16),
            pltpu.SMEM((requests + 1,), jnp.int32),
            pltpu.SMEM((requests + 1,), jnp.int32),
            pltpu.SemaphoreType.DMA((2,)),
        ]
        + score_scratch(kv, pages * own.shape[2], group * min(48, rows)),
        compiler_params=pltpu.CompilerParams(vmem_limit_bytes=VMEM_LIMIT),
        cost_estimate=pl.CostEstimate(
            flops=2 << 30, bytes_accessed=8 << 20, transcendentals=1 << 10
        ),
        name="far",
    )(meta, chunk, own, sib)


def merge_kernel(
    chips, dims, chunk, len_ref, dst_ref, old_ref, stat_ref, back_ref, ctx_ref, tiles, got, hot,
    todo, begin, take_sem, give_sem,
):
    requests, steps, kv, group, head, pages = dims
    way, first, rows = chunk
    heads = kv * group
    width = heads * head
    many = got.shape[0] // steps
    count = flow(
        chips, requests, way, first, rows, lambda i: len_ref[i], lambda i: dst_ref[i], todo, begin
    )

    def take(j):
        return pltpu.make_async_copy(old_ref.at[todo[j]], tiles.at[j], take_sem.at[j])

    def give(j):
        return pltpu.make_async_copy(tiles.at[j], ctx_ref.at[todo[j]], give_sem.at[j])

    def issue(j, carry):
        take(j).start()
        return carry

    lax.fori_loop(0, count, issue, 0)

    def whole(stat):
        return (
            stat
            + pltpu.roll(stat, STAT - heads, axis=1)
            + pltpu.roll(stat, STAT - 2 * heads, axis=1)
        )

    def one(j, u):
        i = todo[j]
        span = pl.ds(pl.multiple_of(u * steps, steps), steps)
        far_sum = whole(got[span, width : width + STAT])
        near_sum = whole(stat_ref[i].astype(jnp.float32))
        share = 1.0 / (1.0 + jnp.exp(near_sum - far_sum))
        token = lax.broadcasted_iota(jnp.int32, (steps, STAT), 0)
        here = begin[j] + token
        share = jnp.where((token < len_ref[i]) & (here >= 0) & (here < rows), share, 0.0)
        take(j).wait()
        for h in range(heads):
            cut = slice(h * head, (h + 1) * head)
            near = tiles[j, :, cut].astype(jnp.float32)
            mixed = near + share[:, h : h + 1] * (got[span, cut] - near)
            tiles[j, :, cut] = mixed.astype(jnp.bfloat16)
        give(j).start()

    def block(b, carry):
        for u in range(many):
            j = jnp.minimum(b * many + u, count - 1)
            size = jnp.where(b * many + u < count, len_ref[todo[j]], 0)
            token = lax.broadcasted_iota(jnp.int32, (steps, rows), 0)
            row = lax.broadcasted_iota(jnp.int32, (steps, rows), 1)
            match = (begin[j] + token == row) & (token < size)
            hot[u * steps : (u + 1) * steps, :] = jnp.where(match, 1.0, 0.0).astype(jnp.bfloat16)
        got[...] = jnp.dot(hot[...], back_ref[...], preferred_element_type=jnp.float32)

        def each(u, inner):
            one(b * many + u, u)
            return inner

        lax.fori_loop(0, jnp.minimum(count - b * many, many), each, 0)
        return carry

    lax.fori_loop(0, (count + many - 1) // many, block, 0)

    def drain(j, carry):
        give(j).wait()
        return carry

    lax.fori_loop(0, count, drain, 0)


def merge(ctx, stat, back, lengths, target, dims, chips, chunk, room):
    requests, steps, width = ctx.shape
    many = 8
    return pl.pallas_call(
        functools.partial(merge_kernel, chips, dims, chunk),
        in_specs=[sspec(), sspec(), anyspec(), vspec(), vspec()],
        out_specs=anyspec(),
        out_shape=jax.ShapeDtypeStruct(ctx.shape, jnp.bfloat16),
        input_output_aliases={2: 0},
        scratch_shapes=[
            pltpu.VMEM((room, steps, width), jnp.bfloat16),
            pltpu.VMEM((many * steps, width + STAT), jnp.float32),
            pltpu.VMEM((many * steps, chunk[2]), jnp.bfloat16),
            pltpu.SMEM((requests + 1,), jnp.int32),
            pltpu.SMEM((requests + 1,), jnp.int32),
            pltpu.SemaphoreType.DMA((room,)),
            pltpu.SemaphoreType.DMA((room,)),
        ],
        compiler_params=pltpu.CompilerParams(vmem_limit_bytes=VMEM_LIMIT),
        cost_estimate=pl.CostEstimate(
            flops=1 << 29, bytes_accessed=chunk[2] * (8 << 10), transcendentals=0
        ),
        name="merge",
    )(lengths, target, ctx, stat, back)


def shards(queries, suffix_key_value, kv_pool, page_table, lengths, destination):
    replicas = lax.axis_size("replica")
    chips = replicas // 2
    requests, steps, width = queries.shape
    kv, head = suffix_key_value.shape[2], suffix_key_value.shape[3] // 2
    pages = page_table.shape[1]
    dims = (requests, steps, kv, width // (kv * head), head, pages)
    target = destination[:, 0]
    here = lax.axis_index("replica") >> 1
    ways = range(1, chips)

    room = 2 * (requests // replicas + 1)
    most = room * steps
    mean = requests * steps // (2 * chips)
    base = min(most, -(-(mean * 3) // (4 * 32)) * 32)
    sizes = [most - base]
    if chips == 2:
        sizes = []
        for eighths in (9, 10, 11, 13):
            size = -(-(mean * eighths) // (8 * 32)) * 32 - base
            if 0 < size < most - base and size not in sizes:
                sizes.append(size)
        sizes.append(most - base)

    def away(s):
        return [(r, (r + 2 * s) % replicas) for r in range(replicas)]

    def back(s):
        return [((r + 2 * s) % replicas, r) for r in range(replicas)]

    meta = jnp.concatenate([page_table, lengths[:, None], destination], axis=1)
    metas = {s: lax.ppermute(meta, "replica", away(s)) for s in ways}
    packed = [pack(queries, lengths, target, chips, (s, 0, base)) for s in ways]
    arrived = [lax.ppermute(rows, "replica", away(s)) for s, rows in zip(ways, packed)]
    kv_pool, packed = lax.optimization_barrier((kv_pool, packed))

    own = jnp.transpose(kv_pool, (0, 2, 1, 3))
    sib = lax.ppermute(own, "replica", [(r, r ^ 1) for r in range(replicas)])
    suffix = jnp.transpose(suffix_key_value, (0, 2, 1, 3))

    def serve(rows, s, first):
        return far(rows, metas[s], own, sib, dims, chips, first)

    def finish(size):
        def run():
            chunks = [(s, 0, base) for s in ways] + [(s, base, size) for s in ways]
            more = [pack(queries, lengths, target, chips, c) for c in chunks[chips - 1 :]]
            more = [lax.ppermute(r, "replica", away(s)) for s, r in zip(ways, more)]
            first = [serve(r, s, 0) for s, r in zip(ways, arrived)]
            came = [lax.ppermute(r, "replica", back(s)) for s, r in zip(ways, first)]
            near_queries, first = lax.optimization_barrier((queries, first))
            ctx, stat = near_part(near_queries, suffix, lengths, target, dims, chips)
            stat, more = lax.optimization_barrier((stat, more))
            second = [serve(r, s, base) for s, r in zip(ways, more)]
            came += [lax.ppermute(r, "replica", back(s)) for s, r in zip(ways, second)]
            ctx, second = lax.optimization_barrier((ctx, second))
            ctx = local(queries, suffix, own, sib, ctx, page_table, lengths, target, dims, chips)
            for rows, chunk in zip(came, chunks):
                ctx = merge(ctx, stat, rows, lengths, target, dims, chips, chunk, room)
            return ctx

        return run

    if len(sizes) == 1:
        return finish(sizes[0])()

    widest = jnp.zeros((), jnp.int32)
    for s, table in [(0, meta)] + [(s, metas[s]) for s in ways]:
        sender = lax.rem(here - s + chips, chips)
        for chip in range(chips):
            goes = ((table[:, pages + 1] >> 1) == chip) & (sender != chip)
            widest = jnp.maximum(widest, jnp.sum(jnp.where(goes, table[:, pages], 0)))
    widest = widest.reshape(1)
    widest = jnp.maximum(
        widest, lax.ppermute(widest, "replica", [(r, r ^ 1) for r in range(replicas)])
    )
    seen = widest
    parts = lax.axis_size("groups")
    for hop in range(1, parts):
        other = lax.ppermute(seen, "groups", [(g, (g + hop) % parts) for g in range(parts)])
        widest = jnp.maximum(widest, other)
    level = sum((widest[0] > base + size).astype(jnp.int32) for size in sizes[:-1])
    return lax.switch(level, [finish(size) for size in sizes])


def solution(mesh):
    return jax.shard_map(
        shards,
        mesh=mesh,
        in_specs=(
            P(("groups", "replica"), None, "tensor"),
            P(("groups", "replica"), None, "tensor", None),
            P(("groups", "replica"), None, "tensor", None),
            P(("groups", "replica"), None),
            P(("groups", "replica")),
            P(("groups", "replica"), None),
        ),
        out_specs=P(("groups", "replica"), None, "tensor"),
        check_vma=False,
    )
```

```python
import functools
import math

import jax
import jax.numpy as jnp
from jax import lax
from jax.experimental import pallas as pl
from jax.experimental.pallas import tpu as pltpu
from jax.sharding import PartitionSpec as P

BIG = 1 << 14
STAT = 128
VMEM_LIMIT = 60 << 20


def vspec():
    return pl.BlockSpec(memory_space=pltpu.VMEM)


def sspec():
    return pl.BlockSpec(memory_space=pltpu.SMEM)


def anyspec():
    return pl.BlockSpec(memory_space=pl.ANY)


def shift_of(target, chips):
    here = lax.axis_index("replica") >> 1
    step = (target >> 1) - here
    return jnp.where(step < 0, step + chips, step)


def flow(chips, requests, way, first, rows, size_of, to_of, todo, begin):
    def listing(i, carry):
        count, row = carry
        size = jnp.where(shift_of(to_of(i), chips) == way, size_of(i), 0)
        low = jnp.maximum(row, first)
        high = jnp.minimum(row + size, first + rows)
        todo[count] = i
        begin[count] = row - first
        return count + (high > low).astype(jnp.int32), row + size

    return lax.fori_loop(0, requests, listing, (jnp.int32(0), jnp.int32(0)), unroll=8)[0]


def pack_kernel(
    chips, chunk, requests, len_ref, dst_ref, q_ref, out_ref, tiles, hot, todo, begin, sem
):
    way, first, rows = chunk
    many, steps, width = tiles.shape[1:]
    count = flow(
        chips, requests, way, first, rows, lambda i: len_ref[i], lambda i: dst_ref[i], todo, begin
    )
    blocks = (count + many - 1) // many

    def take(j, slot, u):
        i = todo[jnp.minimum(j * many + u, count - 1)]
        return pltpu.make_async_copy(q_ref.at[i], tiles.at[slot, u], sem.at[slot, u])

    def start(j, slot):
        for u in range(many):
            take(j, slot, u).start()

    @pl.when(count > 0)
    def _():
        start(0, 0)

    @pl.when(count == 0)
    def _():
        out_ref[...] = jnp.zeros_like(out_ref)

    def step(j, carry):
        slot = lax.rem(j, 2)

        @pl.when(j + 1 < blocks)
        def _():
            start(j + 1, 1 - slot)

        row = lax.broadcasted_iota(jnp.int32, (rows, many * steps), 0)
        lane = lax.broadcasted_iota(jnp.int32, (1, many * steps), 1)
        place = jnp.full((1, many * steps), -1, jnp.int32)
        for u in range(many):
            n = jnp.minimum(j * many + u, count - 1)
            size = jnp.where(j * many + u < count, len_ref[todo[n]], 0)
            token = lane - u * steps
            place = jnp.where((token >= 0) & (token < size), begin[n] + token, place)
        hot[...] = jnp.where(row == place, 1.0, 0.0).astype(jnp.bfloat16)
        for u in range(many):
            take(j, slot, u).wait()
        block = tiles[slot].reshape(many * steps, width)
        rows_of = jnp.dot(hot[...], block, preferred_element_type=jnp.float32).astype(jnp.bfloat16)

        @pl.when(j == 0)
        def _():
            out_ref[...] = rows_of

        @pl.when(j > 0)
        def _():
            out_ref[...] += rows_of

        return carry

    lax.fori_loop(0, blocks, step, 0)


def pack(queries, lengths, target, chips, chunk):
    requests, steps, width = queries.shape
    rows = chunk[2]
    many = 16
    return pl.pallas_call(
        functools.partial(pack_kernel, chips, chunk, requests),
        in_specs=[sspec(), sspec(), anyspec()],
        out_specs=vspec(),
        out_shape=jax.ShapeDtypeStruct((rows, width), jnp.bfloat16),
        scratch_shapes=[
            pltpu.VMEM((2, many, steps, width), jnp.bfloat16),
            pltpu.VMEM((rows, many * steps), jnp.bfloat16),
            pltpu.SMEM((requests + 1,), jnp.int32),
            pltpu.SMEM((requests + 1,), jnp.int32),
            pltpu.SemaphoreType.DMA((2, many)),
        ],
        compiler_params=pltpu.CompilerParams(vmem_limit_bytes=VMEM_LIMIT),
        cost_estimate=pl.CostEstimate(
            flops=1 << 28, bytes_accessed=rows * width * 4, transcendentals=0
        ),
        name="pack",
    )(lengths, target, queries)


def nt_dot(a, b):
    return lax.dot_general(a, b, (((1,), (1,)), ((), ())), preferred_element_type=jnp.float32)


def with_ones(values):
    return jnp.concatenate([values, jnp.ones_like(values)], axis=1)


def attend(q, dims, window, pool, ids, suffix, s_refs, p_refs, want_sum):
    requests, steps, kv, group, head, pages = dims
    coeff = 1.0 / math.sqrt(head)
    rows = group * window
    nears = []
    if suffix is not None:
        key = lax.broadcasted_iota(jnp.int32, (window, steps), 1)
        token = lax.broadcasted_iota(jnp.int32, (window, steps), 0)
        causal = jnp.where(key <= token, 0.0, -1e30)
        causal = jnp.concatenate([causal] * group, axis=0)
    for k in range(kv):
        qk = jnp.concatenate(
            [q[:, (k * group + g) * head : (k * group + g + 1) * head] for g in range(group)], axis=0
        )
        if pool is not None:
            per = pool.shape[2]
            count = 4 if pages % 4 == 0 else 1
            for p in range(0, pages, count):
                keys = jnp.concatenate(
                    [pool[ids[n], k, :, 0:head] for n in range(p, p + count)], axis=0
                )
                s_refs[k][0:rows, p * per : (p + count) * per] = nt_dot(qk, keys)
        near = None
        if suffix is not None:
            near = nt_dot(qk, suffix[k, :, 0:head])
            near = near + causal
        nears.append(near)
    results = []
    for k in range(kv):
        near = nears[k]
        tops = []
        if pool is not None:
            for r in range(0, rows, 16):
                score = s_refs[k][r : r + 16, :]
                top = jnp.max(score, axis=1, keepdims=True)
                if near is not None:
                    top = jnp.maximum(top, jnp.max(near[r : r + 16], axis=1, keepdims=True))
                p_refs[k][r : r + 16, :] = jnp.exp((score - top) * coeff).astype(jnp.bfloat16)
                tops.append(top)
            top = jnp.concatenate(tops, axis=0)
        else:
            top = jnp.max(near, axis=1, keepdims=True)
        mixed = None
        if pool is not None:
            values = jnp.concatenate([pool[n, k, :, head : 2 * head] for n in ids], axis=0)
            mixed = jnp.dot(
                p_refs[k][0:rows, :], with_ones(values), preferred_element_type=jnp.float32
            )
        if near is not None:
            weight = jnp.exp((near - top) * coeff).astype(jnp.bfloat16)
            more = jnp.dot(
                weight,
                with_ones(suffix[k, :, head : 2 * head]),
                preferred_element_type=jnp.float32,
            )
            mixed = more if mixed is None else mixed + more
        total = mixed[:, head : 2 * head]
        share = pl.reciprocal(total, approx=True)
        share = share * (2.0 - total * share)
        results.append((mixed[:, 0:head] * share, (top * coeff, total) if want_sum else None))
    return results


def split_stat(values, group, window):
    lane = lax.broadcasted_iota(jnp.int32, (window, STAT), 1)
    count = len(values) * group
    assert count & (count - 1) == 0
    which = lane & (count - 1)
    level = jnp.zeros((window, STAT), jnp.float32)
    total = jnp.ones((window, STAT), jnp.float32)
    for k, (top, weight) in enumerate(values):
        for g in range(group):
            here = which == k * group + g
            level = jnp.where(here, top[g * window : (g + 1) * window], level)
            total = jnp.where(here, weight[g * window : (g + 1) * window, 0:STAT], total)
    stat = level + jnp.log(total)
    high = stat.astype(jnp.bfloat16).astype(jnp.float32)
    rest = stat - high
    middle = rest.astype(jnp.bfloat16).astype(jnp.float32)
    low = rest - middle
    stat = jnp.where(lane < count, high, jnp.where(lane < 2 * count, middle, low))
    return jnp.where(lane < 3 * count, stat, 0.0)


def load_pools(own_ref, sib_ref, pool, sem):
    count = own_ref.shape[0]
    return (
        pltpu.make_async_copy(own_ref, pool.at[pl.ds(0, count)], sem.at[0]),
        pltpu.make_async_copy(sib_ref, pool.at[pl.ds(count, count)], sem.at[1]),
    )


def own_first(count, is_own, todo, others):
    def move(j, owned):
        own = is_own(todo[j])
        for ref in (todo,) + others:
            here, there = ref[j], ref[owned]
            ref[j] = jnp.where(own, there, here)
            ref[owned] = jnp.where(own, here, there)
        return owned + own.astype(jnp.int32)

    return lax.fori_loop(0, count, move, jnp.int32(0))


def score_scratch(kv, keys, rows):
    return [pltpu.VMEM((rows, keys), jnp.float32) for _ in range(kv)] + [
        pltpu.VMEM((rows, keys), jnp.bfloat16) for _ in range(kv)
    ]


RING = 4


def near_kernel(
    chips, dims, len_ref, dst_ref, q_ref, suf_ref, ctx_ref, stat_ref, q_buf, o_buf, todo, q_sem, o_sem
):
    requests, steps, kv, group, head, pages = dims

    def listing(i, count):
        todo[count] = i
        return count + (shift_of(dst_ref[i], chips) != 0).astype(jnp.int32)

    count = lax.fori_loop(0, requests, listing, jnp.int32(0), unroll=8)

    def take(j):
        slot = lax.rem(j, RING)
        return pltpu.make_async_copy(q_ref.at[todo[j]], q_buf.at[slot], q_sem.at[slot])

    def give(j):
        slot = lax.rem(j, RING)
        return pltpu.make_async_copy(o_buf.at[slot], ctx_ref.at[todo[j]], o_sem.at[slot])

    def ahead(j, carry):
        take(j).start()
        return carry

    lax.fori_loop(0, jnp.minimum(count, RING - 1), ahead, 0)
    stat_ref[...] = jnp.zeros_like(stat_ref)

    def step(j, carry):
        slot = lax.rem(j, RING)

        @pl.when(j + RING - 1 < count)
        def _():
            take(j + RING - 1).start()

        @pl.when(j >= RING)
        def _():
            give(j - RING).wait()

        take(j).wait()
        i = todo[j]
        found = attend(q_buf[slot], dims, steps, None, None, suf_ref.at[i], None, None, True)
        live = lax.broadcasted_iota(jnp.int32, (steps, head), 0) < len_ref[i]
        for k, (mixed, lse) in enumerate(found):
            for g in range(group):
                h = k * group + g
                part = jnp.where(live, mixed[g * steps : (g + 1) * steps], 0.0)
                o_buf[slot, :, h * head : (h + 1) * head] = part.astype(jnp.bfloat16)
        stat_ref[i] = split_stat([f[1] for f in found], group, steps).astype(jnp.bfloat16)
        give(j).start()
        return carry

    lax.fori_loop(0, count, step, 0)

    def drain(j, carry):
        give(j).wait()
        return carry

    lax.fori_loop(jnp.maximum(count - RING, 0), count, drain, 0)


def near_part(queries, suffix, lengths, target, dims, chips):
    requests, steps, width = queries.shape
    return pl.pallas_call(
        functools.partial(near_kernel, chips, dims),
        in_specs=[sspec(), sspec(), anyspec(), vspec()],
        out_specs=[anyspec(), vspec()],
        out_shape=[
            jax.ShapeDtypeStruct(queries.shape, jnp.bfloat16),
            jax.ShapeDtypeStruct((requests, steps, STAT), jnp.bfloat16),
        ],
        scratch_shapes=[
            pltpu.VMEM((RING, steps, width), jnp.bfloat16),
            pltpu.VMEM((RING, steps, width), jnp.bfloat16),
            pltpu.SMEM((requests + 1,), jnp.int32),
            pltpu.SemaphoreType.DMA((RING,)),
            pltpu.SemaphoreType.DMA((RING,)),
        ],
        compiler_params=pltpu.CompilerParams(vmem_limit_bytes=VMEM_LIMIT),
        cost_estimate=pl.CostEstimate(
            flops=1 << 30, bytes_accessed=2 << 20, transcendentals=1 << 10
        ),
        name="near",
    )(lengths, target, queries, suffix)


def local_kernel(
    chips, dims, len_ref, dst_ref, table_ref, q_ref, suf_ref, own_ref, sib_ref, old_ref,
    ctx_ref, pool, q_buf, o_buf, todo, sem, q_sem, o_sem, *scores,
):
    requests, steps, kv, group, head, pages = dims
    core = lax.rem(lax.axis_index("replica"), 2)
    s_refs, p_refs = scores[:kv], scores[kv:]
    held = own_ref.shape[0]
    load_own, load_sib = load_pools(own_ref, sib_ref, pool, sem)
    load_own.start()
    load_sib.start()

    def listing(i, count):
        todo[count] = i
        return count + (shift_of(dst_ref[i], chips) == 0).astype(jnp.int32)

    count = lax.fori_loop(0, requests, listing, jnp.int32(0), unroll=8)
    owned = own_first(count, lambda i: lax.rem(dst_ref[i], 2) == core, todo, ())

    def take(j):
        slot = lax.rem(j, RING)
        return pltpu.make_async_copy(q_ref.at[todo[j]], q_buf.at[slot], q_sem.at[slot])

    def give(j):
        slot = lax.rem(j, RING)
        return pltpu.make_async_copy(o_buf.at[slot], ctx_ref.at[todo[j]], o_sem.at[slot])

    def ahead(j, carry):
        take(j).start()
        return carry

    lax.fori_loop(0, jnp.minimum(count, RING - 1), ahead, 0)

    def compute(i, slot, ids, window):
        found = attend(
            q_buf[slot, 0:window, :], dims, window, pool, ids, suf_ref.at[i], s_refs, p_refs, False
        )
        live = lax.broadcasted_iota(jnp.int32, (window, head), 0) < len_ref[i]
        for k, (mixed, _) in enumerate(found):
            for g in range(group):
                h = k * group + g
                part = jnp.where(live, mixed[g * window : (g + 1) * window], 0.0)
                o_buf[slot, 0:window, h * head : (h + 1) * head] = part.astype(jnp.bfloat16)
        if window < steps:
            o_buf[slot, window:steps, :] = jnp.zeros(
                (steps - window, o_buf.shape[2]), jnp.bfloat16
            )

    load_own.wait()

    @pl.when(owned == count)
    def _():
        load_sib.wait()

    def step(j, carry):
        slot = lax.rem(j, RING)

        @pl.when(j + RING - 1 < count)
        def _():
            take(j + RING - 1).start()

        @pl.when(j >= RING)
        def _():
            give(j - RING).wait()

        @pl.when(j == owned)
        def _():
            load_sib.wait()

        take(j).wait()
        i = todo[j]
        shift = jnp.where(j < owned, 0, held)
        ids = [table_ref[i, p] + shift for p in range(pages)]
        quarter = steps // 4
        need = (len_ref[i] + quarter - 1) // quarter
        for quarters in (1, 2, 3, 4):

            @pl.when(need == quarters)
            def _():
                compute(i, slot, ids, quarter * quarters)

        give(j).start()
        return carry

    lax.fori_loop(0, count, step, 0)

    def drain(j, carry):
        give(j).wait()
        return carry

    lax.fori_loop(jnp.maximum(count - RING, 0), count, drain, 0)


def local(queries, suffix, own, sib, ctx, table, lengths, target, dims, chips):
    requests, steps, kv, group, head, pages = dims
    width = queries.shape[2]
    held = own.shape[0]
    return pl.pallas_call(
        functools.partial(local_kernel, chips, dims),
        in_specs=[sspec(), sspec(), sspec(), anyspec(), vspec()] + [anyspec()] * 3,
        out_specs=anyspec(),
        out_shape=jax.ShapeDtypeStruct(queries.shape, jnp.bfloat16),
        input_output_aliases={7: 0},
        scratch_shapes=[
            pltpu.VMEM((2 * held,) + own.shape[1:], jnp.bfloat16),
            pltpu.VMEM((RING, steps, width), jnp.bfloat16),
            pltpu.VMEM((RING, steps, width), jnp.bfloat16),
            pltpu.SMEM((requests + 1,), jnp.int32),
            pltpu.SemaphoreType.DMA((2,)),
            pltpu.SemaphoreType.DMA((RING,)),
            pltpu.SemaphoreType.DMA((RING,)),
        ]
        + score_scratch(kv, pages * own.shape[2], group * steps),
        compiler_params=pltpu.CompilerParams(vmem_limit_bytes=VMEM_LIMIT),
        cost_estimate=pl.CostEstimate(
            flops=2 << 30, bytes_accessed=8 << 20, transcendentals=1 << 10
        ),
        name="local",
    )(lengths, target, table, queries, suffix, own, sib, ctx)


def far_kernel(
    chips, dims, first, rows, meta_ref, q_ref, own_ref, sib_ref, out_ref, pool, todo, begin, sem,
    *scores,
):
    requests, steps, kv, group, head, pages = dims
    core = lax.rem(lax.axis_index("replica"), 2)
    width = kv * group * head
    s_refs, p_refs = scores[:kv], scores[kv:]
    held = own_ref.shape[0]
    load_own, load_sib = load_pools(own_ref, sib_ref, pool, sem)
    load_own.start()
    load_sib.start()
    count = flow(
        chips, requests, 0, first, rows, lambda i: meta_ref[i, pages],
        lambda i: meta_ref[i, pages + 1], todo, begin,
    )
    owned = own_first(
        count, lambda i: lax.rem(meta_ref[i, pages + 1], 2) == core, todo, (begin,)
    )
    out_ref[...] = jnp.zeros_like(out_ref)

    def compute(low, high, ids, window):
        base = jnp.minimum((low // 16) * 16, rows - window)
        base = pl.multiple_of(base, 16)
        span = pl.ds(base, window)
        found = attend(q_ref[span, :], dims, window, pool, ids, None, s_refs, p_refs, True)
        row = base + lax.broadcasted_iota(jnp.int32, (window, STAT), 0)
        live = (row >= low) & (row < high)
        for k, (mixed, _) in enumerate(found):
            for g in range(group):
                cut = slice((k * group + g) * head, (k * group + g + 1) * head)
                old = out_ref[span, cut].astype(jnp.float32)
                part = jnp.where(live, mixed[g * window : (g + 1) * window], old)
                out_ref[span, cut] = part.astype(jnp.bfloat16)
        old = out_ref[span, width : width + STAT].astype(jnp.float32)
        new = split_stat([f[1] for f in found], group, window)
        out_ref[span, width : width + STAT] = jnp.where(live, new, old).astype(jnp.bfloat16)

    load_own.wait()

    @pl.when(owned == count)
    def _():
        load_sib.wait()

    def step(j, carry):
        @pl.when(j == owned)
        def _():
            load_sib.wait()

        i = todo[j]
        shift = jnp.where(j < owned, 0, held)
        ids = [meta_ref[i, p] + shift for p in range(pages)]
        low = jnp.maximum(begin[j], 0)
        high = jnp.minimum(begin[j] + meta_ref[i, pages], rows)
        need = (high - (low // 16) * 16 + 15) // 16
        for blocks in (1, 2, 3):
            if 16 * blocks <= rows:

                @pl.when(need == blocks)
                def _():
                    compute(low, high, ids, 16 * blocks)

        return carry

    lax.fori_loop(0, count, step, 0)


def far(chunk, meta, own, sib, dims, chips, first):
    rows, width = chunk.shape
    requests, steps, kv, group, head, pages = dims
    held = own.shape[0]
    return pl.pallas_call(
        functools.partial(far_kernel, chips, dims, first, rows),
        in_specs=[sspec(), vspec(), anyspec(), anyspec()],
        out_specs=vspec(),
        out_shape=jax.ShapeDtypeStruct((rows, width + STAT), jnp.bfloat16),
        scratch_shapes=[
            pltpu.VMEM((2 * held,) + own.shape[1:], jnp.bfloat16),
            pltpu.SMEM((requests + 1,), jnp.int32),
            pltpu.SMEM((requests + 1,), jnp.int32),
            pltpu.SemaphoreType.DMA((2,)),
        ]
        + score_scratch(kv, pages * own.shape[2], group * min(48, rows)),
        compiler_params=pltpu.CompilerParams(vmem_limit_bytes=VMEM_LIMIT),
        cost_estimate=pl.CostEstimate(
            flops=2 << 30, bytes_accessed=8 << 20, transcendentals=1 << 10
        ),
        name="far",
    )(meta, chunk, own, sib)


def merge_kernel(
    chips, dims, chunk, len_ref, dst_ref, old_ref, stat_ref, back_hbm, ctx_ref, back_ref, tiles, got,
    hot, todo, begin, take_sem, give_sem, back_sem,
):
    requests, steps, kv, group, head, pages = dims
    way, first, rows = chunk
    heads = kv * group
    width = heads * head
    many = got.shape[0] // steps
    back = pltpu.make_async_copy(back_hbm, back_ref, back_sem)
    back.start()
    count = flow(
        chips, requests, way, first, rows, lambda i: len_ref[i], lambda i: dst_ref[i], todo, begin
    )

    def take(j):
        return pltpu.make_async_copy(old_ref.at[todo[j]], tiles.at[j], take_sem.at[j])

    def give(j):
        return pltpu.make_async_copy(tiles.at[j], ctx_ref.at[todo[j]], give_sem.at[j])

    def issue(j, carry):
        take(j).start()
        return carry

    lax.fori_loop(0, count, issue, 0)
    back.wait()

    def whole(stat):
        return (
            stat
            + pltpu.roll(stat, STAT - heads, axis=1)
            + pltpu.roll(stat, STAT - 2 * heads, axis=1)
        )

    def one(j, u):
        i = todo[j]
        span = pl.ds(pl.multiple_of(u * steps, steps), steps)
        far_sum = whole(got[span, width : width + STAT])
        near_sum = whole(stat_ref[i].astype(jnp.float32))
        share = 1.0 / (1.0 + jnp.exp(near_sum - far_sum))
        token = lax.broadcasted_iota(jnp.int32, (steps, STAT), 0)
        here = begin[j] + token
        share = jnp.where((token < len_ref[i]) & (here >= 0) & (here < rows), share, 0.0)
        take(j).wait()
        for h in range(heads):
            cut = slice(h * head, (h + 1) * head)
            near = tiles[j, :, cut].astype(jnp.float32)
            mixed = near + share[:, h : h + 1] * (got[span, cut] - near)
            tiles[j, :, cut] = mixed.astype(jnp.bfloat16)
        give(j).start()

    def block(b, carry):
        for u in range(many):
            j = jnp.minimum(b * many + u, count - 1)
            size = jnp.where(b * many + u < count, len_ref[todo[j]], 0)
            token = lax.broadcasted_iota(jnp.int32, (steps, rows), 0)
            row = lax.broadcasted_iota(jnp.int32, (steps, rows), 1)
            match = (begin[j] + token == row) & (token < size)
            hot[u * steps : (u + 1) * steps, :] = jnp.where(match, 1.0, 0.0).astype(jnp.bfloat16)
        got[...] = jnp.dot(hot[...], back_ref[...], preferred_element_type=jnp.float32)

        def each(u, inner):
            one(b * many + u, u)
            return inner

        lax.fori_loop(0, jnp.minimum(count - b * many, many), each, 0)
        return carry

    lax.fori_loop(0, (count + many - 1) // many, block, 0)

    def drain(j, carry):
        give(j).wait()
        return carry

    lax.fori_loop(0, count, drain, 0)


def merge(ctx, stat, back, lengths, target, dims, chips, chunk, room):
    requests, steps, width = ctx.shape
    many = 8
    return pl.pallas_call(
        functools.partial(merge_kernel, chips, dims, chunk),
        in_specs=[sspec(), sspec(), anyspec(), vspec(), anyspec()],
        out_specs=anyspec(),
        out_shape=jax.ShapeDtypeStruct(ctx.shape, jnp.bfloat16),
        input_output_aliases={2: 0},
        scratch_shapes=[
            pltpu.VMEM(back.shape, jnp.bfloat16),
            pltpu.VMEM((room, steps, width), jnp.bfloat16),
            pltpu.VMEM((many * steps, width + STAT), jnp.float32),
            pltpu.VMEM((many * steps, chunk[2]), jnp.bfloat16),
            pltpu.SMEM((requests + 1,), jnp.int32),
            pltpu.SMEM((requests + 1,), jnp.int32),
            pltpu.SemaphoreType.DMA((room,)),
            pltpu.SemaphoreType.DMA((room,)),
            pltpu.SemaphoreType.DMA,
        ],
        compiler_params=pltpu.CompilerParams(vmem_limit_bytes=VMEM_LIMIT),
        cost_estimate=pl.CostEstimate(
            flops=1 << 29, bytes_accessed=chunk[2] * (8 << 10), transcendentals=0
        ),
        name="merge",
    )(lengths, target, ctx, stat, back)


def shards(queries, suffix_key_value, kv_pool, page_table, lengths, destination):
    replicas = lax.axis_size("replica")
    chips = replicas // 2
    requests, steps, width = queries.shape
    kv, head = suffix_key_value.shape[2], suffix_key_value.shape[3] // 2
    pages = page_table.shape[1]
    dims = (requests, steps, kv, width // (kv * head), head, pages)
    target = destination[:, 0]
    here = lax.axis_index("replica") >> 1
    ways = range(1, chips)

    room = 2 * (requests // replicas + 1)
    most = room * steps
    mean = requests * steps // (2 * chips)
    base = min(most, -(-(mean * 3) // (4 * 32)) * 32)
    usual = min(most, -(-(mean * 11) // (8 * 32)) * 32)

    def away(s):
        return [(r, (r + 2 * s) % replicas) for r in range(replicas)]

    def back(s):
        return [((r + 2 * s) % replicas, r) for r in range(replicas)]

    def send(s, first, rows, after=None):
        where, _ = lax.optimization_barrier((target, after))
        packed = pack(queries, lengths, where, chips, (s, first, rows))
        return packed, lax.ppermute(packed, "replica", away(s))

    def serve(rows, s, first):
        out = far(rows, metas[s], own, sib, dims, chips, first)
        return out, lax.ppermute(out, "replica", back(s))

    meta = jnp.concatenate([page_table, lengths[:, None], destination], axis=1)
    metas = {s: lax.ppermute(meta, "replica", away(s)) for s in ways}
    packed, arrived = zip(*[send(s, 0, base) for s in ways])
    pool, packed = lax.optimization_barrier((kv_pool, packed))
    own = jnp.transpose(pool, (0, 2, 1, 3))
    sib = lax.ppermute(own, "replica", [(r, r ^ 1) for r in range(replicas)])
    suffix = jnp.transpose(suffix_key_value, (0, 2, 1, 3))
    packed, more = zip(*[send(s, base, usual - base, packed) for s in ways])
    near_target, packed = lax.optimization_barrier((target, packed))
    ctx, stat = near_part(queries, suffix, lengths, near_target, dims, chips)
    stat, arrived = lax.optimization_barrier((stat, arrived))
    first, came_first = zip(*[serve(r, s, 0) for s, r in zip(ways, arrived)])
    more, first = lax.optimization_barrier((more, first))
    second, came_second = zip(*[serve(r, s, base) for s, r in zip(ways, more)])
    ctx, second = lax.optimization_barrier((ctx, second))
    ctx = local(queries, suffix, own, sib, ctx, page_table, lengths, target, dims, chips)
    for s, rows in zip(ways, came_first):
        ctx = merge(ctx, stat, rows, lengths, target, dims, chips, (s, 0, base), room)
    for s, rows in zip(ways, came_second):
        ctx = merge(ctx, stat, rows, lengths, target, dims, chips, (s, base, usual - base), room)
    if usual == most:
        return ctx

    widest = jnp.zeros((), jnp.int32)
    for s, table in [(0, meta)] + [(s, metas[s]) for s in ways]:
        sender = lax.rem(here - s + chips, chips)
        for chip in range(chips):
            goes = ((table[:, pages + 1] >> 1) == chip) & (sender != chip)
            widest = jnp.maximum(widest, jnp.sum(jnp.where(goes, table[:, pages], 0)))
    widest = widest.reshape(1)
    widest = jnp.maximum(
        widest, lax.ppermute(widest, "replica", [(r, r ^ 1) for r in range(replicas)])
    )
    seen = widest
    parts = lax.axis_size("groups")
    for hop in range(1, parts):
        other = lax.ppermute(seen, "groups", [(g, (g + hop) % parts) for g in range(parts)])
        widest = jnp.maximum(widest, other)

    def rest():
        done = ctx
        for s in ways:
            _, rows = send(s, usual, most - usual)
            _, rows = serve(rows, s, usual)
            chunk = (s, usual, most - usual)
            done = merge(done, stat, rows, lengths, target, dims, chips, chunk, room)
        return done

    return lax.cond(widest[0] > usual, rest, lambda: ctx)


def solution(mesh):
    return jax.shard_map(
        shards,
        mesh=mesh,
        in_specs=(
            P(("groups", "replica"), None, "tensor"),
            P(("groups", "replica"), None, "tensor", None),
            P(("groups", "replica"), None, "tensor", None),
            P(("groups", "replica"), None),
            P(("groups", "replica")),
            P(("groups", "replica"), None),
        ),
        out_specs=P(("groups", "replica"), None, "tensor"),
        check_vma=False,
    )
```

```python
import functools
import math

import jax
import jax.numpy as jnp
from jax import lax
from jax.experimental import pallas as pl
from jax.experimental.pallas import tpu as pltpu
from jax.sharding import PartitionSpec as P

BIG = 1 << 14
STAT = 128
VMEM_LIMIT = 60 << 20


def cost(microseconds):
    return pl.CostEstimate(
        flops=int(microseconds * 1.1e9), bytes_accessed=1 << 10, transcendentals=0
    )


def vspec():
    return pl.BlockSpec(memory_space=pltpu.VMEM)


def sspec():
    return pl.BlockSpec(memory_space=pltpu.SMEM)


def anyspec():
    return pl.BlockSpec(memory_space=pl.ANY)


def shift_of(target, chips):
    here = lax.axis_index("replica") >> 1
    step = (target >> 1) - here
    return jnp.where(step < 0, step + chips, step)


def flow(chips, requests, way, first, rows, size_of, to_of, todo, begin):
    def listing(i, carry):
        count, row = carry
        size = jnp.where(shift_of(to_of(i), chips) == way, size_of(i), 0)
        low = jnp.maximum(row, first)
        high = jnp.minimum(row + size, first + rows)
        todo[count] = i
        begin[count] = row - first
        return count + (high > low).astype(jnp.int32), row + size

    return lax.fori_loop(0, requests, listing, (jnp.int32(0), jnp.int32(0)), unroll=8)[0]


def pack_kernel(
    chips, chunk, requests, len_ref, dst_ref, q_ref, out_ref, tiles, hot, todo, begin, sem
):
    way, first, rows = chunk
    many, steps, width = tiles.shape[1:]
    count = flow(
        chips, requests, way, first, rows, lambda i: len_ref[i], lambda i: dst_ref[i], todo, begin
    )
    blocks = (count + many - 1) // many

    def take(j, slot, u):
        i = todo[jnp.minimum(j * many + u, count - 1)]
        return pltpu.make_async_copy(q_ref.at[i], tiles.at[slot, u], sem.at[slot, u])

    def start(j, slot):
        for u in range(many):
            take(j, slot, u).start()

    @pl.when(count > 0)
    def _():
        start(0, 0)

    @pl.when(count == 0)
    def _():
        out_ref[...] = jnp.zeros_like(out_ref)

    def step(j, carry):
        slot = lax.rem(j, 2)

        @pl.when(j + 1 < blocks)
        def _():
            start(j + 1, 1 - slot)

        row = lax.broadcasted_iota(jnp.int32, (rows, many * steps), 0)
        lane = lax.broadcasted_iota(jnp.int32, (1, many * steps), 1)
        place = jnp.full((1, many * steps), -1, jnp.int32)
        for u in range(many):
            n = jnp.minimum(j * many + u, count - 1)
            size = jnp.where(j * many + u < count, len_ref[todo[n]], 0)
            token = lane - u * steps
            place = jnp.where((token >= 0) & (token < size), begin[n] + token, place)
        hot[...] = jnp.where(row == place, 1.0, 0.0).astype(jnp.bfloat16)
        for u in range(many):
            take(j, slot, u).wait()
        block = tiles[slot].reshape(many * steps, width)
        rows_of = jnp.dot(hot[...], block, preferred_element_type=jnp.float32).astype(jnp.bfloat16)

        @pl.when(j == 0)
        def _():
            out_ref[...] = rows_of

        @pl.when(j > 0)
        def _():
            out_ref[...] += rows_of

        return carry

    lax.fori_loop(0, blocks, step, 0)


def pack(queries, lengths, target, chips, chunk):
    requests, steps, width = queries.shape
    rows = chunk[2]
    many = 16
    return pl.pallas_call(
        functools.partial(pack_kernel, chips, chunk, requests),
        in_specs=[sspec(), sspec(), anyspec()],
        out_specs=vspec(),
        out_shape=jax.ShapeDtypeStruct((rows, width), jnp.bfloat16),
        scratch_shapes=[
            pltpu.VMEM((2, many, steps, width), jnp.bfloat16),
            pltpu.VMEM((rows, many * steps), jnp.bfloat16),
            pltpu.SMEM((requests + 1,), jnp.int32),
            pltpu.SMEM((requests + 1,), jnp.int32),
            pltpu.SemaphoreType.DMA((2, many)),
        ],
        compiler_params=pltpu.CompilerParams(vmem_limit_bytes=VMEM_LIMIT),
        cost_estimate=cost(1),
        name="pack",
    )(lengths, target, queries)


def nt_dot(a, b):
    return lax.dot_general(a, b, (((1,), (1,)), ((), ())), preferred_element_type=jnp.float32)


def with_ones(values):
    return jnp.concatenate([values, jnp.ones_like(values)], axis=1)


def stacked(q, k, group, head):
    return jnp.concatenate(
        [q[:, (k * group + g) * head : (k * group + g + 1) * head] for g in range(group)], axis=0
    )


def attend(items, dims, window, pool, scores):
    requests, steps, kv, group, head, pages = dims
    coeff = 1.0 / math.sqrt(head)
    rows = group * window
    per = pool.shape[2]
    count = 4 if pages % 4 == 0 else 1
    work = [(n, k) for n in range(len(items)) for k in range(kv)]
    s_refs = dict(zip(work, scores[: len(work)]))
    p_refs = dict(zip(work, scores[len(work) :]))
    if items[0][2] is not None:
        key = lax.broadcasted_iota(jnp.int32, (window, steps), 1)
        token = lax.broadcasted_iota(jnp.int32, (window, steps), 0)
        causal = jnp.where(key <= token, 0.0, -1e30)
        causal = jnp.concatenate([causal] * group, axis=0)
    nears = {}
    for n, k in work:
        q, ids, suffix = items[n]
        qk = stacked(q, k, group, head)
        for p in range(0, pages, count):
            keys = jnp.concatenate([pool[i, k, :, 0:head] for i in ids[p : p + count]], axis=0)
            s_refs[n, k][0:rows, p * per : (p + count) * per] = nt_dot(qk, keys)
        if suffix is not None:
            nears[n, k] = nt_dot(qk, suffix[k, :, 0:head]) + causal
    tops = {}
    for n, k in work:
        found = []
        for r in range(0, rows, 16):
            score = s_refs[n, k][r : r + 16, :]
            top = jnp.max(score, axis=1, keepdims=True)
            if (n, k) in nears:
                near = nears[n, k][r : r + 16]
                top = jnp.maximum(top, jnp.max(near, axis=1, keepdims=True))
            p_refs[n, k][r : r + 16, :] = jnp.exp((score - top) * coeff).astype(jnp.bfloat16)
            found.append(top)
        tops[n, k] = jnp.concatenate(found, axis=0)
    mixes = {}
    for n, k in work:
        q, ids, suffix = items[n]
        values = jnp.concatenate([pool[i, k, :, head : 2 * head] for i in ids], axis=0)
        mixed = jnp.dot(
            p_refs[n, k][0:rows, :], with_ones(values), preferred_element_type=jnp.float32
        )
        if suffix is not None:
            weight = jnp.exp((nears[n, k] - tops[n, k]) * coeff).astype(jnp.bfloat16)
            mixed += jnp.dot(
                weight,
                with_ones(suffix[k, :, head : 2 * head]),
                preferred_element_type=jnp.float32,
            )
        mixes[n, k] = mixed
    results = [[None] * kv for _ in items]
    for n, k in work:
        total = mixes[n, k][:, head : 2 * head]
        results[n][k] = (mixes[n, k][:, 0:head] * inverse(total), tops[n, k] * coeff, total)
    return results


def inverse(total):
    share = pl.reciprocal(total, approx=True)
    return share * (2.0 - total * share)


def split_stat(values, group, window):
    lane = lax.broadcasted_iota(jnp.int32, (window, STAT), 1)
    count = len(values) * group
    assert count & (count - 1) == 0
    which = lane & (count - 1)
    level = jnp.zeros((window, STAT), jnp.float32)
    total = jnp.ones((window, STAT), jnp.float32)
    for k, (_, top, weight) in enumerate(values):
        for g in range(group):
            here = which == k * group + g
            level = jnp.where(here, top[g * window : (g + 1) * window], level)
            total = jnp.where(here, weight[g * window : (g + 1) * window, 0:STAT], total)
    stat = level + jnp.log(total)
    high = stat.astype(jnp.bfloat16).astype(jnp.float32)
    rest = stat - high
    middle = rest.astype(jnp.bfloat16).astype(jnp.float32)
    low = rest - middle
    stat = jnp.where(lane < count, high, jnp.where(lane < 2 * count, middle, low))
    return jnp.where(lane < 3 * count, stat, 0.0)


def load_pools(own_ref, sib_ref, pool, sem):
    count = own_ref.shape[0]
    return (
        pltpu.make_async_copy(own_ref, pool.at[pl.ds(0, count)], sem.at[0]),
        pltpu.make_async_copy(sib_ref, pool.at[pl.ds(count, count)], sem.at[1]),
    )


def arrange(requests, classes, class_of, keys, counts, todo):
    for c in range(classes + 1):
        counts[c] = 0

    def tally(i, carry):
        c = class_of(i)
        keys[i] = c
        counts[c + 1] = counts[c + 1] + 1
        return carry

    lax.fori_loop(0, requests, tally, 0, unroll=8)
    for c in range(classes):
        counts[c + 1] = counts[c + 1] + counts[c]

    def place(i, carry):
        c = keys[i]
        spot = counts[c]
        todo[spot] = i
        counts[c] = spot + 1
        return carry

    lax.fori_loop(0, requests, place, 0, unroll=8)


def score_scratch(kv, keys, rows):
    return [pltpu.VMEM((rows, keys), jnp.float32) for _ in range(2 * kv)] + [
        pltpu.VMEM((rows, keys), jnp.bfloat16) for _ in range(2 * kv)
    ]


BATCH = 4


def near_kernel(
    chips, dims, len_ref, dst_ref, q_ref, suf_ref, ctx_ref, stat_ref, q_buf, o_buf, todo, q_sem, o_sem
):
    requests, steps, kv, group, head, pages = dims
    coeff = 1.0 / math.sqrt(head)

    def listing(i, count):
        todo[count] = i
        return count + (shift_of(dst_ref[i], chips) != 0).astype(jnp.int32)

    count = lax.fori_loop(0, requests, listing, jnp.int32(0), unroll=8)
    blocks = (count + BATCH - 1) // BATCH

    def each(block, make, act):
        for u in range(BATCH):

            @pl.when(block * BATCH + u < count)
            def _():
                getattr(make(block, u), act)()

    def take(block, u):
        slot = lax.rem(block, 2)
        i = todo[block * BATCH + u]
        return pltpu.make_async_copy(q_ref.at[i], q_buf.at[slot, u], q_sem.at[slot, u])

    def give(block, u):
        slot = lax.rem(block, 2)
        i = todo[block * BATCH + u]
        return pltpu.make_async_copy(o_buf.at[slot, u], ctx_ref.at[i], o_sem.at[slot, u])

    each(0, take, "start")
    stat_ref[...] = jnp.zeros_like(stat_ref)
    key = lax.broadcasted_iota(jnp.int32, (steps, BATCH * steps), 1)
    token = lax.broadcasted_iota(jnp.int32, (steps, BATCH * steps), 0)
    masks = []
    for u in range(BATCH):
        mine = (key >= u * steps) & (key - u * steps <= token)
        masks.append(jnp.concatenate([jnp.where(mine, 0.0, -1e30)] * group, axis=0))

    def step(block, carry):
        slot = lax.rem(block, 2)
        each(block + 1, take, "start")
        @pl.when(block >= 2)
        def _():
            each(block - 2, give, "wait")

        each(block, take, "wait")
        picked = [todo[jnp.minimum(block * BATCH + u, count - 1)] for u in range(BATCH)]
        found = []
        for k in range(kv):
            keys = jnp.concatenate([suf_ref[i, k, :, 0:head] for i in picked], axis=0)
            found.append(
                [
                    nt_dot(stacked(q_buf[slot, u], k, group, head), keys) + masks[u]
                    for u in range(BATCH)
                ]
            )
        tops = [[jnp.max(score, axis=1, keepdims=True) for score in scores] for scores in found]
        for u in range(BATCH):
            i = picked[u]
            live = lax.broadcasted_iota(jnp.int32, (steps, head), 0) < len_ref[i]
            values = []
            for k in range(kv):
                rows = jnp.concatenate([suf_ref[n, k, :, head : 2 * head] for n in picked], axis=0)
                weight = jnp.exp((found[k][u] - tops[k][u]) * coeff).astype(jnp.bfloat16)
                mixed = jnp.dot(weight, with_ones(rows), preferred_element_type=jnp.float32)
                total = mixed[:, head : 2 * head]
                mixed = mixed[:, 0:head] * inverse(total)
                values.append((None, tops[k][u] * coeff, total))
                for g in range(group):
                    h = k * group + g
                    part = jnp.where(live, mixed[g * steps : (g + 1) * steps], 0.0)
                    o_buf[slot, u, :, h * head : (h + 1) * head] = part.astype(jnp.bfloat16)
            stat = split_stat(values, group, steps).astype(jnp.bfloat16)

            @pl.when(block * BATCH + u < count)
            def _():
                stat_ref[i] = stat

        each(block, give, "start")
        return carry

    lax.fori_loop(0, blocks, step, 0)

    def drain(block, carry):
        each(block, give, "wait")
        return carry

    lax.fori_loop(jnp.maximum(blocks - 2, 0), blocks, drain, 0)


def near_part(queries, suffix, lengths, target, dims, chips):
    requests, steps, width = queries.shape
    return pl.pallas_call(
        functools.partial(near_kernel, chips, dims),
        in_specs=[sspec(), sspec(), anyspec(), vspec()],
        out_specs=[anyspec(), vspec()],
        out_shape=[
            jax.ShapeDtypeStruct(queries.shape, jnp.bfloat16),
            jax.ShapeDtypeStruct((requests, steps, STAT), jnp.bfloat16),
        ],
        scratch_shapes=[
            pltpu.VMEM((2, BATCH, steps, width), jnp.bfloat16),
            pltpu.VMEM((2, BATCH, steps, width), jnp.bfloat16),
            pltpu.SMEM((requests + 1,), jnp.int32),
            pltpu.SemaphoreType.DMA((2, BATCH)),
            pltpu.SemaphoreType.DMA((2, BATCH)),
        ],
        compiler_params=pltpu.CompilerParams(vmem_limit_bytes=VMEM_LIMIT),
        cost_estimate=cost(2),
        name="near",
    )(lengths, target, queries, suffix)


DEPTH = 3


def local_kernel(
    chips, dims, len_ref, dst_ref, table_ref, q_ref, suf_ref, own_ref, sib_ref, old_ref,
    ctx_ref, pool, q_buf, o_buf, todo, keys, ends, sem, q_sem, o_sem, *scores,
):
    requests, steps, kv, group, head, pages = dims
    core = lax.rem(lax.axis_index("replica"), 2)
    held = own_ref.shape[0]
    quarter = steps // 4
    load_own, load_sib = load_pools(own_ref, sib_ref, pool, sem)
    load_own.start()
    load_sib.start()

    def class_of(i):
        need = (len_ref[i] + quarter - 1) // quarter
        mine = jnp.where(lax.rem(dst_ref[i], 2) == core, 0, 4) + 4 - need
        return jnp.where(shift_of(dst_ref[i], chips) == 0, mine, 8)

    arrange(requests, 9, class_of, keys, ends, todo)
    owned, count = ends[3], ends[7]
    pairs = (count + 1) // 2

    def each(pair, make, act):
        for u in range(2):

            @pl.when(2 * pair + u < count)
            def _():
                getattr(make(pair, u), act)()

    def take(pair, u):
        slot = 2 * lax.rem(pair, DEPTH) + u
        return pltpu.make_async_copy(q_ref.at[todo[2 * pair + u]], q_buf.at[slot], q_sem.at[slot])

    def give(pair, u):
        slot = 2 * lax.rem(pair, DEPTH) + u
        return pltpu.make_async_copy(o_buf.at[slot], ctx_ref.at[todo[2 * pair + u]], o_sem.at[slot])

    for ahead in range(DEPTH - 1):
        each(ahead, take, "start")

    def compute(pair, picked, window):
        slots = [2 * lax.rem(pair, DEPTH) + u for u in range(2)]
        items = []
        for u, i in enumerate(picked):
            shift = jnp.where(lax.rem(dst_ref[i], 2) == core, 0, held)
            ids = [table_ref[i, p] + shift for p in range(pages)]
            items.append((q_buf[slots[u], 0:window, :], ids, suf_ref.at[i]))
        found = attend(items, dims, window, pool, scores)
        for u, i in enumerate(picked):
            live = lax.broadcasted_iota(jnp.int32, (window, head), 0) < len_ref[i]
            for k in range(kv):
                for g in range(group):
                    h = k * group + g
                    part = found[u][k][0][g * window : (g + 1) * window]
                    part = jnp.where(live, part, 0.0).astype(jnp.bfloat16)
                    o_buf[slots[u], 0:window, h * head : (h + 1) * head] = part
            if window < steps:
                o_buf[slots[u], window:steps, :] = jnp.zeros(
                    (steps - window, o_buf.shape[2]), jnp.bfloat16
                )

    load_own.wait()

    @pl.when(owned == count)
    def _():
        load_sib.wait()

    def step(pair, carry):
        each(pair + DEPTH - 1, take, "start")

        @pl.when(pair >= DEPTH)
        def _():
            each(pair - DEPTH, give, "wait")

        @pl.when((owned < count) & (pair == owned // 2))
        def _():
            load_sib.wait()

        each(pair, take, "wait")
        picked = [todo[2 * pair], todo[jnp.minimum(2 * pair + 1, count - 1)]]
        size = jnp.maximum(len_ref[picked[0]], len_ref[picked[1]])
        need = (size + quarter - 1) // quarter
        for quarters in (1, 2, 3, 4):

            @pl.when(need == quarters)
            def _():
                compute(pair, picked, quarter * quarters)

        each(pair, give, "start")
        return carry

    lax.fori_loop(0, pairs, step, 0)

    def drain(pair, carry):
        each(pair, give, "wait")
        return carry

    lax.fori_loop(jnp.maximum(pairs - DEPTH, 0), pairs, drain, 0)


def local(queries, suffix, own, sib, ctx, table, lengths, target, dims, chips):
    requests, steps, kv, group, head, pages = dims
    width = queries.shape[2]
    held = own.shape[0]
    return pl.pallas_call(
        functools.partial(local_kernel, chips, dims),
        in_specs=[sspec(), sspec(), sspec(), anyspec(), vspec()] + [anyspec()] * 3,
        out_specs=anyspec(),
        out_shape=jax.ShapeDtypeStruct(queries.shape, jnp.bfloat16),
        input_output_aliases={7: 0},
        scratch_shapes=[
            pltpu.VMEM((2 * held,) + own.shape[1:], jnp.bfloat16),
            pltpu.VMEM((2 * DEPTH, steps, width), jnp.bfloat16),
            pltpu.VMEM((2 * DEPTH, steps, width), jnp.bfloat16),
            pltpu.SMEM((requests,), jnp.int32),
            pltpu.SMEM((requests,), jnp.int32),
            pltpu.SMEM((16,), jnp.int32),
            pltpu.SemaphoreType.DMA((2,)),
            pltpu.SemaphoreType.DMA((2 * DEPTH,)),
            pltpu.SemaphoreType.DMA((2 * DEPTH,)),
        ]
        + score_scratch(kv, pages * own.shape[2], group * steps),
        compiler_params=pltpu.CompilerParams(vmem_limit_bytes=VMEM_LIMIT),
        cost_estimate=cost(12),
        name="local",
    )(lengths, target, table, queries, suffix, own, sib, ctx)


def far_kernel(
    chips, dims, first, rows, meta_ref, q_ref, own_ref, sib_ref, out_ref, pool, todo, keys, begin,
    row_at, ends, sem, *scores,
):
    requests, steps, kv, group, head, pages = dims
    core = lax.rem(lax.axis_index("replica"), 2)
    width = kv * group * head
    held = own_ref.shape[0]
    load_own, load_sib = load_pools(own_ref, sib_ref, pool, sem)
    load_own.start()
    load_sib.start()
    row_at[0] = 0

    def bounds(i):
        low = jnp.maximum(begin[i], 0)
        high = jnp.minimum(begin[i] + meta_ref[i, pages], rows)
        return low, high, (high - (low // 16) * 16 + 15) // 16

    def class_of(i):
        here = shift_of(meta_ref[i, pages + 1], chips) == 0
        row = row_at[0]
        row_at[0] = row + jnp.where(here, meta_ref[i, pages], 0)
        begin[i] = row - first
        low, high, need = bounds(i)
        mine = jnp.where(lax.rem(meta_ref[i, pages + 1], 2) == core, 0, 3) + 3 - need
        return jnp.where(here & (high > low), mine, 6)

    arrange(requests, 7, class_of, keys, ends, todo)
    owned, count = ends[2], ends[5]
    out_ref[...] = jnp.zeros_like(out_ref)

    def compute(picked, window):
        items, spans, lives = [], [], []
        for i in picked:
            low, high, _ = bounds(i)
            base = pl.multiple_of(jnp.minimum((low // 16) * 16, rows - window), 16)
            span = pl.ds(base, window)
            row = base + lax.broadcasted_iota(jnp.int32, (window, STAT), 0)
            shift = jnp.where(lax.rem(meta_ref[i, pages + 1], 2) == core, 0, held)
            ids = [meta_ref[i, p] + shift for p in range(pages)]
            items.append((q_ref[span, :], ids, None))
            spans.append(span)
            lives.append((row >= low) & (row < high))
        found = attend(items, dims, window, pool, scores)
        for u, (span, live) in enumerate(zip(spans, lives)):
            for k in range(kv):
                for g in range(group):
                    cut = slice((k * group + g) * head, (k * group + g + 1) * head)
                    old = out_ref[span, cut].astype(jnp.float32)
                    part = found[u][k][0][g * window : (g + 1) * window]
                    out_ref[span, cut] = jnp.where(live, part, old).astype(jnp.bfloat16)
            old = out_ref[span, width : width + STAT].astype(jnp.float32)
            new = split_stat(found[u], group, window)
            out_ref[span, width : width + STAT] = jnp.where(live, new, old).astype(jnp.bfloat16)

    load_own.wait()

    @pl.when(owned == count)
    def _():
        load_sib.wait()

    def step(pair, carry):
        @pl.when((owned < count) & (pair == owned // 2))
        def _():
            load_sib.wait()

        picked = [todo[2 * pair], todo[jnp.minimum(2 * pair + 1, count - 1)]]
        need = jnp.maximum(bounds(picked[0])[2], bounds(picked[1])[2])
        for blocks in (1, 2, 3):
            if 16 * blocks <= rows:

                @pl.when(need == blocks)
                def _():
                    compute(picked, 16 * blocks)

        return carry

    lax.fori_loop(0, (count + 1) // 2, step, 0)


def far(chunk, meta, own, sib, dims, chips, first):
    rows, width = chunk.shape
    requests, steps, kv, group, head, pages = dims
    held = own.shape[0]
    return pl.pallas_call(
        functools.partial(far_kernel, chips, dims, first, rows),
        in_specs=[sspec(), vspec(), anyspec(), anyspec()],
        out_specs=vspec(),
        out_shape=jax.ShapeDtypeStruct((rows, width + STAT), jnp.bfloat16),
        scratch_shapes=[
            pltpu.VMEM((2 * held,) + own.shape[1:], jnp.bfloat16),
            pltpu.SMEM((requests,), jnp.int32),
            pltpu.SMEM((requests,), jnp.int32),
            pltpu.SMEM((requests,), jnp.int32),
            pltpu.SMEM((1,), jnp.int32),
            pltpu.SMEM((16,), jnp.int32),
            pltpu.SemaphoreType.DMA((2,)),
        ]
        + score_scratch(kv, pages * own.shape[2], group * min(48, rows)),
        compiler_params=pltpu.CompilerParams(vmem_limit_bytes=VMEM_LIMIT),
        cost_estimate=cost(6),
        name="far",
    )(meta, chunk, own, sib)


def merge_kernel(
    chips, dims, chunk, len_ref, dst_ref, old_ref, stat_ref, back_hbm, ctx_ref, back_ref, tiles, got,
    hot, todo, begin, take_sem, give_sem, back_sem,
):
    requests, steps, kv, group, head, pages = dims
    way, first, rows = chunk
    heads = kv * group
    width = heads * head
    many = got.shape[0] // steps
    back = pltpu.make_async_copy(back_hbm, back_ref, back_sem)
    back.start()
    count = flow(
        chips, requests, way, first, rows, lambda i: len_ref[i], lambda i: dst_ref[i], todo, begin
    )

    def take(j):
        return pltpu.make_async_copy(old_ref.at[todo[j]], tiles.at[j], take_sem.at[j])

    def give(j):
        return pltpu.make_async_copy(tiles.at[j], ctx_ref.at[todo[j]], give_sem.at[j])

    def issue(j, carry):
        take(j).start()
        return carry

    lax.fori_loop(0, count, issue, 0)
    back.wait()

    def whole(stat):
        return (
            stat
            + pltpu.roll(stat, STAT - heads, axis=1)
            + pltpu.roll(stat, STAT - 2 * heads, axis=1)
        )

    def some(j, u):
        picked = [jnp.minimum(j + n, count - 1) for n in range(4)]
        for n in range(4):

            @pl.when(j + n < count)
            def _():
                take(j + n).wait()

        for n, at in enumerate(picked):
            i = todo[at]
            span = pl.ds(pl.multiple_of((u + n) * steps, steps), steps)
            far_sum = whole(got[span, width : width + STAT])
            near_sum = whole(stat_ref[i].astype(jnp.float32))
            share = 1.0 / (1.0 + jnp.exp(near_sum - far_sum))
            token = lax.broadcasted_iota(jnp.int32, (steps, STAT), 0)
            here = begin[at] + token
            share = jnp.where((token < len_ref[i]) & (here >= 0) & (here < rows), share, 0.0)
            for h in range(heads):
                cut = slice(h * head, (h + 1) * head)
                near = tiles[j + n, :, cut].astype(jnp.float32)
                mixed = near + share[:, h : h + 1] * (got[span, cut] - near)
                tiles[j + n, :, cut] = mixed.astype(jnp.bfloat16)
        for n in range(4):

            @pl.when(j + n < count)
            def _():
                give(j + n).start()

    def block(b, carry):
        for u in range(many):
            j = jnp.minimum(b * many + u, count - 1)
            size = jnp.where(b * many + u < count, len_ref[todo[j]], 0)
            token = lax.broadcasted_iota(jnp.int32, (steps, rows), 0)
            row = lax.broadcasted_iota(jnp.int32, (steps, rows), 1)
            match = (begin[j] + token == row) & (token < size)
            hot[u * steps : (u + 1) * steps, :] = jnp.where(match, 1.0, 0.0).astype(jnp.bfloat16)
        got[...] = jnp.dot(hot[...], back_ref[...], preferred_element_type=jnp.float32)

        def each(quad, inner):
            some(b * many + quad * 4, quad * 4)
            return inner

        left = jnp.minimum(count - b * many, many)
        lax.fori_loop(0, (left + 3) // 4, each, 0)
        return carry

    lax.fori_loop(0, (count + many - 1) // many, block, 0)

    def drain(j, carry):
        give(j).wait()
        return carry

    lax.fori_loop(0, count, drain, 0)


def merge(ctx, stat, back, lengths, target, dims, chips, chunk, room):
    requests, steps, width = ctx.shape
    many = 8
    return pl.pallas_call(
        functools.partial(merge_kernel, chips, dims, chunk),
        in_specs=[sspec(), sspec(), anyspec(), vspec(), anyspec()],
        out_specs=anyspec(),
        out_shape=jax.ShapeDtypeStruct(ctx.shape, jnp.bfloat16),
        input_output_aliases={2: 0},
        scratch_shapes=[
            pltpu.VMEM(back.shape, jnp.bfloat16),
            pltpu.VMEM((-(-room // many) * many, steps, width), jnp.bfloat16),
            pltpu.VMEM((many * steps, width + STAT), jnp.float32),
            pltpu.VMEM((many * steps, chunk[2]), jnp.bfloat16),
            pltpu.SMEM((requests + 1,), jnp.int32),
            pltpu.SMEM((requests + 1,), jnp.int32),
            pltpu.SemaphoreType.DMA((room,)),
            pltpu.SemaphoreType.DMA((room,)),
            pltpu.SemaphoreType.DMA,
        ],
        compiler_params=pltpu.CompilerParams(vmem_limit_bytes=VMEM_LIMIT),
        cost_estimate=cost(3),
        name="merge",
    )(lengths, target, ctx, stat, back)


def shards(queries, suffix_key_value, kv_pool, page_table, lengths, destination):
    replicas = lax.axis_size("replica")
    chips = replicas // 2
    requests, steps, width = queries.shape
    kv, head = suffix_key_value.shape[2], suffix_key_value.shape[3] // 2
    pages = page_table.shape[1]
    dims = (requests, steps, kv, width // (kv * head), head, pages)
    target = destination[:, 0]
    here = lax.axis_index("replica") >> 1
    ways = range(1, chips)

    room = 2 * (requests // replicas + 1)
    most = room * steps
    mean = requests * steps // (2 * chips)
    base = min(most, -(-(mean * 3) // (4 * 32)) * 32)
    sizes = [most - base]
    if chips == 2:
        sizes = sorted({min(most, mean * n // 8) - base for n in (9, 10, 11, 12, 14)} - {0})
        sizes = [-(-size // 16) * 16 for size in sizes if size < most - base] + [most - base]

    def away(s):
        return [(r, (r + 2 * s) % replicas) for r in range(replicas)]

    def back(s):
        return [((r + 2 * s) % replicas, r) for r in range(replicas)]

    meta = jnp.concatenate([page_table, lengths[:, None], destination], axis=1)
    metas = {s: lax.ppermute(meta, "replica", away(s)) for s in ways}
    packed = [pack(queries, lengths, target, chips, (s, 0, base)) for s in ways]
    packed, metas = lax.optimization_barrier((packed, metas))
    arrived = [lax.ppermute(rows, "replica", away(s)) for s, rows in zip(ways, packed)]
    sib = lax.ppermute(kv_pool, "replica", [(r, r ^ 1) for r in range(replicas)])
    pool, sib, packed = lax.optimization_barrier((kv_pool, sib, packed))
    own = jnp.transpose(pool, (0, 2, 1, 3))
    sib = jnp.transpose(sib, (0, 2, 1, 3))
    suffix = jnp.transpose(suffix_key_value, (0, 2, 1, 3))

    def finish(size):
        def run():
            def serve(rows, s, first):
                out = far(rows, metas[s], own, sib, dims, chips, first)
                return out, lax.ppermute(out, "replica", back(s))

            more = [pack(queries, lengths, target, chips, (s, base, size)) for s in ways]
            more = [lax.ppermute(rows, "replica", away(s)) for s, rows in zip(ways, more)]
            first, came_first = zip(*[serve(r, s, 0) for s, r in zip(ways, arrived)])
            near_target, first = lax.optimization_barrier((target, first))
            ctx, stat = near_part(queries, suffix, lengths, near_target, dims, chips)
            stat, more = lax.optimization_barrier((stat, more))
            second, came_second = zip(*[serve(r, s, base) for s, r in zip(ways, more)])
            ctx, second = lax.optimization_barrier((ctx, second))
            ctx = local(queries, suffix, own, sib, ctx, page_table, lengths, target, dims, chips)
            for first_row, rows, came in ((0, base, came_first), (base, size, came_second)):
                for s, r in zip(ways, came):
                    chunk = (s, first_row, rows)
                    ctx = merge(ctx, stat, r, lengths, target, dims, chips, chunk, room)
            return ctx

        return run

    if len(sizes) == 1:
        return finish(sizes[0])()

    def flow_of(table, sender):
        goes = (table[:, pages + 1] >> 1) != sender
        return jnp.sum(jnp.where(goes, table[:, pages], 0))

    widest = jnp.maximum(flow_of(meta, here), flow_of(metas[1], 1 - here)).reshape(1)
    widest = jnp.maximum(
        widest, lax.ppermute(widest, "replica", [(r, r ^ 1) for r in range(replicas)])
    )
    seen = widest
    parts = lax.axis_size("groups")
    for hop in range(1, parts):
        other = lax.ppermute(seen, "groups", [(g, (g + hop) % parts) for g in range(parts)])
        widest = jnp.maximum(widest, other)
    level = sum((widest[0] > base + size).astype(jnp.int32) for size in sizes[:-1])
    return lax.switch(level, [finish(size) for size in sizes])


def solution(mesh):
    return jax.shard_map(
        shards,
        mesh=mesh,
        in_specs=(
            P(("groups", "replica"), None, "tensor"),
            P(("groups", "replica"), None, "tensor", None),
            P(("groups", "replica"), None, "tensor", None),
            P(("groups", "replica"), None),
            P(("groups", "replica")),
            P(("groups", "replica"), None),
        ),
        out_specs=P(("groups", "replica"), None, "tensor"),
        check_vma=False,
    )
```

```python
import functools
import math

import jax
import jax.numpy as jnp
from jax import lax
from jax.experimental import pallas as pl
from jax.experimental.pallas import tpu as pltpu
from jax.sharding import PartitionSpec as P

BIG = 1 << 14
STAT = 128
VMEM_LIMIT = 60 << 20


def cost(microseconds):
    return pl.CostEstimate(
        flops=int(microseconds * 1.1e9), bytes_accessed=1 << 10, transcendentals=0
    )


def vspec():
    return pl.BlockSpec(memory_space=pltpu.VMEM)


def sspec():
    return pl.BlockSpec(memory_space=pltpu.SMEM)


def anyspec():
    return pl.BlockSpec(memory_space=pl.ANY)


def shift_of(target, chips):
    here = lax.axis_index("replica") >> 1
    step = (target >> 1) - here
    return jnp.where(step < 0, step + chips, step)


def flow(chips, requests, way, first, rows, size_of, to_of, todo, begin):
    def listing(i, carry):
        count, row = carry
        size = jnp.where(shift_of(to_of(i), chips) == way, size_of(i), 0)
        low = jnp.maximum(row, first)
        high = jnp.minimum(row + size, first + rows)
        todo[count] = i
        begin[count] = row - first
        return count + (high > low).astype(jnp.int32), row + size

    return lax.fori_loop(0, requests, listing, (jnp.int32(0), jnp.int32(0)), unroll=8)[0]


def pack_kernel(
    chips, chunk, requests, len_ref, dst_ref, q_ref, out_ref, tiles, hot, todo, begin, sem
):
    way, first, rows = chunk
    many, steps, width = tiles.shape[1:]
    count = flow(
        chips, requests, way, first, rows, lambda i: len_ref[i], lambda i: dst_ref[i], todo, begin
    )
    blocks = (count + many - 1) // many

    def take(j, slot, u):
        i = todo[jnp.minimum(j * many + u, count - 1)]
        return pltpu.make_async_copy(q_ref.at[i], tiles.at[slot, u], sem.at[slot, u])

    def start(j, slot):
        for u in range(many):
            take(j, slot, u).start()

    @pl.when(count > 0)
    def _():
        start(0, 0)

    @pl.when(count == 0)
    def _():
        out_ref[...] = jnp.zeros_like(out_ref)

    def step(j, carry):
        slot = lax.rem(j, 2)

        @pl.when(j + 1 < blocks)
        def _():
            start(j + 1, 1 - slot)

        row = lax.broadcasted_iota(jnp.int32, (rows, many * steps), 0)
        lane = lax.broadcasted_iota(jnp.int32, (1, many * steps), 1)
        place = jnp.full((1, many * steps), -1, jnp.int32)
        for u in range(many):
            n = jnp.minimum(j * many + u, count - 1)
            size = jnp.where(j * many + u < count, len_ref[todo[n]], 0)
            token = lane - u * steps
            place = jnp.where((token >= 0) & (token < size), begin[n] + token, place)
        hot[...] = jnp.where(row == place, 1.0, 0.0).astype(jnp.bfloat16)
        for u in range(many):
            take(j, slot, u).wait()

        def column(c, inner):
            cut = pl.ds(pl.multiple_of(c * 256, 256), 256)
            block = tiles[slot, :, :, cut].reshape(many * steps, 256)
            rows_of = jnp.dot(hot[...], block, preferred_element_type=jnp.float32)

            @pl.when(j > 0)
            def _():
                out_ref[:, cut] = (out_ref[:, cut].astype(jnp.float32) + rows_of).astype(
                    jnp.bfloat16
                )

            @pl.when(j == 0)
            def _():
                out_ref[:, cut] = rows_of.astype(jnp.bfloat16)

            return inner

        lax.fori_loop(0, width // 256, column, 0)
        return carry

    lax.fori_loop(0, blocks, step, 0)


def pack(queries, lengths, target, chips, chunk):
    requests, steps, width = queries.shape
    rows = chunk[2]
    many = 16
    return pl.pallas_call(
        functools.partial(pack_kernel, chips, chunk, requests),
        in_specs=[sspec(), sspec(), anyspec()],
        out_specs=vspec(),
        out_shape=jax.ShapeDtypeStruct((rows, width), jnp.bfloat16),
        scratch_shapes=[
            pltpu.VMEM((2, many, steps, width), jnp.bfloat16),
            pltpu.VMEM((rows, many * steps), jnp.bfloat16),
            pltpu.SMEM((requests + 1,), jnp.int32),
            pltpu.SMEM((requests + 1,), jnp.int32),
            pltpu.SemaphoreType.DMA((2, many)),
        ],
        compiler_params=pltpu.CompilerParams(vmem_limit_bytes=VMEM_LIMIT),
        cost_estimate=cost(1),
        name="pack",
    )(lengths, target, queries)


def nt_dot(a, b):
    return lax.dot_general(a, b, (((1,), (1,)), ((), ())), preferred_element_type=jnp.float32)


def with_ones(values):
    return jnp.concatenate([values, jnp.ones_like(values)], axis=1)


def attend(q, k, dims, window, pool, ids, suffix, s_ref, p_ref):
    requests, steps, kv, group, head, pages = dims
    coeff = 1.0 / math.sqrt(head)
    rows = group * window
    qk = jnp.concatenate([q[:, g * head : (g + 1) * head] for g in range(group)], axis=0)
    near = None
    if suffix is not None:
        key = lax.broadcasted_iota(jnp.int32, (window, steps), 1)
        token = lax.broadcasted_iota(jnp.int32, (window, steps), 0)
        causal = jnp.where(key <= token, 0.0, -1e30)
        near = nt_dot(qk, suffix[k, :, 0:head]) + jnp.concatenate([causal] * group, axis=0)
    if pool is None:
        top = jnp.max(near, axis=1, keepdims=True)
        mixed = None
    else:
        per = pool.shape[2]
        count = 4 if pages % 4 == 0 else 1
        for p in range(0, pages, count):
            keys = jnp.concatenate([pool[i, k, :, 0:head] for i in ids[p : p + count]], axis=0)
            s_ref[0:rows, p * per : (p + count) * per] = nt_dot(qk, keys)
        found = []
        for r in range(0, rows, 16):
            score = s_ref[r : r + 16, :]
            top = jnp.max(score, axis=1, keepdims=True)
            if near is not None:
                top = jnp.maximum(top, jnp.max(near[r : r + 16], axis=1, keepdims=True))
            p_ref[r : r + 16, :] = jnp.exp((score - top) * coeff).astype(jnp.bfloat16)
            found.append(top)
        top = jnp.concatenate(found, axis=0)
        values = jnp.concatenate([pool[i, k, :, head : 2 * head] for i in ids], axis=0)
        mixed = jnp.dot(p_ref[0:rows, :], with_ones(values), preferred_element_type=jnp.float32)
    if near is not None:
        weight = jnp.exp((near - top) * coeff).astype(jnp.bfloat16)
        more = jnp.dot(
            weight, with_ones(suffix[k, :, head : 2 * head]), preferred_element_type=jnp.float32
        )
        mixed = more if mixed is None else mixed + more
    total = mixed[:, head : 2 * head]
    return mixed[:, 0:head] * inverse(total), top * coeff, total


def inverse(total):
    share = pl.reciprocal(total, approx=True)
    return share * (2.0 - total * share)


def note_stat(level_ref, total_ref, k, group, window, top, total):
    lane = lax.broadcasted_iota(jnp.int32, (window, STAT), 1)
    level, weight = level_ref[0:window, :], total_ref[0:window, :]
    for g in range(group):
        here = lane == k * group + g
        level = jnp.where(here, top[g * window : (g + 1) * window], level)
        weight = jnp.where(here, total[g * window : (g + 1) * window, 0:STAT], weight)
    level_ref[0:window, :] = level
    total_ref[0:window, :] = weight


def split_stat(level, total, count):
    lane = lax.broadcasted_iota(jnp.int32, level.shape, 1)
    stat = jnp.where(lane < count, level + jnp.log(jnp.where(lane < count, total, 1.0)), 0.0)
    high = stat.astype(jnp.bfloat16).astype(jnp.float32)
    rest = stat - high
    middle = rest.astype(jnp.bfloat16).astype(jnp.float32)
    low = rest - middle
    return high + pltpu.roll(middle, count, axis=1) + pltpu.roll(low, 2 * count, axis=1)


def load_pools(own_ref, sib_ref, pool, sem):
    count = own_ref.shape[0]
    return (
        pltpu.make_async_copy(own_ref, pool.at[pl.ds(0, count)], sem.at[0]),
        pltpu.make_async_copy(sib_ref, pool.at[pl.ds(count, count)], sem.at[1]),
    )


def arrange(requests, classes, class_of, keys, counts, todo):
    for c in range(classes + 1):
        counts[c] = 0

    def tally(i, carry):
        c = class_of(i)
        keys[i] = c
        counts[c + 1] = counts[c + 1] + 1
        return carry

    lax.fori_loop(0, requests, tally, 0, unroll=8)
    for c in range(classes):
        counts[c + 1] = counts[c + 1] + counts[c]

    def place(i, carry):
        c = keys[i]
        spot = counts[c]
        todo[spot] = i
        counts[c] = spot + 1
        return carry

    lax.fori_loop(0, requests, place, 0, unroll=8)


def score_scratch(kv, keys, rows):
    return [pltpu.VMEM((rows, keys), jnp.float32), pltpu.VMEM((rows, keys), jnp.bfloat16)]


BATCH = 4


def near_kernel(
    chips, dims, len_ref, dst_ref, q_ref, suf_ref, ctx_ref, stat_ref, q_buf, o_buf, level, total,
    todo, q_sem, o_sem,
):
    requests, steps, kv, group, head, pages = dims
    span = group * head

    def listing(i, count):
        todo[count] = i
        return count + (shift_of(dst_ref[i], chips) != 0).astype(jnp.int32)

    count = lax.fori_loop(0, requests, listing, jnp.int32(0), unroll=8)
    blocks = (count + BATCH - 1) // BATCH

    def each(block, make, act):
        for u in range(BATCH):

            @pl.when(block * BATCH + u < count)
            def _():
                getattr(make(block, u), act)()

    def take(block, u):
        slot = lax.rem(block, 2)
        i = todo[block * BATCH + u]
        return pltpu.make_async_copy(q_ref.at[i], q_buf.at[slot, u], q_sem.at[slot, u])

    def give(block, u):
        slot = lax.rem(block, 2)
        i = todo[block * BATCH + u]
        return pltpu.make_async_copy(o_buf.at[slot, u], ctx_ref.at[i], o_sem.at[slot, u])

    each(0, take, "start")
    stat_ref[...] = jnp.zeros_like(stat_ref)
    def step(block, carry):
        slot = lax.rem(block, 2)
        each(block + 1, take, "start")
        @pl.when(block >= 2)
        def _():
            each(block - 2, give, "wait")

        each(block, take, "wait")

        def one(u, carry):
            i = todo[block * BATCH + u]
            live = lax.broadcasted_iota(jnp.int32, (steps, head), 0) < len_ref[i]

            def part(k, inner):
                at = pl.multiple_of(k * span, span)
                mixed, top, weight = attend(
                    q_buf[slot, u, :, pl.ds(at, span)], k, dims, steps, None, None,
                    suf_ref.at[i], None, None,
                )
                for g in range(group):
                    piece = jnp.where(live, mixed[g * steps : (g + 1) * steps], 0.0)
                    cut = pl.ds(pl.multiple_of(at + g * head, head), head)
                    o_buf[slot, u, :, cut] = piece.astype(jnp.bfloat16)
                note_stat(level, total, k, group, steps, top, weight)
                return inner

            lax.fori_loop(0, kv, part, 0)
            stat = split_stat(level[0:steps, :], total[0:steps, :], kv * group)
            stat_ref[i] = stat.astype(jnp.bfloat16)
            return carry

        lax.fori_loop(0, jnp.minimum(count - block * BATCH, BATCH), one, 0)
        each(block, give, "start")
        return carry

    lax.fori_loop(0, blocks, step, 0)

    def drain(block, carry):
        each(block, give, "wait")
        return carry

    lax.fori_loop(jnp.maximum(blocks - 2, 0), blocks, drain, 0)


def near_part(queries, suffix, lengths, target, dims, chips):
    requests, steps, width = queries.shape
    return pl.pallas_call(
        functools.partial(near_kernel, chips, dims),
        in_specs=[sspec(), sspec(), anyspec(), vspec()],
        out_specs=[anyspec(), vspec()],
        out_shape=[
            jax.ShapeDtypeStruct(queries.shape, jnp.bfloat16),
            jax.ShapeDtypeStruct((requests, steps, STAT), jnp.bfloat16),
        ],
        scratch_shapes=[
            pltpu.VMEM((2, BATCH, steps, width), jnp.bfloat16),
            pltpu.VMEM((2, BATCH, steps, width), jnp.bfloat16),
            pltpu.VMEM((steps, STAT), jnp.float32),
            pltpu.VMEM((steps, STAT), jnp.float32),
            pltpu.SMEM((requests + 1,), jnp.int32),
            pltpu.SemaphoreType.DMA((2, BATCH)),
            pltpu.SemaphoreType.DMA((2, BATCH)),
        ],
        compiler_params=pltpu.CompilerParams(vmem_limit_bytes=VMEM_LIMIT),
        cost_estimate=cost(2),
        name="near",
    )(lengths, target, queries, suffix)


DEPTH = 3


def local_kernel(
    chips, dims, len_ref, dst_ref, table_ref, q_ref, suf_ref, own_ref, sib_ref, old_ref,
    ctx_ref, pool, q_buf, o_buf, todo, keys, ends, sem, q_sem, o_sem, *scores,
):
    requests, steps, kv, group, head, pages = dims
    core = lax.rem(lax.axis_index("replica"), 2)
    held = own_ref.shape[0]
    quarter = steps // 4
    load_own, load_sib = load_pools(own_ref, sib_ref, pool, sem)
    load_own.start()
    load_sib.start()

    def class_of(i):
        need = (len_ref[i] + quarter - 1) // quarter
        mine = jnp.where(lax.rem(dst_ref[i], 2) == core, 0, 4) + 4 - need
        return jnp.where(shift_of(dst_ref[i], chips) == 0, mine, 8)

    arrange(requests, 9, class_of, keys, ends, todo)
    owned, count = ends[3], ends[7]
    pairs = (count + 1) // 2

    def each(pair, make, act):
        for u in range(2):

            @pl.when(2 * pair + u < count)
            def _():
                getattr(make(pair, u), act)()

    def take(pair, u):
        slot = 2 * lax.rem(pair, DEPTH) + u
        return pltpu.make_async_copy(q_ref.at[todo[2 * pair + u]], q_buf.at[slot], q_sem.at[slot])

    def give(pair, u):
        slot = 2 * lax.rem(pair, DEPTH) + u
        return pltpu.make_async_copy(o_buf.at[slot], ctx_ref.at[todo[2 * pair + u]], o_sem.at[slot])

    for ahead in range(DEPTH - 1):
        each(ahead, take, "start")

    def compute(slot, i, window):
        shift = jnp.where(lax.rem(dst_ref[i], 2) == core, 0, held)
        ids = [table_ref[i, p] + shift for p in range(pages)]
        live = lax.broadcasted_iota(jnp.int32, (window, head), 0) < len_ref[i]
        span = group * head

        def part(k, inner):
            at = pl.multiple_of(k * span, span)
            mixed, _, _ = attend(
                q_buf[slot, 0:window, pl.ds(at, span)], k, dims, window, pool, ids,
                suf_ref.at[i], *scores,
            )
            for g in range(group):
                piece = jnp.where(live, mixed[g * window : (g + 1) * window], 0.0)
                cut = pl.ds(pl.multiple_of(at + g * head, head), head)
                o_buf[slot, 0:window, cut] = piece.astype(jnp.bfloat16)
            return inner

        lax.fori_loop(0, kv, part, 0)
        if window < steps:
            o_buf[slot, window:steps, :] = jnp.zeros(
                (steps - window, o_buf.shape[2]), jnp.bfloat16
            )

    load_own.wait()

    @pl.when(owned == count)
    def _():
        load_sib.wait()

    def step(pair, carry):
        each(pair + DEPTH - 1, take, "start")

        @pl.when(pair >= DEPTH)
        def _():
            each(pair - DEPTH, give, "wait")

        @pl.when((owned < count) & (pair == owned // 2))
        def _():
            load_sib.wait()

        each(pair, take, "wait")

        def one(u, inner):
            i = todo[2 * pair + u]
            slot = 2 * lax.rem(pair, DEPTH) + u
            need = (len_ref[i] + steps // 2 - 1) // (steps // 2)
            for halves in (1, 2):

                @pl.when(need == halves)
                def _():
                    compute(slot, i, halves * (steps // 2))

            return inner

        lax.fori_loop(0, jnp.minimum(count - 2 * pair, 2), one, 0)
        each(pair, give, "start")
        return carry

    lax.fori_loop(0, pairs, step, 0)

    def drain(pair, carry):
        each(pair, give, "wait")
        return carry

    lax.fori_loop(jnp.maximum(pairs - DEPTH, 0), pairs, drain, 0)


def local(queries, suffix, own, sib, ctx, table, lengths, target, dims, chips):
    requests, steps, kv, group, head, pages = dims
    width = queries.shape[2]
    held = own.shape[0]
    return pl.pallas_call(
        functools.partial(local_kernel, chips, dims),
        in_specs=[sspec(), sspec(), sspec(), anyspec(), vspec()] + [anyspec()] * 3,
        out_specs=anyspec(),
        out_shape=jax.ShapeDtypeStruct(queries.shape, jnp.bfloat16),
        input_output_aliases={7: 0},
        scratch_shapes=[
            pltpu.VMEM((2 * held,) + own.shape[1:], jnp.bfloat16),
            pltpu.VMEM((2 * DEPTH, steps, width), jnp.bfloat16),
            pltpu.VMEM((2 * DEPTH, steps, width), jnp.bfloat16),
            pltpu.SMEM((requests,), jnp.int32),
            pltpu.SMEM((requests,), jnp.int32),
            pltpu.SMEM((16,), jnp.int32),
            pltpu.SemaphoreType.DMA((2,)),
            pltpu.SemaphoreType.DMA((2 * DEPTH,)),
            pltpu.SemaphoreType.DMA((2 * DEPTH,)),
        ]
        + score_scratch(kv, pages * own.shape[2], group * steps),
        compiler_params=pltpu.CompilerParams(vmem_limit_bytes=VMEM_LIMIT),
        cost_estimate=cost(12),
        name="local",
    )(lengths, target, table, queries, suffix, own, sib, ctx)


def far_kernel(
    chips, dims, first, rows, meta_ref, q_ref, own_ref, sib_ref, out_ref, pool, level, total, todo,
    keys, begin, row_at, ends, sem, *scores,
):
    requests, steps, kv, group, head, pages = dims
    core = lax.rem(lax.axis_index("replica"), 2)
    width = kv * group * head
    held = own_ref.shape[0]
    load_own, load_sib = load_pools(own_ref, sib_ref, pool, sem)
    load_own.start()
    load_sib.start()
    row_at[0] = 0

    def bounds(i):
        low = jnp.maximum(begin[i], 0)
        high = jnp.minimum(begin[i] + meta_ref[i, pages], rows)
        return low, high, (high - (low // 16) * 16 + 15) // 16

    def class_of(i):
        here = shift_of(meta_ref[i, pages + 1], chips) == 0
        row = row_at[0]
        row_at[0] = row + jnp.where(here, meta_ref[i, pages], 0)
        begin[i] = row - first
        low, high, need = bounds(i)
        mine = jnp.where(lax.rem(meta_ref[i, pages + 1], 2) == core, 0, 3) + 3 - need
        return jnp.where(here & (high > low), mine, 6)

    arrange(requests, 7, class_of, keys, ends, todo)
    owned, count = ends[2], ends[5]
    out_ref[...] = jnp.zeros_like(out_ref)

    def compute(i, window):
        low, high, _ = bounds(i)
        base = pl.multiple_of(jnp.minimum((low // 16) * 16, rows - window), 16)
        span = pl.ds(base, window)
        row = base + lax.broadcasted_iota(jnp.int32, (window, STAT), 0)
        live = (row >= low) & (row < high)
        shift = jnp.where(lax.rem(meta_ref[i, pages + 1], 2) == core, 0, held)
        ids = [meta_ref[i, p] + shift for p in range(pages)]
        wide = group * head

        def part(k, inner):
            at = pl.multiple_of(k * wide, wide)
            mixed, top, weight = attend(
                q_ref[span, pl.ds(at, wide)], k, dims, window, pool, ids, None, *scores
            )
            for g in range(group):
                cut = pl.ds(pl.multiple_of(at + g * head, head), head)
                old = out_ref[span, cut].astype(jnp.float32)
                piece = jnp.where(live, mixed[g * window : (g + 1) * window], old)
                out_ref[span, cut] = piece.astype(jnp.bfloat16)
            note_stat(level, total, k, group, window, top, weight)
            return inner

        lax.fori_loop(0, kv, part, 0)
        old = out_ref[span, width : width + STAT].astype(jnp.float32)
        new = split_stat(level[0:window, :], total[0:window, :], kv * group)
        out_ref[span, width : width + STAT] = jnp.where(live, new, old).astype(jnp.bfloat16)

    load_own.wait()

    @pl.when(owned == count)
    def _():
        load_sib.wait()

    def step(j, carry):
        @pl.when(j == owned)
        def _():
            load_sib.wait()

        i = todo[j]
        need = bounds(i)[2]
        for blocks in (1, 2, 3):
            if 16 * blocks <= rows:

                @pl.when(need == blocks)
                def _():
                    compute(i, 16 * blocks)

        return carry

    lax.fori_loop(0, count, step, 0)


def far(chunk, meta, own, sib, dims, chips, first):
    rows, width = chunk.shape
    requests, steps, kv, group, head, pages = dims
    held = own.shape[0]
    return pl.pallas_call(
        functools.partial(far_kernel, chips, dims, first, rows),
        in_specs=[sspec(), vspec(), anyspec(), anyspec()],
        out_specs=vspec(),
        out_shape=jax.ShapeDtypeStruct((rows, width + STAT), jnp.bfloat16),
        scratch_shapes=[
            pltpu.VMEM((2 * held,) + own.shape[1:], jnp.bfloat16),
            pltpu.VMEM((48, STAT), jnp.float32),
            pltpu.VMEM((48, STAT), jnp.float32),
            pltpu.SMEM((requests,), jnp.int32),
            pltpu.SMEM((requests,), jnp.int32),
            pltpu.SMEM((requests,), jnp.int32),
            pltpu.SMEM((1,), jnp.int32),
            pltpu.SMEM((16,), jnp.int32),
            pltpu.SemaphoreType.DMA((2,)),
        ]
        + score_scratch(kv, pages * own.shape[2], group * min(48, rows)),
        compiler_params=pltpu.CompilerParams(vmem_limit_bytes=VMEM_LIMIT),
        cost_estimate=cost(6),
        name="far",
    )(meta, chunk, own, sib)


def merge_kernel(
    chips, dims, chunk, len_ref, dst_ref, old_ref, stat_ref, back_hbm, ctx_ref, back_ref, tiles, got,
    hot, todo, begin, take_sem, give_sem, back_sem,
):
    requests, steps, kv, group, head, pages = dims
    way, first, rows = chunk
    heads = kv * group
    width = heads * head
    many = got.shape[0] // steps
    back = pltpu.make_async_copy(back_hbm, back_ref, back_sem)
    back.start()
    count = flow(
        chips, requests, way, first, rows, lambda i: len_ref[i], lambda i: dst_ref[i], todo, begin
    )

    def take(j):
        return pltpu.make_async_copy(old_ref.at[todo[j]], tiles.at[j], take_sem.at[j])

    def give(j):
        return pltpu.make_async_copy(tiles.at[j], ctx_ref.at[todo[j]], give_sem.at[j])

    def issue(j, carry):
        take(j).start()
        return carry

    lax.fori_loop(0, count, issue, 0)
    back.wait()

    def whole(stat):
        return (
            stat
            + pltpu.roll(stat, STAT - heads, axis=1)
            + pltpu.roll(stat, STAT - 2 * heads, axis=1)
        )

    def one(j, u):
        i = todo[j]
        span = pl.ds(pl.multiple_of(u * steps, steps), steps)
        far_sum = whole(got[span, width : width + STAT])
        near_sum = whole(stat_ref[i].astype(jnp.float32))
        share = 1.0 / (1.0 + jnp.exp(near_sum - far_sum))
        token = lax.broadcasted_iota(jnp.int32, (steps, STAT), 0)
        here = begin[j] + token
        share = jnp.where((token < len_ref[i]) & (here >= 0) & (here < rows), share, 0.0)
        take(j).wait()
        for h in range(heads):
            cut = slice(h * head, (h + 1) * head)
            near = tiles[j, :, cut].astype(jnp.float32)
            mixed = near + share[:, h : h + 1] * (got[span, cut] - near)
            tiles[j, :, cut] = mixed.astype(jnp.bfloat16)
        give(j).start()

    def block(b, carry):
        for u in range(many):
            j = jnp.minimum(b * many + u, count - 1)
            size = jnp.where(b * many + u < count, len_ref[todo[j]], 0)
            token = lax.broadcasted_iota(jnp.int32, (steps, rows), 0)
            row = lax.broadcasted_iota(jnp.int32, (steps, rows), 1)
            match = (begin[j] + token == row) & (token < size)
            hot[u * steps : (u + 1) * steps, :] = jnp.where(match, 1.0, 0.0).astype(jnp.bfloat16)

        def column(c, inner):
            cut = pl.ds(pl.multiple_of(c * 256, 256), 256)
            got[:, cut] = jnp.dot(
                hot[...], back_ref[:, cut], preferred_element_type=jnp.float32
            )
            return inner

        lax.fori_loop(0, width // 256, column, 0)
        got[:, width : width + STAT] = jnp.dot(
            hot[...], back_ref[:, width : width + STAT], preferred_element_type=jnp.float32
        )

        def each(u, inner):
            one(b * many + u, u)
            return inner

        lax.fori_loop(0, jnp.minimum(count - b * many, many), each, 0)
        return carry

    lax.fori_loop(0, (count + many - 1) // many, block, 0)

    def drain(j, carry):
        give(j).wait()
        return carry

    lax.fori_loop(0, count, drain, 0)


def merge(ctx, stat, back, lengths, target, dims, chips, chunk, room):
    requests, steps, width = ctx.shape
    many = 8
    return pl.pallas_call(
        functools.partial(merge_kernel, chips, dims, chunk),
        in_specs=[sspec(), sspec(), anyspec(), vspec(), anyspec()],
        out_specs=anyspec(),
        out_shape=jax.ShapeDtypeStruct(ctx.shape, jnp.bfloat16),
        input_output_aliases={2: 0},
        scratch_shapes=[
            pltpu.VMEM(back.shape, jnp.bfloat16),
            pltpu.VMEM((-(-room // many) * many, steps, width), jnp.bfloat16),
            pltpu.VMEM((many * steps, width + STAT), jnp.float32),
            pltpu.VMEM((many * steps, chunk[2]), jnp.bfloat16),
            pltpu.SMEM((requests + 1,), jnp.int32),
            pltpu.SMEM((requests + 1,), jnp.int32),
            pltpu.SemaphoreType.DMA((room,)),
            pltpu.SemaphoreType.DMA((room,)),
            pltpu.SemaphoreType.DMA,
        ],
        compiler_params=pltpu.CompilerParams(vmem_limit_bytes=VMEM_LIMIT),
        cost_estimate=cost(3),
        name="merge",
    )(lengths, target, ctx, stat, back)


def shards(queries, suffix_key_value, kv_pool, page_table, lengths, destination):
    replicas = lax.axis_size("replica")
    chips = replicas // 2
    requests, steps, width = queries.shape
    kv, head = suffix_key_value.shape[2], suffix_key_value.shape[3] // 2
    pages = page_table.shape[1]
    dims = (requests, steps, kv, width // (kv * head), head, pages)
    target = destination[:, 0]
    here = lax.axis_index("replica") >> 1
    ways = range(1, chips)

    room = 2 * (requests // replicas + 1)
    most = room * steps
    mean = requests * steps // (2 * chips)
    base = min(most, -(-(mean * 3) // (4 * 32)) * 32)
    sizes = [most - base]
    if chips == 2:
        sizes = sorted({min(most, mean * n // 8) - base for n in (10, 12)} - {0})
        sizes = [-(-size // 16) * 16 for size in sizes if size < most - base] + [most - base]

    def away(s):
        return [(r, (r + 2 * s) % replicas) for r in range(replicas)]

    def back(s):
        return [((r + 2 * s) % replicas, r) for r in range(replicas)]

    meta = jnp.concatenate([page_table, lengths[:, None], destination], axis=1)
    metas = {s: lax.ppermute(meta, "replica", away(s)) for s in ways}
    packed = [pack(queries, lengths, target, chips, (s, 0, base)) for s in ways]
    packed, metas = lax.optimization_barrier((packed, metas))
    arrived = [lax.ppermute(rows, "replica", away(s)) for s, rows in zip(ways, packed)]
    own = jnp.transpose(kv_pool, (0, 2, 1, 3))
    sib = lax.ppermute(own, "replica", [(r, r ^ 1) for r in range(replicas)])
    suffix = jnp.transpose(suffix_key_value, (0, 2, 1, 3))
    near_target, packed = lax.optimization_barrier((target, packed))
    begun, stat = near_part(queries, suffix, lengths, near_target, dims, chips)

    def finish(size):
        def run():
            def serve(rows, s, first):
                out = far(rows, metas[s], own, sib, dims, chips, first)
                return out, lax.ppermute(out, "replica", back(s))

            more = [pack(queries, lengths, target, chips, (s, base, size)) for s in ways]
            more = [lax.ppermute(rows, "replica", away(s)) for s, rows in zip(ways, more)]
            first, came_first = zip(*[serve(r, s, 0) for s, r in zip(ways, arrived)])
            more, first = lax.optimization_barrier((more, first))
            second, came_second = zip(*[serve(r, s, base) for s, r in zip(ways, more)])
            ctx, second = lax.optimization_barrier((begun, second))
            ctx = local(queries, suffix, own, sib, ctx, page_table, lengths, target, dims, chips)
            for first_row, rows, came in ((0, base, came_first), (base, size, came_second)):
                for s, r in zip(ways, came):
                    chunk = (s, first_row, rows)
                    ctx = merge(ctx, stat, r, lengths, target, dims, chips, chunk, room)
            return ctx

        return run

    if len(sizes) == 1:
        return finish(sizes[0])()

    def flow_of(table, sender):
        goes = (table[:, pages + 1] >> 1) != sender
        return jnp.sum(jnp.where(goes, table[:, pages], 0))

    widest = jnp.maximum(flow_of(meta, here), flow_of(metas[1], 1 - here)).reshape(1)
    widest = jnp.maximum(
        widest, lax.ppermute(widest, "replica", [(r, r ^ 1) for r in range(replicas)])
    )
    seen = widest
    parts = lax.axis_size("groups")
    for hop in range(1, parts):
        other = lax.ppermute(seen, "groups", [(g, (g + hop) % parts) for g in range(parts)])
        widest = jnp.maximum(widest, other)
    level = sum((widest[0] > base + size).astype(jnp.int32) for size in sizes[:-1])
    return lax.switch(level, [finish(size) for size in sizes])


def solution(mesh):
    return jax.shard_map(
        shards,
        mesh=mesh,
        in_specs=(
            P(("groups", "replica"), None, "tensor"),
            P(("groups", "replica"), None, "tensor", None),
            P(("groups", "replica"), None, "tensor", None),
            P(("groups", "replica"), None),
            P(("groups", "replica")),
            P(("groups", "replica"), None),
        ),
        out_specs=P(("groups", "replica"), None, "tensor"),
        check_vma=False,
    )
```

```python
import functools
import math

import jax
import jax.numpy as jnp
from jax import lax
from jax.experimental import pallas as pl
from jax.experimental.pallas import tpu as pltpu
from jax.sharding import PartitionSpec as P

BIG = 1 << 14
STAT = 128
VMEM_LIMIT = 60 << 20


def cost(microseconds):
    return pl.CostEstimate(
        flops=int(microseconds * 1.1e9), bytes_accessed=1 << 10, transcendentals=0
    )


def vspec():
    return pl.BlockSpec(memory_space=pltpu.VMEM)


def sspec():
    return pl.BlockSpec(memory_space=pltpu.SMEM)


def anyspec():
    return pl.BlockSpec(memory_space=pl.ANY)


def shift_of(target, chips):
    here = lax.axis_index("replica") >> 1
    step = (target >> 1) - here
    return jnp.where(step < 0, step + chips, step)


def flow(chips, requests, way, first, rows, size_of, to_of, todo, begin):
    def listing(i, carry):
        count, row = carry
        size = jnp.where(shift_of(to_of(i), chips) == way, size_of(i), 0)
        low = jnp.maximum(row, first)
        high = jnp.minimum(row + size, first + rows)
        todo[count] = i
        begin[count] = row - first
        return count + (high > low).astype(jnp.int32), row + size

    return lax.fori_loop(0, requests, listing, (jnp.int32(0), jnp.int32(0)), unroll=8)[0]


def pack_kernel(
    chips, chunk, requests, len_ref, dst_ref, q_ref, out_ref, tiles, hot, todo, begin, sem
):
    way, first, rows = chunk
    many, steps, width = tiles.shape[1:]
    count = flow(
        chips, requests, way, first, rows, lambda i: len_ref[i], lambda i: dst_ref[i], todo, begin
    )
    blocks = (count + many - 1) // many

    def take(j, slot, u):
        i = todo[jnp.minimum(j * many + u, count - 1)]
        return pltpu.make_async_copy(q_ref.at[i], tiles.at[slot, u], sem.at[slot, u])

    def start(j, slot):
        for u in range(many):
            take(j, slot, u).start()

    @pl.when(count > 0)
    def _():
        start(0, 0)

    @pl.when(count == 0)
    def _():
        out_ref[...] = jnp.zeros_like(out_ref)

    def step(j, carry):
        slot = lax.rem(j, 2)

        @pl.when(j + 1 < blocks)
        def _():
            start(j + 1, 1 - slot)

        row = lax.broadcasted_iota(jnp.int32, (rows, many * steps), 0)
        lane = lax.broadcasted_iota(jnp.int32, (1, many * steps), 1)
        place = jnp.full((1, many * steps), -1, jnp.int32)
        for u in range(many):
            n = jnp.minimum(j * many + u, count - 1)
            size = jnp.where(j * many + u < count, len_ref[todo[n]], 0)
            token = lane - u * steps
            place = jnp.where((token >= 0) & (token < size), begin[n] + token, place)
        hot[...] = jnp.where(row == place, 1.0, 0.0).astype(jnp.bfloat16)
        for u in range(many):
            take(j, slot, u).wait()
        block = tiles[slot].reshape(many * steps, width)
        rows_of = jnp.dot(hot[...], block, preferred_element_type=jnp.float32).astype(jnp.bfloat16)

        @pl.when(j == 0)
        def _():
            out_ref[...] = rows_of

        @pl.when(j > 0)
        def _():
            out_ref[...] += rows_of

        return carry

    lax.fori_loop(0, blocks, step, 0)


def pack(queries, lengths, target, chips, chunk):
    requests, steps, width = queries.shape
    rows = chunk[2]
    many = 16
    return pl.pallas_call(
        functools.partial(pack_kernel, chips, chunk, requests),
        in_specs=[sspec(), sspec(), anyspec()],
        out_specs=vspec(),
        out_shape=jax.ShapeDtypeStruct((rows, width), jnp.bfloat16),
        scratch_shapes=[
            pltpu.VMEM((2, many, steps, width), jnp.bfloat16),
            pltpu.VMEM((rows, many * steps), jnp.bfloat16),
            pltpu.SMEM((requests + 1,), jnp.int32),
            pltpu.SMEM((requests + 1,), jnp.int32),
            pltpu.SemaphoreType.DMA((2, many)),
        ],
        compiler_params=pltpu.CompilerParams(vmem_limit_bytes=VMEM_LIMIT),
        cost_estimate=cost(1),
        name="pack",
    )(lengths, target, queries)


def nt_dot(a, b):
    return lax.dot_general(a, b, (((1,), (1,)), ((), ())), preferred_element_type=jnp.float32)


def with_ones(values):
    return jnp.concatenate([values, jnp.ones_like(values)], axis=1)


def stacked(q, k, group, head):
    return jnp.concatenate(
        [q[:, (k * group + g) * head : (k * group + g + 1) * head] for g in range(group)], axis=0
    )


def attend(items, dims, window, pool, scores):
    requests, steps, kv, group, head, pages = dims
    coeff = 1.0 / math.sqrt(head)
    rows = group * window
    per = pool.shape[2]
    count = 4 if pages % 4 == 0 else 1
    work = [(n, k) for n in range(len(items)) for k in range(kv)]
    s_refs = dict(zip(work, scores[: len(work)]))
    p_refs = dict(zip(work, scores[len(work) :]))
    if items[0][2] is not None:
        key = lax.broadcasted_iota(jnp.int32, (window, steps), 1)
        token = lax.broadcasted_iota(jnp.int32, (window, steps), 0)
        causal = jnp.where(key <= token, 0.0, -1e30)
        causal = jnp.concatenate([causal] * group, axis=0)
    nears = {}
    for n, k in work:
        q, ids, suffix = items[n]
        qk = stacked(q, k, group, head)
        for p in range(0, pages, count):
            keys = jnp.concatenate([pool[i, k, :, 0:head] for i in ids[p : p + count]], axis=0)
            s_refs[n, k][0:rows, p * per : (p + count) * per] = nt_dot(qk, keys)
        if suffix is not None:
            nears[n, k] = nt_dot(qk, suffix[k, :, 0:head]) + causal
    tops = {}
    for n, k in work:
        found = []
        for r in range(0, rows, 16):
            score = s_refs[n, k][r : r + 16, :]
            top = jnp.max(score, axis=1, keepdims=True)
            if (n, k) in nears:
                near = nears[n, k][r : r + 16]
                top = jnp.maximum(top, jnp.max(near, axis=1, keepdims=True))
            p_refs[n, k][r : r + 16, :] = jnp.exp((score - top) * coeff).astype(jnp.bfloat16)
            found.append(top)
        tops[n, k] = jnp.concatenate(found, axis=0)
    mixes = {}
    for n, k in work:
        q, ids, suffix = items[n]
        values = jnp.concatenate([pool[i, k, :, head : 2 * head] for i in ids], axis=0)
        mixed = jnp.dot(
            p_refs[n, k][0:rows, :], with_ones(values), preferred_element_type=jnp.float32
        )
        if suffix is not None:
            weight = jnp.exp((nears[n, k] - tops[n, k]) * coeff).astype(jnp.bfloat16)
            mixed += jnp.dot(
                weight,
                with_ones(suffix[k, :, head : 2 * head]),
                preferred_element_type=jnp.float32,
            )
        mixes[n, k] = mixed
    results = [[None] * kv for _ in items]
    for n, k in work:
        total = mixes[n, k][:, head : 2 * head]
        results[n][k] = (mixes[n, k][:, 0:head] * inverse(total), tops[n, k] * coeff, total)
    return results


def inverse(total):
    share = pl.reciprocal(total, approx=True)
    return share * (2.0 - total * share)


def split_stat(values, group, window):
    lane = lax.broadcasted_iota(jnp.int32, (window, STAT), 1)
    count = len(values) * group
    assert count & (count - 1) == 0
    which = lane & (count - 1)
    level = jnp.zeros((window, STAT), jnp.float32)
    total = jnp.ones((window, STAT), jnp.float32)
    for k, (_, top, weight) in enumerate(values):
        for g in range(group):
            here = which == k * group + g
            level = jnp.where(here, top[g * window : (g + 1) * window], level)
            total = jnp.where(here, weight[g * window : (g + 1) * window, 0:STAT], total)
    stat = level + jnp.log(total)
    high = stat.astype(jnp.bfloat16).astype(jnp.float32)
    rest = stat - high
    middle = rest.astype(jnp.bfloat16).astype(jnp.float32)
    low = rest - middle
    stat = jnp.where(lane < count, high, jnp.where(lane < 2 * count, middle, low))
    return jnp.where(lane < 3 * count, stat, 0.0)


def load_pools(own_ref, sib_ref, pool, sem):
    count = own_ref.shape[0]
    return (
        pltpu.make_async_copy(own_ref, pool.at[pl.ds(0, count)], sem.at[0]),
        pltpu.make_async_copy(sib_ref, pool.at[pl.ds(count, count)], sem.at[1]),
    )


def arrange(requests, classes, class_of, keys, counts, todo):
    for c in range(classes + 1):
        counts[c] = 0

    def tally(i, carry):
        c = class_of(i)
        keys[i] = c
        counts[c + 1] = counts[c + 1] + 1
        return carry

    lax.fori_loop(0, requests, tally, 0, unroll=8)
    for c in range(classes):
        counts[c + 1] = counts[c + 1] + counts[c]

    def place(i, carry):
        c = keys[i]
        spot = counts[c]
        todo[spot] = i
        counts[c] = spot + 1
        return carry

    lax.fori_loop(0, requests, place, 0, unroll=8)


def score_scratch(kv, keys, rows):
    return [pltpu.VMEM((rows, keys), jnp.float32) for _ in range(2 * kv)] + [
        pltpu.VMEM((rows, keys), jnp.bfloat16) for _ in range(2 * kv)
    ]


BATCH = 4


def near_kernel(
    chips, dims, len_ref, dst_ref, q_ref, suf_ref, ctx_ref, stat_ref, q_buf, o_buf, todo, q_sem, o_sem
):
    requests, steps, kv, group, head, pages = dims
    coeff = 1.0 / math.sqrt(head)

    def listing(i, count):
        todo[count] = i
        return count + (shift_of(dst_ref[i], chips) != 0).astype(jnp.int32)

    count = lax.fori_loop(0, requests, listing, jnp.int32(0), unroll=8)
    blocks = (count + BATCH - 1) // BATCH

    def each(block, make, act):
        for u in range(BATCH):

            @pl.when(block * BATCH + u < count)
            def _():
                getattr(make(block, u), act)()

    def take(block, u):
        slot = lax.rem(block, 2)
        i = todo[block * BATCH + u]
        return pltpu.make_async_copy(q_ref.at[i], q_buf.at[slot, u], q_sem.at[slot, u])

    def give(block, u):
        slot = lax.rem(block, 2)
        i = todo[block * BATCH + u]
        return pltpu.make_async_copy(o_buf.at[slot, u], ctx_ref.at[i], o_sem.at[slot, u])

    each(0, take, "start")
    stat_ref[...] = jnp.zeros_like(stat_ref)
    key = lax.broadcasted_iota(jnp.int32, (steps, BATCH * steps), 1)
    token = lax.broadcasted_iota(jnp.int32, (steps, BATCH * steps), 0)
    masks = []
    for u in range(BATCH):
        mine = (key >= u * steps) & (key - u * steps <= token)
        masks.append(jnp.concatenate([jnp.where(mine, 0.0, -1e30)] * group, axis=0))

    def step(block, carry):
        slot = lax.rem(block, 2)
        each(block + 1, take, "start")
        @pl.when(block >= 2)
        def _():
            each(block - 2, give, "wait")

        each(block, take, "wait")
        picked = [todo[jnp.minimum(block * BATCH + u, count - 1)] for u in range(BATCH)]
        found = []
        for k in range(kv):
            keys = jnp.concatenate([suf_ref[i, k, :, 0:head] for i in picked], axis=0)
            found.append(
                [
                    nt_dot(stacked(q_buf[slot, u], k, group, head), keys) + masks[u]
                    for u in range(BATCH)
                ]
            )
        tops = [[jnp.max(score, axis=1, keepdims=True) for score in scores] for scores in found]
        for u in range(BATCH):
            i = picked[u]
            live = lax.broadcasted_iota(jnp.int32, (steps, head), 0) < len_ref[i]
            values = []
            for k in range(kv):
                rows = jnp.concatenate([suf_ref[n, k, :, head : 2 * head] for n in picked], axis=0)
                weight = jnp.exp((found[k][u] - tops[k][u]) * coeff).astype(jnp.bfloat16)
                mixed = jnp.dot(weight, with_ones(rows), preferred_element_type=jnp.float32)
                total = mixed[:, head : 2 * head]
                mixed = mixed[:, 0:head] * inverse(total)
                values.append((None, tops[k][u] * coeff, total))
                for g in range(group):
                    h = k * group + g
                    part = jnp.where(live, mixed[g * steps : (g + 1) * steps], 0.0)
                    o_buf[slot, u, :, h * head : (h + 1) * head] = part.astype(jnp.bfloat16)
            stat = split_stat(values, group, steps).astype(jnp.bfloat16)

            @pl.when(block * BATCH + u < count)
            def _():
                stat_ref[i] = stat

        each(block, give, "start")
        return carry

    lax.fori_loop(0, blocks, step, 0)

    def drain(block, carry):
        each(block, give, "wait")
        return carry

    lax.fori_loop(jnp.maximum(blocks - 2, 0), blocks, drain, 0)


def near_part(queries, suffix, lengths, target, dims, chips):
    requests, steps, width = queries.shape
    return pl.pallas_call(
        functools.partial(near_kernel, chips, dims),
        in_specs=[sspec(), sspec(), anyspec(), vspec()],
        out_specs=[anyspec(), vspec()],
        out_shape=[
            jax.ShapeDtypeStruct(queries.shape, jnp.bfloat16),
            jax.ShapeDtypeStruct((requests, steps, STAT), jnp.bfloat16),
        ],
        scratch_shapes=[
            pltpu.VMEM((2, BATCH, steps, width), jnp.bfloat16),
            pltpu.VMEM((2, BATCH, steps, width), jnp.bfloat16),
            pltpu.SMEM((requests + 1,), jnp.int32),
            pltpu.SemaphoreType.DMA((2, BATCH)),
            pltpu.SemaphoreType.DMA((2, BATCH)),
        ],
        compiler_params=pltpu.CompilerParams(vmem_limit_bytes=VMEM_LIMIT),
        cost_estimate=cost(2),
        name="near",
    )(lengths, target, queries, suffix)


DEPTH = 3


def local_kernel(
    chips, dims, len_ref, dst_ref, table_ref, q_ref, suf_ref, own_ref, sib_ref, old_ref,
    ctx_ref, pool, q_buf, o_buf, todo, keys, ends, sem, q_sem, o_sem, *scores,
):
    requests, steps, kv, group, head, pages = dims
    core = lax.rem(lax.axis_index("replica"), 2)
    held = own_ref.shape[0]
    quarter = steps // 4
    load_own, load_sib = load_pools(own_ref, sib_ref, pool, sem)
    load_own.start()
    load_sib.start()

    def class_of(i):
        need = (len_ref[i] + quarter - 1) // quarter
        mine = jnp.where(lax.rem(dst_ref[i], 2) == core, 0, 4) + 4 - need
        return jnp.where(shift_of(dst_ref[i], chips) == 0, mine, 8)

    arrange(requests, 9, class_of, keys, ends, todo)
    owned, count = ends[3], ends[7]
    pairs = (count + 1) // 2

    def each(pair, make, act):
        for u in range(2):

            @pl.when(2 * pair + u < count)
            def _():
                getattr(make(pair, u), act)()

    def take(pair, u):
        slot = 2 * lax.rem(pair, DEPTH) + u
        return pltpu.make_async_copy(q_ref.at[todo[2 * pair + u]], q_buf.at[slot], q_sem.at[slot])

    def give(pair, u):
        slot = 2 * lax.rem(pair, DEPTH) + u
        return pltpu.make_async_copy(o_buf.at[slot], ctx_ref.at[todo[2 * pair + u]], o_sem.at[slot])

    for ahead in range(DEPTH - 1):
        each(ahead, take, "start")

    def compute(pair, picked, window):
        slots = [2 * lax.rem(pair, DEPTH) + u for u in range(2)]
        items = []
        for u, i in enumerate(picked):
            shift = jnp.where(lax.rem(dst_ref[i], 2) == core, 0, held)
            ids = [table_ref[i, p] + shift for p in range(pages)]
            items.append((q_buf[slots[u], 0:window, :], ids, suf_ref.at[i]))
        found = attend(items, dims, window, pool, scores)
        for u, i in enumerate(picked):
            live = lax.broadcasted_iota(jnp.int32, (window, head), 0) < len_ref[i]
            for k in range(kv):
                for g in range(group):
                    h = k * group + g
                    part = found[u][k][0][g * window : (g + 1) * window]
                    part = jnp.where(live, part, 0.0).astype(jnp.bfloat16)
                    o_buf[slots[u], 0:window, h * head : (h + 1) * head] = part
            if window < steps:
                o_buf[slots[u], window:steps, :] = jnp.zeros(
                    (steps - window, o_buf.shape[2]), jnp.bfloat16
                )

    load_own.wait()

    @pl.when(owned == count)
    def _():
        load_sib.wait()

    def step(pair, carry):
        each(pair + DEPTH - 1, take, "start")

        @pl.when(pair >= DEPTH)
        def _():
            each(pair - DEPTH, give, "wait")

        @pl.when((owned < count) & (pair == owned // 2))
        def _():
            load_sib.wait()

        each(pair, take, "wait")
        picked = [todo[2 * pair], todo[jnp.minimum(2 * pair + 1, count - 1)]]
        size = jnp.maximum(len_ref[picked[0]], len_ref[picked[1]])
        need = (size + quarter - 1) // quarter
        for quarters in (1, 2, 3, 4):

            @pl.when(need == quarters)
            def _():
                compute(pair, picked, quarter * quarters)

        each(pair, give, "start")
        return carry

    lax.fori_loop(0, pairs, step, 0)

    def drain(pair, carry):
        each(pair, give, "wait")
        return carry

    lax.fori_loop(jnp.maximum(pairs - DEPTH, 0), pairs, drain, 0)


def local(queries, suffix, own, sib, ctx, table, lengths, target, dims, chips):
    requests, steps, kv, group, head, pages = dims
    width = queries.shape[2]
    held = own.shape[0]
    return pl.pallas_call(
        functools.partial(local_kernel, chips, dims),
        in_specs=[sspec(), sspec(), sspec(), anyspec(), vspec()] + [anyspec()] * 3,
        out_specs=anyspec(),
        out_shape=jax.ShapeDtypeStruct(queries.shape, jnp.bfloat16),
        input_output_aliases={7: 0},
        scratch_shapes=[
            pltpu.VMEM((2 * held,) + own.shape[1:], jnp.bfloat16),
            pltpu.VMEM((2 * DEPTH, steps, width), jnp.bfloat16),
            pltpu.VMEM((2 * DEPTH, steps, width), jnp.bfloat16),
            pltpu.SMEM((requests,), jnp.int32),
            pltpu.SMEM((requests,), jnp.int32),
            pltpu.SMEM((16,), jnp.int32),
            pltpu.SemaphoreType.DMA((2,)),
            pltpu.SemaphoreType.DMA((2 * DEPTH,)),
            pltpu.SemaphoreType.DMA((2 * DEPTH,)),
        ]
        + score_scratch(kv, pages * own.shape[2], group * steps),
        compiler_params=pltpu.CompilerParams(vmem_limit_bytes=VMEM_LIMIT),
        cost_estimate=cost(12),
        name="local",
    )(lengths, target, table, queries, suffix, own, sib, ctx)


def far_kernel(
    chips, dims, first, rows, meta_ref, q_ref, own_ref, sib_ref, out_ref, pool, todo, keys, begin,
    row_at, ends, sem, *scores,
):
    requests, steps, kv, group, head, pages = dims
    core = lax.rem(lax.axis_index("replica"), 2)
    width = kv * group * head
    held = own_ref.shape[0]
    load_own, load_sib = load_pools(own_ref, sib_ref, pool, sem)
    load_own.start()
    load_sib.start()
    row_at[0] = 0

    def bounds(i):
        low = jnp.maximum(begin[i], 0)
        high = jnp.minimum(begin[i] + meta_ref[i, pages], rows)
        return low, high, (high - (low // 16) * 16 + 15) // 16

    def class_of(i):
        here = shift_of(meta_ref[i, pages + 1], chips) == 0
        row = row_at[0]
        row_at[0] = row + jnp.where(here, meta_ref[i, pages], 0)
        begin[i] = row - first
        low, high, need = bounds(i)
        mine = jnp.where(lax.rem(meta_ref[i, pages + 1], 2) == core, 0, 3) + 3 - need
        return jnp.where(here & (high > low), mine, 6)

    arrange(requests, 7, class_of, keys, ends, todo)
    owned, count = ends[2], ends[5]
    out_ref[...] = jnp.zeros_like(out_ref)

    def compute(picked, window):
        items, spans, lives = [], [], []
        for i in picked:
            low, high, _ = bounds(i)
            base = pl.multiple_of(jnp.minimum((low // 16) * 16, rows - window), 16)
            span = pl.ds(base, window)
            row = base + lax.broadcasted_iota(jnp.int32, (window, STAT), 0)
            shift = jnp.where(lax.rem(meta_ref[i, pages + 1], 2) == core, 0, held)
            ids = [meta_ref[i, p] + shift for p in range(pages)]
            items.append((q_ref[span, :], ids, None))
            spans.append(span)
            lives.append((row >= low) & (row < high))
        found = attend(items, dims, window, pool, scores)
        for u, (span, live) in enumerate(zip(spans, lives)):
            for k in range(kv):
                for g in range(group):
                    cut = slice((k * group + g) * head, (k * group + g + 1) * head)
                    old = out_ref[span, cut].astype(jnp.float32)
                    part = found[u][k][0][g * window : (g + 1) * window]
                    out_ref[span, cut] = jnp.where(live, part, old).astype(jnp.bfloat16)
            old = out_ref[span, width : width + STAT].astype(jnp.float32)
            new = split_stat(found[u], group, window)
            out_ref[span, width : width + STAT] = jnp.where(live, new, old).astype(jnp.bfloat16)

    load_own.wait()

    @pl.when(owned == count)
    def _():
        load_sib.wait()

    def step(pair, carry):
        @pl.when((owned < count) & (pair == owned // 2))
        def _():
            load_sib.wait()

        picked = [todo[2 * pair], todo[jnp.minimum(2 * pair + 1, count - 1)]]
        need = jnp.maximum(bounds(picked[0])[2], bounds(picked[1])[2])
        for blocks in (1, 2, 3):
            if 16 * blocks <= rows:

                @pl.when(need == blocks)
                def _():
                    compute(picked, 16 * blocks)

        return carry

    lax.fori_loop(0, (count + 1) // 2, step, 0)


def far(chunk, meta, own, sib, dims, chips, first):
    rows, width = chunk.shape
    requests, steps, kv, group, head, pages = dims
    held = own.shape[0]
    return pl.pallas_call(
        functools.partial(far_kernel, chips, dims, first, rows),
        in_specs=[sspec(), vspec(), anyspec(), anyspec()],
        out_specs=vspec(),
        out_shape=jax.ShapeDtypeStruct((rows, width + STAT), jnp.bfloat16),
        scratch_shapes=[
            pltpu.VMEM((2 * held,) + own.shape[1:], jnp.bfloat16),
            pltpu.SMEM((requests,), jnp.int32),
            pltpu.SMEM((requests,), jnp.int32),
            pltpu.SMEM((requests,), jnp.int32),
            pltpu.SMEM((1,), jnp.int32),
            pltpu.SMEM((16,), jnp.int32),
            pltpu.SemaphoreType.DMA((2,)),
        ]
        + score_scratch(kv, pages * own.shape[2], group * min(48, rows)),
        compiler_params=pltpu.CompilerParams(vmem_limit_bytes=VMEM_LIMIT),
        cost_estimate=cost(6),
        name="far",
    )(meta, chunk, own, sib)


def merge_kernel(
    chips, dims, chunk, len_ref, dst_ref, old_ref, stat_ref, back_hbm, ctx_ref, back_ref, tiles, got,
    hot, todo, begin, take_sem, give_sem, back_sem,
):
    requests, steps, kv, group, head, pages = dims
    way, first, rows = chunk
    heads = kv * group
    width = heads * head
    many = got.shape[0] // steps
    back = pltpu.make_async_copy(back_hbm, back_ref, back_sem)
    back.start()
    count = flow(
        chips, requests, way, first, rows, lambda i: len_ref[i], lambda i: dst_ref[i], todo, begin
    )

    def take(j):
        return pltpu.make_async_copy(old_ref.at[todo[j]], tiles.at[j], take_sem.at[j])

    def give(j):
        return pltpu.make_async_copy(tiles.at[j], ctx_ref.at[todo[j]], give_sem.at[j])

    def issue(j, carry):
        take(j).start()
        return carry

    lax.fori_loop(0, count, issue, 0)
    back.wait()

    def whole(stat):
        return (
            stat
            + pltpu.roll(stat, STAT - heads, axis=1)
            + pltpu.roll(stat, STAT - 2 * heads, axis=1)
        )

    def some(j, u):
        picked = [jnp.minimum(j + n, count - 1) for n in range(4)]
        for n in range(4):

            @pl.when(j + n < count)
            def _():
                take(j + n).wait()

        for n, at in enumerate(picked):
            i = todo[at]
            span = pl.ds(pl.multiple_of((u + n) * steps, steps), steps)
            far_sum = whole(got[span, width : width + STAT])
            near_sum = whole(stat_ref[i].astype(jnp.float32))
            share = 1.0 / (1.0 + jnp.exp(near_sum - far_sum))
            token = lax.broadcasted_iota(jnp.int32, (steps, STAT), 0)
            here = begin[at] + token
            share = jnp.where((token < len_ref[i]) & (here >= 0) & (here < rows), share, 0.0)
            for h in range(heads):
                cut = slice(h * head, (h + 1) * head)
                near = tiles[j + n, :, cut].astype(jnp.float32)
                mixed = near + share[:, h : h + 1] * (got[span, cut] - near)
                tiles[j + n, :, cut] = mixed.astype(jnp.bfloat16)
        for n in range(4):

            @pl.when(j + n < count)
            def _():
                give(j + n).start()

    def block(b, carry):
        for u in range(many):
            j = jnp.minimum(b * many + u, count - 1)
            size = jnp.where(b * many + u < count, len_ref[todo[j]], 0)
            token = lax.broadcasted_iota(jnp.int32, (steps, rows), 0)
            row = lax.broadcasted_iota(jnp.int32, (steps, rows), 1)
            match = (begin[j] + token == row) & (token < size)
            hot[u * steps : (u + 1) * steps, :] = jnp.where(match, 1.0, 0.0).astype(jnp.bfloat16)
        got[...] = jnp.dot(hot[...], back_ref[...], preferred_element_type=jnp.float32)

        def each(quad, inner):
            some(b * many + quad * 4, quad * 4)
            return inner

        left = jnp.minimum(count - b * many, many)
        lax.fori_loop(0, (left + 3) // 4, each, 0)
        return carry

    lax.fori_loop(0, (count + many - 1) // many, block, 0)

    def drain(j, carry):
        give(j).wait()
        return carry

    lax.fori_loop(0, count, drain, 0)


def merge(ctx, stat, back, lengths, target, dims, chips, chunk, room):
    requests, steps, width = ctx.shape
    many = 8
    return pl.pallas_call(
        functools.partial(merge_kernel, chips, dims, chunk),
        in_specs=[sspec(), sspec(), anyspec(), vspec(), anyspec()],
        out_specs=anyspec(),
        out_shape=jax.ShapeDtypeStruct(ctx.shape, jnp.bfloat16),
        input_output_aliases={2: 0},
        scratch_shapes=[
            pltpu.VMEM(back.shape, jnp.bfloat16),
            pltpu.VMEM((-(-room // many) * many, steps, width), jnp.bfloat16),
            pltpu.VMEM((many * steps, width + STAT), jnp.float32),
            pltpu.VMEM((many * steps, chunk[2]), jnp.bfloat16),
            pltpu.SMEM((requests + 1,), jnp.int32),
            pltpu.SMEM((requests + 1,), jnp.int32),
            pltpu.SemaphoreType.DMA((room,)),
            pltpu.SemaphoreType.DMA((room,)),
            pltpu.SemaphoreType.DMA,
        ],
        compiler_params=pltpu.CompilerParams(vmem_limit_bytes=VMEM_LIMIT),
        cost_estimate=cost(3),
        name="merge",
    )(lengths, target, ctx, stat, back)


def shards(queries, suffix_key_value, kv_pool, page_table, lengths, destination):
    replicas = lax.axis_size("replica")
    chips = replicas // 2
    requests, steps, width = queries.shape
    kv, head = suffix_key_value.shape[2], suffix_key_value.shape[3] // 2
    pages = page_table.shape[1]
    dims = (requests, steps, kv, width // (kv * head), head, pages)
    target = destination[:, 0]
    here = lax.axis_index("replica") >> 1
    ways = range(1, chips)

    room = 2 * (requests // replicas + 1)
    most = room * steps
    mean = requests * steps // (2 * chips)
    base = min(most, -(-(mean * 3) // (4 * 32)) * 32)
    sizes = [most - base]
    if chips == 2:
        sizes = sorted({min(most, mean * n // 8) - base for n in (12,)} - {0})
        sizes = [-(-size // 16) * 16 for size in sizes if size < most - base] + [most - base]

    def away(s):
        return [(r, (r + 2 * s) % replicas) for r in range(replicas)]

    def back(s):
        return [((r + 2 * s) % replicas, r) for r in range(replicas)]

    meta = jnp.concatenate([page_table, lengths[:, None], destination], axis=1)
    metas = {s: lax.ppermute(meta, "replica", away(s)) for s in ways}
    packed = [pack(queries, lengths, target, chips, (s, 0, base)) for s in ways]
    packed, metas = lax.optimization_barrier((packed, metas))
    arrived = [lax.ppermute(rows, "replica", away(s)) for s, rows in zip(ways, packed)]
    own = jnp.transpose(kv_pool, (0, 2, 1, 3))
    sib = lax.ppermute(own, "replica", [(r, r ^ 1) for r in range(replicas)])
    suffix = jnp.transpose(suffix_key_value, (0, 2, 1, 3))
    near_target, packed = lax.optimization_barrier((target, packed))
    begun, stat = near_part(queries, suffix, lengths, near_target, dims, chips)

    def finish(size):
        def run():
            def serve(rows, s, first):
                out = far(rows, metas[s], own, sib, dims, chips, first)
                return out, lax.ppermute(out, "replica", back(s))

            more = [pack(queries, lengths, target, chips, (s, base, size)) for s in ways]
            more = [lax.ppermute(rows, "replica", away(s)) for s, rows in zip(ways, more)]
            first, came_first = zip(*[serve(r, s, 0) for s, r in zip(ways, arrived)])
            more, first = lax.optimization_barrier((more, first))
            second, came_second = zip(*[serve(r, s, base) for s, r in zip(ways, more)])
            ctx, second = lax.optimization_barrier((begun, second))
            ctx = local(queries, suffix, own, sib, ctx, page_table, lengths, target, dims, chips)
            for first_row, rows, came in ((0, base, came_first), (base, size, came_second)):
                for s, r in zip(ways, came):
                    chunk = (s, first_row, rows)
                    ctx = merge(ctx, stat, r, lengths, target, dims, chips, chunk, room)
            return ctx

        return run

    if len(sizes) == 1:
        return finish(sizes[0])()

    def flow_of(table, sender):
        goes = (table[:, pages + 1] >> 1) != sender
        return jnp.sum(jnp.where(goes, table[:, pages], 0))

    widest = jnp.maximum(flow_of(meta, here), flow_of(metas[1], 1 - here)).reshape(1)
    widest = jnp.maximum(
        widest, lax.ppermute(widest, "replica", [(r, r ^ 1) for r in range(replicas)])
    )
    seen = widest
    parts = lax.axis_size("groups")
    for hop in range(1, parts):
        other = lax.ppermute(seen, "groups", [(g, (g + hop) % parts) for g in range(parts)])
        widest = jnp.maximum(widest, other)
    level = sum((widest[0] > base + size).astype(jnp.int32) for size in sizes[:-1])
    return lax.switch(level, [finish(size) for size in sizes])


def solution(mesh):
    return jax.shard_map(
        shards,
        mesh=mesh,
        in_specs=(
            P(("groups", "replica"), None, "tensor"),
            P(("groups", "replica"), None, "tensor", None),
            P(("groups", "replica"), None, "tensor", None),
            P(("groups", "replica"), None),
            P(("groups", "replica")),
            P(("groups", "replica"), None),
        ),
        out_specs=P(("groups", "replica"), None, "tensor"),
        check_vma=False,
    )
```
